32 devices in a mesh: batch: 16 (over z, y, core), seq: 2 (over x).
Axes of the slice: x: 2, y: 2, z: 4, core: 2. Of those that a mesh axis runs over, the one named last changes fastest.
Arguments:
- hidden_in: bfloat16 [1024, 32, 768], P('seq', 'batch'), may hold values from -6 to 6
- memory: bfloat16 [1024, 32, 768], P('seq', 'batch'), may hold values from -6 to 6
- src_len: int32 [32], P('batch'), may hold values from 1 to 1024, as said below
- out_grad: bfloat16 [1024, 32, 768], P('seq', 'batch'), may hold values from -6 to 6
- w_self_qkv: bfloat16 [768, 2304], replicated, may hold values from -0.21875 to 0.21875
- w_self_out: bfloat16 [768, 768], replicated, may hold values from -1.75 to 1.75
- w_cross_q: bfloat16 [768, 768], replicated, may hold values from -0.21875 to 0.21875
- w_cross_kv: bfloat16 [768, 1536], replicated, may hold values from -0.21875 to 0.21875
- w_cross_out: bfloat16 [768, 768], replicated, may hold values from -1.75 to 1.75
- w_ffn_in: bfloat16 [768, 3072], replicated, may hold values from -0.21875 to 0.21875
- w_ffn_out: bfloat16 [3072, 768], replicated, may hold values from -0.109375 to 0.109375
- biases: float32 [7, 768], replicated, may hold values from -1 to 1
- ffn_bias: float32 [3072], replicated, may hold values from -1 to 1
- norm_gain: float32 [3, 768], replicated, may hold values from 0.5 to 1.5
- norm_shift: float32 [3, 768], replicated, may hold values from -1 to 1
Outputs:
- layer_out: bfloat16 [1024, 32, 768], P('seq', 'batch')
- grad_in: float32 [1024, 32, 768], P('seq', 'batch')
- grad_memory: float32 [1024, 32, 768], P('seq', 'batch')
- grad_self_qkv: float32 [768, 2304], P('batch', 'seq')
- grad_self_out: float32 [768, 768], P('batch', 'seq')
- grad_cross_q: float32 [768, 768], P('batch', 'seq')
- grad_cross_kv: float32 [768, 1536], P('batch', 'seq')
- grad_cross_out: float32 [768, 768], P('batch', 'seq')
- grad_ffn_in: float32 [768, 3072], P('batch', 'seq')
- grad_ffn_out: float32 [3072, 768], P('batch', 'seq')
- grad_biases: float32 [7, 768], P(None, 'seq')
- grad_ffn_bias: float32 [3072], P('seq')
- grad_norm_gain: float32 [3, 768], P(None, 'seq')
- grad_norm_shift: float32 [3, 768], P(None, 'seq')
The draws below stay inside these ranges and needn't reach their ends.
Inputs may be any that keep to these rules, and one draw needn't show every extreme that they name: `src_len`: among the 2 sequences of each index of batch one uses all 1024 source tokens.
All inputs are finite; a program needn't handle non-finite values.
Results may differ from the reference program's by a relative error of at most 0.03.
Values may be sent and summed in bfloat16 or wider, within the bound.
No kernel may reach another device: no remote copies, remote signals or barrier semaphores. Data moves between devices by JAX's collectives and lax.ppermute only.
A program may use at most 448 MiB of HBM per device.

```python
import jax
import jax.numpy as jnp
from jax import lax

D = 768
H = 12
HD = 64
FF = 3072
SEQ_DEV = 2
LENGTH = 1024
SEQS = 32


def draw_src_len(key, part):
    key = jax.random.fold_in(key, 7)
    key_base, key_pick = jax.random.split(key)
    base = jax.random.randint(key_base, (SEQS,), 1, LENGTH + 1)
    pick = jax.random.randint(key_pick, (SEQS // SEQ_DEV,), 0, SEQ_DEV)
    chosen = jnp.arange(SEQS) % SEQ_DEV == jnp.repeat(pick, SEQ_DEV)
    return jnp.where(chosen, LENGTH, base).astype(jnp.int32)


def spiked(values, rng, source, target, parts, factor):
    owner, partner = [(jnp.arange(values.shape[dim]) // (values.shape[dim] // parts)).reshape([-1 if axis == dim else 1 for axis in range(values.ndim)]) for dim in (source, target)]
    chosen = jax.random.permutation(rng, parts)[partner]
    strong = (owner == chosen) | (owner == (partner + parts // 2) % parts)
    return jnp.where(strong, factor * values, values)


def block_scale(own_key, shape, shards, least, top_value):
    level = 1.0
    for axis_at, parts in shards:
        draws = jax.random.uniform(jax.random.fold_in(jax.random.fold_in(own_key, 6), axis_at), (parts,), jnp.float32, least / len(shards), top_value / len(shards))
        level = level * jnp.repeat(jnp.exp(draws), shape[axis_at] // parts).reshape((-1,) + (1,) * (len(shape) - 1 - axis_at))
    return level


def noise(rng, extent, deviation, reach, cuts=(), dtype=jnp.bfloat16):
    loudness = block_scale(rng, extent, cuts, -0.22, 0.18) if cuts else 1.0
    values = jax.random.normal(rng, extent, jnp.float32) * deviation * loudness
    return jnp.minimum(jnp.maximum(values, -reach), reach).astype(dtype)


def gaussian_with(rng, extent, width, most, cuts, heavy, held_as=jnp.bfloat16):
    values = width * jax.random.normal(rng, extent, jnp.float32)
    if cuts:
        values = values * block_scale(rng, extent, cuts, -0.22, 0.18)
    return jnp.clip(spiked(values, jax.random.fold_in(rng, 3), *heavy), -most, most).astype(held_as)


def setup_inputs(seed: int = 0) -> dict:
    arg_keys = jax.random.split(jax.random.key(seed), 16)
    hidden_in = noise(arg_keys[0], (LENGTH, SEQS, D), 1.0, 6.0, ((0, 2), (1, 16)))
    memory = noise(arg_keys[1], (LENGTH, SEQS, D), 1.0, 6.0, ((0, 2), (1, 16)))
    src_len = draw_src_len(jax.random.fold_in(arg_keys[15], 71), 0)
    out_grad = gaussian_with(arg_keys[3], (LENGTH, SEQS, D), 1.0, 6.0, ((0, 2), (1, 16)), (1, 2, 16, 2.0))
    w_self_qkv = noise(arg_keys[4], (D, 3 * D), D ** -0.5, 0.21875)
    w_self_out = noise(arg_keys[5], (D, D), (D // 64) ** -0.5, 1.75)
    w_cross_q = noise(arg_keys[6], (D, D), D ** -0.5, 0.21875)
    w_cross_kv = noise(arg_keys[7], (D, 2 * D), D ** -0.5, 0.21875)
    w_cross_out = noise(arg_keys[8], (D, D), (D // 64) ** -0.5, 1.75)
    w_ffn_in = noise(arg_keys[9], (D, FF), D ** -0.5, 0.21875)
    w_ffn_out = noise(arg_keys[10], (FF, D), FF ** -0.5, 0.109375)
    biases = noise(arg_keys[11], (7, D), 0.2, 1.0, (), jnp.float32)
    ffn_bias = noise(arg_keys[12], (FF,), 0.2, 1.0, (), jnp.float32)
    norm_gain = jnp.clip(1.0 + 0.1 * jax.random.normal(arg_keys[13], (3, D), jnp.float32), 0.5, 1.5)
    norm_shift = noise(arg_keys[14], (3, D), 0.2, 1.0, (), jnp.float32)
    return dict(hidden_in=hidden_in, memory=memory, src_len=src_len, out_grad=out_grad, w_self_qkv=w_self_qkv, w_self_out=w_self_out, w_cross_q=w_cross_q, w_cross_kv=w_cross_kv, w_cross_out=w_cross_out, w_ffn_in=w_ffn_in, w_ffn_out=w_ffn_out, biases=biases, ffn_bias=ffn_bias, norm_gain=norm_gain, norm_shift=norm_shift)


@jax.custom_vjp
def low(v):
    return lax.optimization_barrier(v.astype(jnp.bfloat16)).astype(jnp.float32)

@jax.custom_vjp
def low_back(v):
    return v

def low_keep(v):
    return (low(v), None)

def low_pass(kept, grad):
    return (grad,)

def back_keep(v):
    return (v, None)

def back_low(kept, grad):
    return (low(grad),)
low.defvjp(low_keep, low_pass)
low_back.defvjp(back_keep, back_low)
NEGATIVE = -1e+30

def product(left, right):
    return jnp.dot(left, right, precision=lax.Precision.HIGHEST)

def layer_norm(value, gain, shift):
    mean = lax.optimization_barrier(jnp.mean(value, axis=-1, keepdims=True))
    centred = value - mean
    spread = lax.optimization_barrier(jnp.mean(centred * centred, axis=-1, keepdims=True))
    return centred * lax.rsqrt(spread + 1e-05) * gain + shift

def attention(query, keys, values, allowed):
    query_heads = query.reshape(query.shape[0], H, HD)
    key_heads = keys.reshape(keys.shape[0], H, HD)
    value_heads = values.reshape(values.shape[0], H, HD)
    scores = low_back(jnp.einsum('qhd,khd->hqk', query_heads, key_heads, precision=lax.Precision.HIGHEST))
    masked = jnp.where(allowed[None], scores, NEGATIVE)
    top = lax.optimization_barrier(jnp.max(masked, axis=-1, keepdims=True))
    weights = jnp.where(allowed[None], jnp.exp(masked - top), 0.0)
    weights = weights / lax.optimization_barrier(jnp.sum(weights, axis=-1, keepdims=True))
    mixed = jnp.einsum('hqk,khd->qhd', low(weights), value_heads, precision=lax.Precision.HIGHEST)
    return mixed.reshape(query.shape[0], H * HD)

def forward(hidden, source, length, params):
    w_self_qkv, w_self_out, w_cross_q, w_cross_kv, w_cross_out, w_ffn_in, w_ffn_out, biases, ffn_bias, norm_gain, norm_shift = params
    positions = jnp.arange(LENGTH)
    causal = positions[:, None] >= positions[None, :]
    visible = jnp.broadcast_to(positions[None, :] < length, (LENGTH, LENGTH))
    joined = product(hidden, w_self_qkv)
    query = low(low_back((joined[:, :D] + biases[0]) * 0.125))
    keys = low(low_back(joined[:, D:2 * D]))
    values = low(low_back(joined[:, 2 * D:] + biases[1]))
    mixed = low(low_back(attention(query, keys, values, causal)))
    first = layer_norm(hidden + low_back(product(mixed, w_self_out)) + biases[2], norm_gain[0], norm_shift[0])
    query = low(low_back((product(low(first), w_cross_q) + biases[3]) * 0.125))
    pair = product(source, w_cross_kv)
    keys = low(low_back(pair[:, :D]))
    values = low(low_back(pair[:, D:] + biases[4]))
    mixed = low(low_back(attention(query, keys, values, visible)))
    second = layer_norm(first + low_back(product(mixed, w_cross_out)) + biases[5], norm_gain[1], norm_shift[1])
    inner = low_back(product(low(second), w_ffn_in) + ffn_bias)
    active = low(jax.nn.gelu(inner, approximate=False))
    return layer_norm(second + low_back(product(active, w_ffn_out)) + biases[6], norm_gain[2], norm_shift[2])

def reference(hidden_in, memory, src_len, out_grad, w_self_qkv, w_self_out, w_cross_q, w_cross_kv, w_cross_out, w_ffn_in, w_ffn_out, biases, ffn_bias, norm_gain, norm_shift):
    params = tuple((array.astype(jnp.float32) for array in (w_self_qkv, w_self_out, w_cross_q, w_cross_kv, w_cross_out, w_ffn_in, w_ffn_out, biases, ffn_bias, norm_gain, norm_shift)))
    inputs = jnp.swapaxes(hidden_in.astype(jnp.float32), 0, 1)
    sources = jnp.swapaxes(memory.astype(jnp.float32), 0, 1)
    cotangents = jnp.swapaxes(out_grad.astype(jnp.float32), 0, 1)

    def one_sequence(totals, item):
        hidden, source, length, cotangent = item

        def run(hidden, source, params):
            return forward(hidden, source, length, params)
        result, pull = jax.vjp(run, hidden, source, params)
        grad_hidden, grad_source, grad_params = pull(cotangent)
        totals = jax.tree.map(jnp.add, totals, grad_params)
        return (totals, (result.astype(jnp.bfloat16), grad_hidden, grad_source))
    zeros = jax.tree.map(jnp.zeros_like, params)
    totals, (results, grad_hidden, grad_source) = lax.scan(one_sequence, zeros, (inputs, sources, src_len, cotangents))
    return (jnp.swapaxes(results, 0, 1), jnp.swapaxes(grad_hidden, 0, 1), jnp.swapaxes(grad_source, 0, 1), totals[0], totals[1], totals[2], totals[3], totals[4], totals[5], totals[6], totals[7], totals[8], totals[9], totals[10])
```

```python
import functools
from functools import partial

import jax
import jax.numpy as jnp
from jax import lax
from jax.experimental import pallas as pl
from jax.experimental.pallas import tpu as pltpu
from jax.sharding import PartitionSpec as P

H = 12


NEGATIVE = -1e30


def from_behind(value, axis, steps):
    count = lax.axis_size(axis)
    pairs = [(source, (source + steps) % count) for source in range(count)]
    return lax.ppermute(value, axis, pairs)


def shifted(block, axis, distance):
    devices = range(lax.axis_size(axis))
    route = [(i - distance, i) for i in devices if i - distance in devices]
    return lax.ppermute(block, axis, route)


def contract_rows(left, right):
    return lax.dot_general(
        left, right, (((0,), (0,)), ((), ())), preferred_element_type=jnp.float32
    )


def times_transposed(grad, weight):
    return lax.dot_general(
        grad, weight, (((1,), (1,)), ((), ())), preferred_element_type=jnp.float32
    )


def norm_forward(value, gain, shift):
    mean = jnp.mean(value, axis=-1, keepdims=True)
    centred = value - mean
    scale = lax.rsqrt(jnp.mean(centred * centred, axis=-1, keepdims=True) + 1e-05)
    unit = centred * scale
    return (unit * gain + shift, unit, scale)


def norm_backward(grad, unit, scale, gain):
    weighted = grad * gain
    inner = (
        weighted
        - jnp.mean(weighted, axis=-1, keepdims=True)
        - unit * jnp.mean(weighted * unit, axis=-1, keepdims=True)
    )
    return (scale * inner, jnp.sum(grad * unit, axis=0), jnp.sum(grad, axis=0))


def allowed_keys(query_pos, key_pos, lengths, causal):
    if causal:
        return (query_pos[:, None] >= key_pos[None, :])[None, None]
    return (key_pos[None, :] < lengths[:, None])[:, None, None, :]


def attend_forward(query, keys, values, lengths, causal, heads):
    span, batch, width = query.shape
    size = width // heads
    query_heads = query.reshape(span, batch, heads, size)
    query_pos = lax.axis_index("seq") * span + lax.iota(jnp.int32, span)

    def block(carry, key_block, value_block, first):
        previous, total, summed = carry
        rows = key_block.shape[0]
        key_pos = first + lax.iota(jnp.int32, rows)
        scores = jnp.einsum(
            "qshd,kshd->shqk",
            query_heads,
            key_block.reshape(rows, batch, heads, size),
            preferred_element_type=jnp.float32,
        )
        allowed = allowed_keys(query_pos, key_pos, lengths, causal)
        top = jnp.maximum(previous, jnp.max(jnp.where(allowed, scores, NEGATIVE), axis=-1))
        weights = jnp.where(allowed, jnp.exp(scores - top[..., None]), 0.0)
        rescale = jnp.exp(previous - top)
        total = total * rescale + jnp.sum(weights, axis=-1)
        summed = summed * rescale[..., None] + jnp.einsum(
            "shqk,kshd->shqd",
            weights.astype(jnp.bfloat16),
            value_block.reshape(rows, batch, heads, size),
            preferred_element_type=jnp.float32,
        )
        return (top, total, summed)

    def fold(carry, piece):
        key_piece, value_piece = piece
        rows = key_piece.shape[0]
        count = rows // span
        firsts = span * lax.iota(jnp.int32, count)

        def inner(state, parts):
            return (block(state, parts[0], parts[1], parts[2]), None)

        carry, unused = lax.scan(
            inner,
            carry,
            (
                key_piece.reshape(count, span, batch, width),
                value_piece.reshape(count, span, batch, width),
                firsts,
            ),
        )
        return carry

    empty = (
        jnp.full((batch, heads, span), NEGATIVE, jnp.float32),
        jnp.zeros((batch, heads, span), jnp.float32),
        jnp.zeros((batch, heads, span, size), jnp.float32),
    )
    if causal:
        top, total, summed = fold(
            empty,
            (
                lax.all_gather(keys, "seq", axis=0, tiled=True),
                lax.all_gather(values, "seq", axis=0, tiled=True),
            ),
        )
    else:
        top, total, summed = fold(
            empty,
            (
                lax.all_gather(keys, "seq", axis=0, tiled=True),
                lax.all_gather(values, "seq", axis=0, tiled=True),
            ),
        )
    mixed = summed / total[..., None]
    mixed = jnp.transpose(mixed, (2, 0, 1, 3)).reshape(span, batch, width)
    return (mixed, top + jnp.log(total))


def block_backward(
    query_heads, grad_heads, delta, logsum, key_block, value_block, allowed, batch, heads, size
):
    span = key_block.shape[0]
    width = heads * size
    key_heads = key_block.reshape(span, batch, heads, size)
    value_heads = value_block.reshape(span, batch, heads, size)
    scores = jnp.einsum(
        "qshd,kshd->shqk", query_heads, key_heads, preferred_element_type=jnp.float32
    )
    weights = jnp.where(allowed, jnp.exp(scores - logsum[..., None]), 0.0)
    grad_weights = jnp.einsum(
        "qshd,kshd->shqk", grad_heads, value_heads, preferred_element_type=jnp.float32
    )
    grad_scores = (weights * (grad_weights - delta[..., None])).astype(jnp.bfloat16)
    grad_query = jnp.einsum(
        "shqk,kshd->qshd", grad_scores, key_heads, preferred_element_type=jnp.float32
    )
    grad_keys = jnp.einsum(
        "shqk,qshd->kshd", grad_scores, query_heads, preferred_element_type=jnp.float32
    ).reshape(span, batch, width)
    grad_values = jnp.einsum(
        "shqk,qshd->kshd",
        weights.astype(jnp.bfloat16),
        grad_heads,
        preferred_element_type=jnp.float32,
    ).reshape(span, batch, width)
    return (grad_query, grad_keys, grad_values)


def attend_backward(query, keys, values, mixed, grad_mixed, logsum, lengths, causal, heads):
    span, batch, width = query.shape
    size = width // heads
    query_heads = query.reshape(span, batch, heads, size)
    grad_heads = grad_mixed.reshape(span, batch, heads, size)
    delta = jnp.sum(
        grad_heads.astype(jnp.float32) * mixed.reshape(span, batch, heads, size), axis=-1
    )
    delta = jnp.transpose(delta, (1, 2, 0))
    devices = lax.axis_size("seq")
    place = lax.axis_index("seq")
    query_pos = place * span + lax.iota(jnp.int32, span)
    grad_query = jnp.zeros((span, batch, heads, size), jnp.float32)
    grad_keys = jnp.zeros((span, batch, width), jnp.float32)
    grad_values = jnp.zeros((span, batch, width), jnp.float32)
    key_block, value_block = (keys, values)
    for step in range(devices):
        owner = (place - step + devices) % devices
        key_pos = owner * span + lax.iota(jnp.int32, span)
        allowed = allowed_keys(query_pos, key_pos, lengths, causal)
        part_query, part_keys, part_values = block_backward(
            query_heads,
            grad_heads,
            delta,
            logsum,
            key_block,
            value_block,
            allowed,
            batch,
            heads,
            size,
        )
        grad_query = grad_query + part_query
        grad_keys = grad_keys + part_keys
        grad_values = grad_values + part_values
        if causal:
            grad_keys, grad_values = (
                from_behind(grad_keys.astype(jnp.bfloat16), "seq", 1).astype(grad_keys.dtype),
                from_behind(grad_values.astype(jnp.bfloat16), "seq", 1).astype(grad_values.dtype),
            )
        else:
            grad_keys, grad_values = (
                from_behind(grad_keys.astype(jnp.bfloat16), "seq", 1).astype(grad_keys.dtype),
                from_behind(grad_values.astype(jnp.bfloat16), "seq", 1).astype(grad_values.dtype),
            )
        if step + 1 < devices:
            if causal:
                key_block, value_block = shifted((key_block, value_block), "seq", 1)
            else:
                key_block, value_block = from_behind((key_block, value_block), "seq", 1)
    return (grad_query.reshape(span, batch, width), grad_keys, grad_values)


def per_device_general(
    hidden_in,
    memory,
    src_len,
    out_grad,
    w_self_qkv,
    w_self_out,
    w_cross_q,
    w_cross_kv,
    w_cross_out,
    w_ffn_in,
    w_ffn_out,
    biases,
    ffn_bias,
    norm_gain,
    norm_shift,
):
    span, batch, width = hidden_in.shape
    heads = H
    rows = span * batch
    layout = (span, batch, width)
    tokens = hidden_in.reshape(rows, width)
    sources = memory.reshape(rows, width)
    joined = jnp.dot(tokens, w_self_qkv, preferred_element_type=jnp.float32)
    query_self = ((joined[:, :width] + biases[0]) * 0.125).astype(jnp.bfloat16)
    key_self = joined[:, width : 2 * width].astype(jnp.bfloat16)
    value_self = (joined[:, 2 * width :] + biases[1]).astype(jnp.bfloat16)
    mixed_self, logsum_self = attend_forward(
        query_self.reshape(layout),
        key_self.reshape(layout),
        value_self.reshape(layout),
        src_len,
        True,
        heads,
    )
    out_self = mixed_self.reshape(rows, width).astype(jnp.bfloat16)
    resid_one = (
        tokens.astype(jnp.float32)
        + jnp.dot(out_self, w_self_out, preferred_element_type=jnp.float32)
        + biases[2]
    )
    normed_one, unit_one, scale_one = norm_forward(resid_one, norm_gain[0], norm_shift[0])
    normed_one_low = normed_one.astype(jnp.bfloat16)
    query_cross = (
        (jnp.dot(normed_one_low, w_cross_q, preferred_element_type=jnp.float32) + biases[3]) * 0.125
    ).astype(jnp.bfloat16)
    pair = jnp.dot(sources, w_cross_kv, preferred_element_type=jnp.float32)
    key_cross = pair[:, :width].astype(jnp.bfloat16)
    value_cross = (pair[:, width:] + biases[4]).astype(jnp.bfloat16)
    mixed_cross, logsum_cross = attend_forward(
        query_cross.reshape(layout),
        key_cross.reshape(layout),
        value_cross.reshape(layout),
        src_len,
        False,
        heads,
    )
    out_cross = mixed_cross.reshape(rows, width).astype(jnp.bfloat16)
    resid_two = (
        normed_one + jnp.dot(out_cross, w_cross_out, preferred_element_type=jnp.float32) + biases[5]
    )
    normed_two, unit_two, scale_two = norm_forward(resid_two, norm_gain[1], norm_shift[1])
    normed_two_low = normed_two.astype(jnp.bfloat16)
    inner = jnp.dot(normed_two_low, w_ffn_in, preferred_element_type=jnp.float32) + ffn_bias
    active = jax.nn.gelu(inner, approximate=False).astype(jnp.bfloat16)
    resid_three = (
        normed_two + jnp.dot(active, w_ffn_out, preferred_element_type=jnp.float32) + biases[6]
    )
    result, unit_three, scale_three = norm_forward(resid_three, norm_gain[2], norm_shift[2])
    layer_out = result.astype(jnp.bfloat16).reshape(layout)
    grad_three, gain_three, shift_three = norm_backward(
        out_grad.reshape(rows, width).astype(jnp.float32), unit_three, scale_three, norm_gain[2]
    )
    branch_three = grad_three.astype(jnp.bfloat16)
    hidden_pre, hidden_act = (inner, active)
    grad_ffn_out = contract_rows(hidden_act, branch_three)
    grad_act = times_transposed(branch_three, w_ffn_out)
    unused, pull = jax.vjp(partial(jax.nn.gelu, approximate=False), hidden_pre)
    grad_pre = pull(grad_act)[0].astype(jnp.bfloat16)
    grad_ffn_in = contract_rows(normed_two_low, grad_pre)
    grad_normed_two = grad_three + times_transposed(grad_pre, w_ffn_in)
    grad_two, gain_two, shift_two = norm_backward(
        grad_normed_two, unit_two, scale_two, norm_gain[1]
    )
    branch_two = grad_two.astype(jnp.bfloat16)
    grad_cross_out = contract_rows(out_cross, branch_two)
    grad_mixed_cross = times_transposed(branch_two, w_cross_out).astype(jnp.bfloat16)
    raw_query, grad_keys, grad_values = attend_backward(
        query_cross.reshape(layout),
        key_cross.reshape(layout),
        value_cross.reshape(layout),
        mixed_cross,
        grad_mixed_cross.reshape(layout),
        logsum_cross,
        src_len,
        False,
        heads,
    )
    grad_query_cross = (raw_query.reshape(rows, width) * 0.125).astype(jnp.bfloat16)
    grad_pair = jnp.concatenate(
        [
            grad_keys.reshape(rows, width).astype(jnp.bfloat16),
            grad_values.reshape(rows, width).astype(jnp.bfloat16),
        ],
        axis=1,
    )
    grad_cross_q = contract_rows(normed_one_low, grad_query_cross)
    grad_cross_kv = contract_rows(sources, grad_pair)
    grad_memory = times_transposed(grad_pair, w_cross_kv).reshape(layout)
    grad_normed_one = grad_two + times_transposed(grad_query_cross, w_cross_q)
    grad_one, gain_one, shift_one = norm_backward(
        grad_normed_one, unit_one, scale_one, norm_gain[0]
    )
    branch_one = grad_one.astype(jnp.bfloat16)
    grad_self_out = contract_rows(out_self, branch_one)
    grad_mixed_self = times_transposed(branch_one, w_self_out).astype(jnp.bfloat16)
    raw_query, grad_keys, grad_values = attend_backward(
        query_self.reshape(layout),
        key_self.reshape(layout),
        value_self.reshape(layout),
        mixed_self,
        grad_mixed_self.reshape(layout),
        logsum_self,
        src_len,
        True,
        heads,
    )
    grad_joined = jnp.concatenate(
        [
            (raw_query.reshape(rows, width) * 0.125).astype(jnp.bfloat16),
            grad_keys.reshape(rows, width).astype(jnp.bfloat16),
            grad_values.reshape(rows, width).astype(jnp.bfloat16),
        ],
        axis=1,
    )
    grad_self_qkv = contract_rows(tokens, grad_joined)
    grad_in = (grad_one + times_transposed(grad_joined, w_self_qkv)).reshape(layout)
    vector_terms = jnp.stack(
        [
            jnp.sum(grad_joined[:, :width].astype(jnp.float32), axis=0),
            jnp.sum(grad_joined[:, 2 * width :].astype(jnp.float32), axis=0),
            jnp.sum(grad_one, axis=0),
            jnp.sum(grad_query_cross.astype(jnp.float32), axis=0),
            jnp.sum(grad_pair[:, width:].astype(jnp.float32), axis=0),
            jnp.sum(grad_two, axis=0),
            jnp.sum(grad_three, axis=0),
            gain_one,
            gain_two,
            gain_three,
            shift_one,
            shift_two,
            shift_three,
        ]
    )
    bias_terms = jnp.sum(grad_pre.astype(jnp.float32), axis=0)[None]
    (
        grad_self_qkv,
        grad_self_out,
        grad_cross_q,
        grad_cross_kv,
        grad_cross_out,
        grad_ffn_in,
        grad_ffn_out,
        vector_terms,
        bias_terms,
    ) = (
        lax.psum_scatter(
            grad_self_qkv.astype(jnp.bfloat16), "seq", scatter_dimension=1, tiled=True
        ).astype(jnp.float32),
        lax.psum_scatter(
            grad_self_out.astype(jnp.bfloat16), "seq", scatter_dimension=1, tiled=True
        ).astype(jnp.float32),
        lax.psum_scatter(
            grad_cross_q.astype(jnp.bfloat16), "seq", scatter_dimension=1, tiled=True
        ).astype(jnp.float32),
        lax.psum_scatter(
            grad_cross_kv.astype(jnp.bfloat16), "seq", scatter_dimension=1, tiled=True
        ).astype(jnp.float32),
        lax.psum_scatter(
            grad_cross_out.astype(jnp.bfloat16), "seq", scatter_dimension=1, tiled=True
        ).astype(jnp.float32),
        lax.psum_scatter(
            grad_ffn_in.astype(jnp.bfloat16), "seq", scatter_dimension=1, tiled=True
        ).astype(jnp.float32),
        lax.psum_scatter(
            grad_ffn_out.astype(jnp.bfloat16), "seq", scatter_dimension=1, tiled=True
        ).astype(jnp.float32),
        lax.psum_scatter(
            vector_terms.astype(jnp.bfloat16), "seq", scatter_dimension=1, tiled=True
        ).astype(jnp.float32),
        lax.psum_scatter(
            bias_terms.astype(jnp.bfloat16), "seq", scatter_dimension=1, tiled=True
        ).astype(jnp.float32),
    )
    (
        grad_self_qkv,
        grad_self_out,
        grad_cross_q,
        grad_cross_kv,
        grad_cross_out,
        grad_ffn_in,
        grad_ffn_out,
    ) = (
        lax.psum_scatter(
            grad_self_qkv.astype(jnp.bfloat16), "batch", scatter_dimension=0, tiled=True
        ).astype(jnp.float32),
        lax.psum_scatter(
            grad_self_out.astype(jnp.bfloat16), "batch", scatter_dimension=0, tiled=True
        ).astype(jnp.float32),
        lax.psum_scatter(
            grad_cross_q.astype(jnp.bfloat16), "batch", scatter_dimension=0, tiled=True
        ).astype(jnp.float32),
        lax.psum_scatter(
            grad_cross_kv.astype(jnp.bfloat16), "batch", scatter_dimension=0, tiled=True
        ).astype(jnp.float32),
        lax.psum_scatter(
            grad_cross_out.astype(jnp.bfloat16), "batch", scatter_dimension=0, tiled=True
        ).astype(jnp.float32),
        lax.psum_scatter(
            grad_ffn_in.astype(jnp.bfloat16), "batch", scatter_dimension=0, tiled=True
        ).astype(jnp.float32),
        lax.psum_scatter(
            grad_ffn_out.astype(jnp.bfloat16), "batch", scatter_dimension=0, tiled=True
        ).astype(jnp.float32),
    )
    vector_terms, bias_terms = lax.psum((vector_terms, bias_terms), "batch")
    return (
        layer_out,
        grad_in,
        grad_memory,
        grad_self_qkv,
        grad_self_out,
        grad_cross_q,
        grad_cross_kv,
        grad_cross_out,
        grad_ffn_in,
        grad_ffn_out,
        vector_terms[0:7],
        bias_terms[0],
        vector_terms[7:10],
        vector_terms[10:13],
    )


LOG2E = 1.4426950408889634
NN = (((1,), (0,)), ((), ()))
NT = (((1,), (1,)), ((), ()))
HD = 64
BIG = -1e30
f32, bf16 = jnp.float32, jnp.bfloat16

def dot(a, b, dims=NN):
    return lax.dot_general(a, b, dims, preferred_element_type=f32)

def lanes(shape):
    return lax.broadcasted_iota(jnp.int32, shape, len(shape) - 1)

def swap_halves(x):
    return jnp.concatenate([x[:, HD:], x[:, :HD]], axis=1)

def fwd_kernel(len_ref, q_ref, k_ref, v_ref, o_ref, lp_ref, acc_ref, *, causal, heads, qb, ahead):
    p = pl.program_id(0)
    n = q_ref.shape[0]
    nk = k_ref.shape[0]
    scaled = q_ref[...].astype(f32) * LOG2E
    hi = scaled.astype(bf16)
    lo = (scaled - hi.astype(f32)).astype(bf16)
    first = lanes((n, 128)) < HD
    hi_s, lo_s = swap_halves(hi), swap_halves(lo)
    q_aug = (jnp.where(first, hi, lo_s), jnp.where(first, hi_s, lo))
    kk = k_ref[...]
    k_s = swap_halves(kk)
    k_aug = [jnp.where(first, kk, k_s), jnp.where(first, k_s, kk)]
    if not causal:
        length = len_ref[0]
        row = lax.broadcasted_iota(jnp.int32, (nk, 128), 0)
        extra = jnp.where((row >= length) & (lanes((nk, 128)) == 0), BIG, 0.0).astype(bf16)
        k_aug = [jnp.concatenate([x, extra], axis=1) for x in k_aug]
        one = (lanes((n, 128)) == 0).astype(bf16)
        q_aug = [jnp.concatenate([x, one], axis=1) for x in q_aug]
    vt = jnp.transpose(v_ref[...])
    ones = jnp.ones((16, nk), bf16)
    va = [jnp.concatenate([vt[h * HD:(h + 1) * HD], ones], axis=0) for h in range(2)]

    def scores(c, h):
        top_k = (c + 1) * qb if causal else nk
        s = dot(k_aug[h][:top_k], q_aug[h][c * qb:(c + 1) * qb], NT)
        if causal:
            r = lax.broadcasted_iota(jnp.int32, (qb, qb), 0)
            d = jnp.where(r <= lanes((qb, qb)), s[c * qb:], BIG)
            s = jnp.concatenate([s[:c * qb], d], axis=0) if c else d
        return s

    steps = [(c, h) for c in range(n // qb) for h in range(2)]
    queue = [scores(*x) for x in steps[:ahead]]
    parts = []
    for i, (c, h) in enumerate(steps):
        if i + ahead < len(steps):
            queue.append(scores(*steps[i + ahead]))
        s = queue.pop(0)
        m = jnp.max(s, axis=0, keepdims=True)
        pt = jnp.exp2(s - m).astype(bf16)
        ot = dot(va[h][:, :s.shape[0]], pt)
        l = ot[HD:HD + 1]
        parts.append(ot[:HD] * (1.0 / l))
        acc_ref[pl.ds(2 * p + h, 1), c * qb:(c + 1) * qb] = m + jnp.log2(l)
        if h == 1:
            o_ref[c * qb:(c + 1) * qb, :] = jnp.transpose(jnp.concatenate(parts, axis=0)).astype(bf16)
            parts = []

    @pl.when(p == pl.num_programs(0) - 1)
    def _():
        rows = acc_ref[...]
        wide = jnp.concatenate([rows, jnp.zeros((128 - rows.shape[0], n), f32)], axis=0)
        cols = jnp.transpose(wide)
        a = cols.astype(bf16)
        cols = cols - a.astype(f32)
        b = cols.astype(bf16)
        c = (cols - b.astype(f32)).astype(bf16)
        lane = lanes((n, 128))
        sh = lambda x, k: jnp.concatenate([jnp.zeros((n, k), bf16), x[:, :128 - k]], axis=1)
        out = jnp.where(lane < 16, a, jnp.where(lane < 32, sh(b, 16), jnp.where(lane < 48, sh(c, 32), jnp.where(lane == 127, 1.0, 0.0).astype(bf16))))
        lp_ref[...] = out

def attn_fwd(length, q, k, v, causal, qb=256, ahead=2):
    n, d = q.shape
    blk = lambda r: pl.BlockSpec((r, 128), lambda p, l: (0, p))
    return pl.pallas_call(
        functools.partial(fwd_kernel, causal=causal, heads=d // HD, qb=qb, ahead=ahead),
        grid_spec=pltpu.PrefetchScalarGridSpec(
            num_scalar_prefetch=1, grid=(d // 128,),
            in_specs=[blk(n), blk(k.shape[0]), blk(k.shape[0])],
            out_specs=[blk(n), pl.BlockSpec((n, 128), lambda p, l: (0, 0))],
            scratch_shapes=[pltpu.VMEM((16, n), f32)]),
        out_shape=[pltpu.HBM((n, d), bf16), pltpu.HBM((n, 128), bf16)],
        compiler_params=params(40),
        cost_estimate=cost((n + 256) * n * 1024 // (2 if causal else 1) * (d // HD), 8 * n * d, n * n * d // HD),
        name="attn_fwd",
    )(length, *hbm(q, k, v))

def side_rows(kind, refs, own):
    if kind == "early":
        one, cross_a, cross_b, ffn, bias = refs
        both = lambda r: jnp.concatenate([cross_a[r : r + 1, :], cross_b[r : r + 1, :]], axis=1)
        rows = [one[2:3, :], both(0), both(1), ffn[5:6, :], ffn[2:3, :], one[0:1, :], ffn[3:4, :], ffn[0:1, :], one[1:2, :], ffn[4:5, :], ffn[1:2, :]]
        half = rows[0].shape[1] // 2
        wide = bias.shape[1] // 2
        sides = []
        for x in range(2):
            sides += [r[:, x * half : (x + 1) * half] for r in rows]
            sides += [bias[0:1, x * wide + c * half : x * wide + (c + 1) * half] for c in range(wide // half)]
            sides += [jnp.zeros((1, half), f32)] * (16 - len(rows) - wide // half)
        return jnp.concatenate(sides, axis=0).astype(bf16)
    rows = [refs[0][0:2, :], refs[1][0:2, :], own[0:2, :], jnp.zeros((10, own.shape[1]), f32)]
    rows = jnp.concatenate(rows, axis=0)
    return jnp.concatenate([rows, jnp.zeros((16, 128), f32)], axis=1).astype(bf16)


def bwd_kernel(len_ref, q_ref, k_ref, v_ref, o_ref, g_ref, lp_ref, *rest, causal, qb, first_pair, stride, unit, kind):
    if unit:
        place, tok_ref, *side, out_ref, sums_ref, send_ref, own_ref = rest
    else:
        out_ref, sums_ref = rest
    p = pl.program_id(0) * stride + first_pair
    n, nk = q_ref.shape[0], k_ref.shape[0]
    first = lanes((n, 128)) < HD
    q = q_ref[...]
    scaled = q.astype(f32) * LOG2E
    hi = scaled.astype(bf16)
    lo = (scaled - hi.astype(f32)).astype(bf16)
    hi_s, lo_s = swap_halves(hi), swap_halves(lo)
    lp = lp_ref[...]
    q_aug = [jnp.concatenate([x, lp], axis=1) for x in (jnp.where(first, hi, lo_s), jnp.where(first, hi_s, lo))]
    kk = k_ref[...]
    k_s = swap_halves(kk)
    v = v_ref[...]
    lane = lanes((nk, 128))
    g = g_ref[...]
    zero = jnp.zeros((), bf16)
    go = g.astype(f32) * o_ref[...].astype(f32)
    go_hi = go.astype(bf16)
    go_lo = (go - go_hi.astype(f32)).astype(bf16)
    br = lax.broadcasted_iota(jnp.int32, (128, 128), 0)
    bl = lanes((128, 128))
    pick = jnp.where(((bl < 3) & (br < HD)) | ((bl >= 3) & (bl < 6) & (br >= HD)), 1.0, 0.0).astype(bf16)
    dl = dot(go_hi, pick) + dot(go_lo, pick)
    da = dl.astype(bf16)
    rest = dl - da.astype(f32)
    db = rest.astype(bf16)
    dc = (rest - db.astype(f32)).astype(bf16)
    part = lanes((n, 128))
    part = jnp.where(part >= 3, part - 3, part)
    dpack = jnp.where(part == 0, da, jnp.where(part == 1, db, dc))
    g_aug = jnp.concatenate([g, dpack], axis=1)
    qt = jnp.transpose(q)
    gt = jnp.transpose(g)
    minus = jnp.full((), -1.0, bf16)
    row = lax.broadcasted_iota(jnp.int32, (nk, 128), 0)
    dq_parts, dkts, dvts = [], [], []
    for h in range(2):
        head = 2 * p + h
        sel = jnp.where((lane < 48) & ((lane & 15) == head), -1.0, 0.0)
        if not causal:
            sel = jnp.where((lane == 127) & (row >= len_ref[0]), BIG, sel)
        k_aug = jnp.concatenate([jnp.where(first, kk, k_s) if h == 0 else jnp.where(first, k_s, kk), sel.astype(bf16)], axis=1)
        dsel = jnp.where((lane >= 3 * h) & (lane < 3 * h + 3), -1.0, 0.0).astype(bf16)
        v_m = jnp.where(first, v, zero) if h == 0 else jnp.where(first, zero, v)
        v_aug = jnp.concatenate([v_m, dsel], axis=1)
        parts = []
        dkt = jnp.zeros((HD, nk), f32)
        dvt = jnp.zeros((HD, nk), f32)
        for c in range(n // qb):
            rows = slice(c * qb, (c + 1) * qb)
            top_k = (c + 1) * qb if causal else nk
            s = dot(q_aug[h][rows], k_aug[:top_k], NT)
            w = jnp.exp2(s)
            if causal:
                r = lax.broadcasted_iota(jnp.int32, (qb, qb), 0)
                dg = jnp.where(r >= lanes((qb, qb)), w[:, c * qb:], 0.0)
                w = jnp.concatenate([w[:, :c * qb], dg], axis=1) if c else dg
            dp = dot(g_aug[rows], v_aug[:top_k], NT)
            ds = (w * dp).astype(bf16)
            wb = w.astype(bf16)
            a = dot(gt[h * HD:(h + 1) * HD, rows], wb)
            b = dot(qt[h * HD:(h + 1) * HD, rows], ds)
            if top_k < nk:
                pad = jnp.zeros((HD, nk - top_k), f32)
                a = jnp.concatenate([a, pad], axis=1)
                b = jnp.concatenate([b, pad], axis=1)
            dvt = dvt + a
            dkt = dkt + b
            parts.append(dot(ds, kk[:top_k]))
        dq_parts.append(parts)
        dkts.append(dkt)
        dvts.append(dvt)
    sums = jnp.zeros((1, 128), f32)
    dqs = []
    for c in range(n // qb):
        rows = slice(c * qb, (c + 1) * qb)
        fl = lanes((qb, 128)) < HD
        dq = (jnp.where(fl, dq_parts[0][c], dq_parts[1][c]) * 0.125).astype(bf16)
        dqs.append(dq)
        sums = sums + jnp.sum(dq.astype(f32), axis=0, keepdims=True)
    dk = jnp.transpose(jnp.concatenate(dkts, axis=0)).astype(bf16)
    dv = jnp.transpose(jnp.concatenate(dvts, axis=0)).astype(bf16)
    v_sums = jnp.sum(dv.astype(f32), axis=0, keepdims=True)
    grads = (jnp.concatenate(dqs, axis=0), dk, dv)
    if not unit:
        sums_ref[...] = jnp.concatenate([sums, v_sums, jnp.zeros((6, 128), f32)], axis=0)
        for m, part in enumerate(grads):
            out_ref[m] = part
        return
    for at in range(2):
        @pl.when(pl.program_id(0) == at)
        def _(at=at):
            cols = slice(at * 128, (at + 1) * 128)
            sums_ref[:, cols] = jnp.concatenate([sums, v_sums, jnp.zeros((6, 128), f32)], axis=0)
            for m, part in enumerate(grads):
                out_ref[m, :, cols] = part

    @pl.when(pl.program_id(0) == 1)
    def _():
        joined = jnp.concatenate([out_ref[0], out_ref[1], out_ref[2]], axis=1)
        store_units(place, dot(tok_ref[...], joined, TN).astype(bf16), unit, send_ref, own_ref)
        if kind:
            rows = side_rows(kind, side, sums_ref[...])
            for ref in (send_ref, own_ref):
                for y in range(2):
                    for x in range(2):
                        for z in range(ref.shape[2]):
                            ref[y, x, z, unit:] = rows


def attn_bwd(length, q, k, v, o, g, lp, causal, first, stride, count, tokens=None, place=None, nb=0, kind="", side=(), qb=256):
    n, d = q.shape
    blk = pl.BlockSpec((n, 128), lambda p, l: (0, first + stride * p))
    ins = [blk] * 5 + [pl.BlockSpec((n, 128), lambda p, l: (0, 0))]
    outs = [pl.BlockSpec((3, n, 128), lambda p, l: (0, 0, p)), pl.BlockSpec((8, 128), lambda p, l: (0, p))]
    shapes = [pltpu.HBM((3, n, count * 128), bf16), pltpu.HBM((8, count * 128), f32)]
    args = hbm(q, k, v, o, g, lp)
    unit = 0
    if tokens is not None:
        unit = d // nb
        rows = unit + {"early": 32, "late": 16, "": 0}[kind]
        ins += [pl.BlockSpec(memory_space=pltpu.SMEM), pl.BlockSpec((n, d), lambda p, l: (0, 0))]
        ins += [pl.BlockSpec(s.shape, lambda p, l: (0, 0)) for s in side]
        args += [place] + hbm(tokens, *side)
        outs = [pl.BlockSpec((3, n, 256), lambda p, l: (0, 0, 0)), pl.BlockSpec((8, 256), lambda p, l: (0, 0))]
        outs += [pl.BlockSpec((2, 2, nb // 4, rows, 384), lambda p, l: (0, 0, 0, 0, 0))] * 2
        shapes += [pltpu.HBM((2, 2, nb // 4, rows, 384), bf16)] * 2
    return pl.pallas_call(
        functools.partial(bwd_kernel, causal=causal, qb=qb, first_pair=first, stride=stride, unit=unit, kind=kind),
        grid_spec=pltpu.PrefetchScalarGridSpec(
            num_scalar_prefetch=1, grid=(count,), in_specs=ins, out_specs=outs),
        out_shape=shapes,
        compiler_params=params(40),
        cost_estimate=cost((n + 256) * n * 2560 // (2 if causal else 1) * count * 2, 16 * n * count * 128, 2 * n * n * count),
        name="attn_bwd",
    )(length, *args)


def cost(flops, moved, exps=0):
    return pl.CostEstimate(flops=int(flops), bytes_accessed=int(moved), transcendentals=int(exps))


def params(mib):
    return pltpu.CompilerParams(vmem_limit_bytes=mib * 2**20)


def hbm(*values):
    return [pltpu.with_memory_space_constraint(v, pltpu.HBM) for v in values]


def whole():
    return pl.BlockSpec(memory_space=pltpu.VMEM)


def fixed(shape):
    return pl.BlockSpec(shape, lambda *_: (0,) * len(shape), pipeline_mode=pl.Buffered(1))


def spread_rows(block):
    return lambda i, *_: (i, 0)


def project_kernel(place, mine, got, weight, biases, *outs, step, plan):
    i = pl.program_id(0)
    x = jnp.where(i // step == place[0], mine[...], got[...])
    outs[0][...] = x
    joined = dot(x, weight[...])
    width = x.shape[1]
    for n, (bias, scale) in enumerate(plan):
        part = joined[:, n * width : (n + 1) * width]
        if bias is not None:
            part = part + biases[bias : bias + 1, :]
        if scale != 1.0:
            part = part * scale
        outs[n + 1][...] = part.astype(bf16)


def project(place, pairs, got, weight, biases, plan, rows=256):
    half, width = got.shape
    step = half // rows
    cols = weight.shape[1]
    block = pl.BlockSpec((rows, width), lambda i, p: (i, 0))
    return pl.pallas_call(
        functools.partial(project_kernel, step=step, plan=plan),
        grid_spec=pltpu.PrefetchScalarGridSpec(
            num_scalar_prefetch=1,
            grid=(2 * step,),
            in_specs=[
                pl.BlockSpec((rows, width), lambda i, p: (i % step, p[0])),
                pl.BlockSpec((rows, width), lambda i, p: (i % step, 0)),
                whole(),
                whole(),
            ],
            out_specs=[block] * (1 + len(plan)),
        ),
        out_shape=[pltpu.HBM((2 * half, width), bf16)] * (1 + len(plan)),
        compiler_params=params(32),
        cost_estimate=cost(4 * half * width * cols, 2 * width * cols + 12 * half * width),
        name="project",
    )(place, *hbm(pairs, got), weight, biases)


def norm_unit(value):
    mean = jnp.mean(value, axis=-1, keepdims=True)
    centred = value - mean
    scale = lax.rsqrt(jnp.mean(centred * centred, axis=-1, keepdims=True) + 1e-05)
    return centred * scale, scale


def norm_back(grad, unit, scale, gain):
    weighted = grad * gain
    return scale * (
        weighted
        - jnp.mean(weighted, axis=-1, keepdims=True)
        - unit * jnp.mean(weighted * unit, axis=-1, keepdims=True)
    )


def row_sum(value):
    return jnp.sum(value, axis=0, keepdims=True)


def after_self_kernel(o, tok, w_out, w_q, biases, gain, shift, unit_ref, scale_ref, low_ref, q_ref):
    resid = tok[...].astype(f32) + dot(o[...], w_out[...]) + biases[2:3, :]
    unit, scale = norm_unit(resid)
    unit_ref[...] = unit
    scale_ref[...] = jnp.broadcast_to(scale, scale_ref.shape)
    low_ = (unit * gain[0:1, :] + shift[0:1, :]).astype(bf16)
    low_ref[...] = low_
    q_ref[...] = ((dot(low_, w_q[...]) + biases[3:4, :]) * 0.125).astype(bf16)


def after_self(o, tok, w_out, w_q, biases, gain, shift, rows=256):
    n, d = o.shape
    block = pl.BlockSpec((rows, d), lambda i: (i, 0))
    return pl.pallas_call(
        after_self_kernel,
        grid=(n // rows,),
        in_specs=[block, block, whole(), whole()] + [whole()] * 3,
        out_specs=[block, pl.BlockSpec((rows, 128), lambda i: (i, 0)), block, block],
        out_shape=[
            pltpu.HBM((n, d), f32),
            pltpu.HBM((n, 128), f32),
            pltpu.HBM((n, d), bf16),
            pltpu.HBM((n, d), bf16),
        ],
        compiler_params=params(32),
        cost_estimate=cost(4 * n * d * d, 4 * d * d + 12 * n * d),
        name="after_self",
    )(*hbm(o, tok), w_out, w_q, biases, gain, shift)


RATE = 0.3275911 * 0.7071067811865476
TAIL = tuple(0.5 * c for c in (0.254829592, -0.284496736, 1.421413741, -1.453152027, 1.061405429))
DENSITY = 0.3989422804014327


def gelu_pair(v):
    size = jnp.abs(v)
    base = 1.0 + RATE * size
    t = pl.reciprocal(base, approx=True)
    t = t * (2.0 - base * t)
    poly = TAIL[4]
    for c in TAIL[3::-1]:
        poly = c + t * poly
    bell = jnp.exp2((v * v) * (-0.5 * LOG2E))
    tail = t * poly * bell
    below = jnp.where(v >= 0.0, 1.0 - tail, tail)
    return v * below, below + v * (DENSITY * bell)


def ffn_kernel(
    o, unit_one, cot, w_co, w_in, w_out, biases, ffn_bias, gain, shift,
    layer_ref, act_ref, pre_ref, low_ref, b3_ref, g2_ref, b2_ref, gm_ref, sums_ref, fsum_ref,
    slope, *, chunk,
):
    i = pl.program_id(0)
    ff = w_in.shape[1]
    n_chunks = ff // chunk

    @pl.when(i == 0)
    def _():
        sums_ref[...] = jnp.zeros_like(sums_ref)
        fsum_ref[...] = jnp.zeros_like(fsum_ref)

    normed_one = unit_one[...] * gain[0:1, :] + shift[0:1, :]
    resid = normed_one + dot(o[...], w_co[...]) + biases[5:6, :]
    unit_two, scale_two = norm_unit(resid)
    normed_two = unit_two * gain[1:2, :] + shift[1:2, :]
    low_two = normed_two.astype(bf16)
    low_ref[...] = low_two

    def inner(j):
        at = slice(j * chunk, (j + 1) * chunk)
        return dot(low_two, w_in[:, at]) + ffn_bias[0:1, at]

    total = normed_two + biases[6:7, :]
    ahead = inner(0)
    for j in range(n_chunks):
        v = ahead
        if j + 1 < n_chunks:
            ahead = inner(j + 1)
        at = slice(j * chunk, (j + 1) * chunk)
        act, grad = gelu_pair(v)
        act = act.astype(bf16)
        act_ref[:, at] = act
        slope[:, at] = grad
        total = total + dot(act, w_out[at, :])
    unit, scale = norm_unit(total)
    layer_ref[...] = (unit * gain[2:3, :] + shift[2:3, :]).astype(bf16)
    g = cot[...].astype(f32)
    grad_three = norm_back(g, unit, scale, gain[2:3, :])
    branch = grad_three.astype(bf16)
    b3_ref[...] = branch
    sums_ref[0:1, :] += row_sum(g * unit)
    sums_ref[1:2, :] += row_sum(g)
    sums_ref[2:3, :] += row_sum(grad_three)

    def back(j):
        return dot(branch, w_out[j * chunk : (j + 1) * chunk, :], NT)

    total = grad_three
    ahead = back(0)
    for j in range(n_chunks):
        v = ahead
        if j + 1 < n_chunks:
            ahead = back(j + 1)
        at = slice(j * chunk, (j + 1) * chunk)
        pre = (v * slope[:, at]).astype(bf16)
        pre_ref[:, at] = pre
        fsum_ref[0:1, at] += row_sum(pre.astype(f32))
        total = total + dot(pre, w_in[:, at], NT)
    grad_two = norm_back(total, unit_two, scale_two, gain[1:2, :])
    g2_ref[...] = grad_two
    branch = grad_two.astype(bf16)
    b2_ref[...] = branch
    sums_ref[3:4, :] += row_sum(total * unit_two)
    sums_ref[4:5, :] += row_sum(total)
    sums_ref[5:6, :] += row_sum(grad_two)
    gm_ref[...] = dot(branch, w_co[...], NT).astype(bf16)


def ffn(o, unit_one, cot, w_co, w_in, w_out, biases, ffn_bias, gain, shift, rows=256, chunk=512):
    n, d = o.shape
    ff = w_in.shape[1]
    block = pl.BlockSpec((rows, d), lambda i: (i, 0))
    wide = pl.BlockSpec((rows, ff), lambda i: (i, 0))
    low_shape = pltpu.HBM((n, d), bf16)
    return pl.pallas_call(
        functools.partial(ffn_kernel, chunk=chunk),
        grid=(n // rows,),
        in_specs=[block, block, block, whole(), whole(), whole()] + [whole()] * 4,
        out_specs=[block, wide, wide, block, block, block, block, block,
                   pl.BlockSpec((8, d), lambda i: (0, 0)), pl.BlockSpec((8, ff), lambda i: (0, 0))],
        out_shape=[
            low_shape,
            pltpu.HBM((n, ff), bf16),
            pltpu.HBM((n, ff), bf16),
            low_shape,
            low_shape,
            pltpu.HBM((n, d), f32),
            low_shape,
            low_shape,
            pltpu.HBM((8, d), f32),
            pltpu.HBM((8, ff), f32),
        ],
        scratch_shapes=[pltpu.VMEM((rows, ff), f32)],
        compiler_params=params(48),
        cost_estimate=cost(8 * n * d * ff + 4 * n * d * d, 4 * d * ff + 4 * n * ff + 20 * n * d, 2 * n * ff),
        name="ffn",
    )(*hbm(o, unit_one, cot), w_co, w_in, w_out, biases, ffn_bias, gain, shift)


def before_self_kernel(g2, gqa, gqb, unit_ref, scale_ref, w_q, w_out, gain, g1_ref, b1_ref, gm_ref, gq_ref, sums_ref):
    @pl.when(pl.program_id(0) == 0)
    def _():
        sums_ref[...] = jnp.zeros_like(sums_ref)

    gq = jnp.concatenate([gqa[0], gqb[0]], axis=1)
    gq_ref[...] = gq
    g = g2[...] + dot(gq, w_q[...], NT)
    unit = unit_ref[...]
    grad = norm_back(g, unit, scale_ref[:, 0:1], gain[0:1, :])
    g1_ref[...] = grad
    branch = grad.astype(bf16)
    b1_ref[...] = branch
    sums_ref[0:1, :] += row_sum(g * unit)
    sums_ref[1:2, :] += row_sum(g)
    sums_ref[2:3, :] += row_sum(grad)
    gm_ref[...] = dot(branch, w_out[...], NT).astype(bf16)


def before_self(g2, gqa, gqb, unit, scale, w_q, w_out, gain, rows=256):
    n, d = g2.shape
    block = pl.BlockSpec((rows, d), lambda i: (i, 0))
    return pl.pallas_call(
        before_self_kernel,
        grid=(n // rows,),
        in_specs=[block, pl.BlockSpec((1, rows, d // 2), lambda i: (0, i, 0)), pl.BlockSpec((1, rows, d // 2), lambda i: (0, i, 0)), block, pl.BlockSpec((rows, 128), lambda i: (i, 0)), whole(), whole(), whole()],
        out_specs=[block, block, block, block, pl.BlockSpec((8, d), lambda i: (0, 0))],
        out_shape=[
            pltpu.HBM((n, d), f32),
            pltpu.HBM((n, d), bf16),
            pltpu.HBM((n, d), bf16),
            pltpu.HBM((n, d), bf16),
            pltpu.HBM((8, d), f32),
        ],
        compiler_params=params(32),
        cost_estimate=cost(4 * n * d * d, 4 * d * d + 18 * n * d),
        name="before_self",
    )(*hbm(g2, gqa, gqb, unit, scale), w_q, w_out, gain)


TN = (((0,), (0,)), ((), ()))


def store_units(place, value, unit, send_ref, own_ref, first=0, z_local=False):
    mx, mz, my, core = place[0], place[1], place[2], place[3]
    half = value.shape[1] // 2
    for mine in range(2):
        @pl.when(core == mine)
        def _():
            for u in range(value.shape[0] // unit):
                ref = own_ref if u % 2 == mine else send_ref
                z = 0 if z_local else jnp.bitwise_xor(u // 4, mz)
                y = jnp.bitwise_xor((u // 2) % 2, my)
                for x in range(2):
                    ref[y, jnp.bitwise_xor(x, mx), z, :unit] = value[u * unit : (u + 1) * unit, x * half : (x + 1) * half]


def tall_kernel(place, a, b, send_ref, own_ref, *, unit):
    value = dot(a[...], b[...], TN).astype(bf16)
    store_units(place, value, unit, send_ref, own_ref, z_local=True)


def tall_grad(place, a, b, nb):
    n, rows = a.shape
    cols = b.shape[1]
    nz = nb // 4
    unit = rows // nb
    out = pltpu.HBM((2, 2, nz, unit, cols // 2), bf16)
    spec = pl.BlockSpec((2, 2, 1, unit, cols // 2), lambda z, p: (0, 0, jnp.bitwise_xor(z, p[1]), 0, 0))
    return pl.pallas_call(
        functools.partial(tall_kernel, unit=unit),
        grid_spec=pltpu.PrefetchScalarGridSpec(
            num_scalar_prefetch=1,
            grid=(nz,),
            in_specs=[pl.BlockSpec((n, rows // nz), lambda z, p: (0, z)), pl.BlockSpec((n, cols), lambda z, p: (0, 0))],
            out_specs=[spec, spec],
        ),
        out_shape=[out, out],
        compiler_params=params(24),
        cost_estimate=cost(2 * n * rows * cols, 2 * (n * rows + n * cols + rows * cols)),
        name="tall_grad",
    )(place, *hbm(a, b))


def wide_kernel(place, *refs, steps, unit):
    send_ref, own_ref = refs[-2:]
    j = pl.program_id(0)
    for a_at, left, right, first, count in steps:
        @pl.when((j >= first) & (j < first + count))
        def _(a_at=a_at, left=left, right=right):
            flat = lambda r: refs[r][...].reshape(refs[r].shape[-2:])
            value = dot(refs[a_at][...], jnp.concatenate([flat(left), flat(right)], axis=1), TN).astype(bf16)
            store_units(place, value, unit, send_ref, own_ref)


def wide_grad(place, terms, nb, block=384):
    n, rows = terms[0][0].shape
    unit = rows // nb
    arrays, specs, steps, first = [], [], [], 0
    whole_a = pl.BlockSpec((n, rows), lambda j, p: (0, 0))
    for a, b, leads in terms:
        if not any(a is other for other in arrays):
            arrays.append(a)
            specs.append(whole_a)
        a_at = next(i for i, other in enumerate(arrays) if other is a)
        count = b.shape[-1] // block // (1 if leads else 2)
        for side in range(2):
            def where(j, p, first=first, count=count, side=side, leads=leads):
                inside = jnp.clip(j - first, 0, count - 1)
                return (leads[side], 0, inside) if leads else (0, side * count + inside)
            arrays.append(b)
            specs.append(pl.BlockSpec((1, n, block) if leads else (n, block), where))
        steps.append((a_at, len(arrays) - 2, len(arrays) - 1, first, count))
        first += count
    steps = [(a, l, r, f, c) for a, l, r, f, c in steps]
    out = pltpu.HBM((2, 2, nb // 4, unit, first * block), bf16)
    spec = pl.BlockSpec((2, 2, nb // 4, unit, block), lambda j, p: (0, 0, 0, 0, j))
    return pl.pallas_call(
        functools.partial(wide_kernel, steps=steps, unit=unit),
        grid_spec=pltpu.PrefetchScalarGridSpec(
            num_scalar_prefetch=1, grid=(first,), in_specs=specs, out_specs=[spec, spec]
        ),
        out_shape=[out, out],
        compiler_params=params(40),
        cost_estimate=cost(4 * n * rows * first * block, 4 * rows * first * block + 4 * n * first * block),
        name="wide_grad",
    )(place, *hbm(*arrays))


def grad_rows_kernel(place, *refs, columns, based):
    gs, weight = refs[: len(columns)], refs[len(columns)]
    out_ref = refs[-1]
    value = None
    for g, chunks in zip(gs, columns):
        for m, starts in enumerate(chunks):
            if not starts:
                continue
            w = [weight[:, s : s + size] for s, size in starts]
            w = w[0] if len(w) == 1 else jnp.concatenate(w, axis=1)
            term = dot(g[m], w, NT)
            value = term if value is None else value + term
    if based:
        value = value + refs[len(columns) + 1][...]

    out_ref[...] = value.astype(out_ref.dtype)


def grad_rows(place, terms, columns, weight, base, mine, rows=256):
    n = terms[0].shape[1]
    d, k = weight.shape
    steps = n // 2 // rows
    half = lambda i, p: (p[0] if mine else 1 - p[0]) * steps + i
    ins = [pl.BlockSpec((t.shape[0], rows, t.shape[2]), lambda i, p: (0, half(i, p), 0)) for t in terms] + [whole()]
    args = hbm(*terms) + [weight]
    if base is not None:
        ins.append(pl.BlockSpec((rows, d), lambda i, p: (half(i, p), 0)))
        args += hbm(base)
    return pl.pallas_call(
        functools.partial(grad_rows_kernel, columns=columns, based=base is not None),
        grid_spec=pltpu.PrefetchScalarGridSpec(
            num_scalar_prefetch=1,
            grid=(steps,),
            in_specs=ins,
            out_specs=pl.BlockSpec((rows, d), lambda i, p: (i, 0)),
        ),
        out_shape=pltpu.HBM((n // 2, d), f32 if mine else bf16),
        compiler_params=params(40),
        cost_estimate=cost(n * k * d, n * k + 2 * k * d + 4 * n * d),
        name="grad_rows",
    )(place, *args)


def route(nb, move):
    dz, dy, dc, dx = move
    pairs = []
    for b in range(nb):
        z, y, core = b // 4, (b // 2) % 2, b % 2
        for x in range(2):
            target = (z ^ dz) * 4 + (y ^ dy) * 2 + (core ^ dc)
            pairs.append((b * 2 + x, target * 2 + (x ^ dx)))
    return pairs


def send(value, nb, move):
    return lax.ppermute(value, ("batch", "seq"), route(nb, move))


def core_stage(buffers, nb):
    to_send, own = buffers
    return own, send(to_send, nb, (0, 0, 1, 0))


def y_prepare(state):
    own, got = state
    return (own[1].astype(f32) + got[1].astype(f32)).astype(bf16), (own, got)


def y_move(value, nb):
    return send(value, nb, (0, 1, 0, 0))


def x_prepare(state):
    own, got, more = state
    total = own[0].astype(f32) + got[0].astype(f32) + more.astype(f32)
    return total[0].astype(bf16), total[1].astype(bf16)


def x_move(value, nb):
    return send(value, nb, (0, 0, 0, 1))


def z_prepare(state):
    kept, got = state
    total = kept.astype(f32) + got.astype(f32)
    return total[0::2].astype(bf16), total[1::2].astype(bf16)


def z_move(value, nb, bit):
    return send(value, nb, (1 << bit, 0, 0, 0))


def after_y(state):
    own, got, more = state
    return (own[0].astype(f32) + got[0].astype(f32) + more.astype(f32)).astype(bf16)


def direct_z(total, nb):
    result = total[:, 0].astype(f32)
    for d in range(1, nb // 4):
        result = result + send(total[:, d], nb, (d, 0, 0, 0)).astype(f32)
    return result


def at(value, index, axis):
    return lax.dynamic_index_in_dim(value, index, axis, keepdims=False)


def last_stage(state):
    kept, got = state
    return (kept.astype(f32) + got.astype(f32))[0]


def tie(*values):
    return lax.optimization_barrier(values)


def swap(value):
    return lax.ppermute(value, "seq", [(0, 1), (1, 0)])


def split_pairs(local):
    positions, _, width = local.shape
    pairs = local.reshape(positions, 2 * width)
    x = lax.axis_index("seq")
    return pairs, lax.dynamic_slice(pairs, (0, (1 - x) * width), (positions, width))


def join_pairs(mine, got):
    x = lax.axis_index("seq")
    got = got.astype(mine.dtype)
    both = jnp.concatenate([jnp.where(x == 0, mine, got), jnp.where(x == 0, got, mine)], axis=1)
    return both.reshape(mine.shape[0], 2, mine.shape[1])


def whole_sequence(pairs, got):
    x = lax.axis_index("seq")
    width = got.shape[1]
    mine = lax.dynamic_slice(pairs, (0, x * width), got.shape)
    return jnp.where(x == 0, jnp.concatenate([mine, got]), jnp.concatenate([got, mine]))


def per_device_fast(
    hidden_in,
    memory,
    src_len,
    out_grad,
    w_self_qkv,
    w_self_out,
    w_cross_q,
    w_cross_kv,
    w_cross_out,
    w_ffn_in,
    w_ffn_out,
    biases,
    ffn_bias,
    norm_gain,
    norm_shift,
):
    nb = lax.axis_size("batch")
    width = hidden_in.shape[2]
    half = width // 2
    x, b = lax.axis_index("seq"), lax.axis_index("batch")
    place = jnp.stack([x, b // 4, (b // 2) % 2, b % 2]).astype(jnp.int32)
    length = lax.dynamic_slice_in_dim(src_len, x, 1)

    pairs, other = split_pairs(hidden_in)
    got = swap(other)
    memory_pairs, memory_other = split_pairs(memory)
    memory_got = swap(memory_other)
    cot_pairs, cot_other = split_pairs(out_grad)
    tokens, query_self, key_self, value_self = project(
        place, pairs, got, w_self_qkv, biases, ((0, 0.125), (None, 1.0), (1, 1.0))
    )
    query_self, cot_other = tie(query_self, cot_other)
    cot_got = swap(cot_other)
    out_self, lp_self = attn_fwd(length, query_self, key_self, value_self, True)
    unit_one, scale_one, low_one, query_cross = after_self(
        out_self, tokens, w_self_out, w_cross_q, biases, norm_gain, norm_shift
    )
    sources, key_cross, value_cross = project(
        place, memory_pairs, memory_got, w_cross_kv, biases, ((None, 1.0), (4, 1.0))
    )
    out_cross, lp_cross = attn_fwd(length, query_cross, key_cross, value_cross, False)
    cotangent = whole_sequence(cot_pairs, cot_got)
    layer, active, grad_pre, low_two, branch_three, grad_two, branch_two, grad_mixed, sums_ffn, bias_sums = ffn(
        out_cross, unit_one, cotangent, w_cross_out, w_ffn_in, w_ffn_out, biases, ffn_bias[None], norm_gain, norm_shift
    )
    span = layer.shape[0] // 2

    one = tall_grad(place, active, branch_three, nb)
    one, low_two = tie(one, low_two)
    one = core_stage(one, nb)
    two = wide_grad(place, [(low_two, grad_pre, None), (out_cross, branch_two, None)], nb)

    two, one, grad_mixed = tie(two, one, grad_mixed)
    two = core_stage(two, nb)
    one_out, one = y_prepare(one)
    one_out, grad_mixed = tie(one_out, grad_mixed)
    one = one + (y_move(one_out, nb),)
    back = partial(attn_bwd, length, query_cross, key_cross, value_cross, out_cross)
    cross_a, sums_ca = back(grad_mixed, lp_cross, False, 0, 1, 3)

    cross_a, two, grad_mixed = tie(cross_a, two, grad_mixed)
    two_out, two = y_prepare(two)
    layer_other = lax.dynamic_slice_in_dim(layer, (1 - x) * span, span, 0)
    two_out, layer_other, grad_mixed = tie(two_out, layer_other, grad_mixed)
    two = two + (y_move(two_out, nb),)
    layer_got = swap(layer_other)
    cross_b, sums_cb = back(grad_mixed, lp_cross, False, 3, 1, 3)

    cross_b, one = tie(cross_b, one)
    one_keep, one_out = x_prepare(one)
    one_out, cross_b = tie(one_out, cross_b)
    one = one_keep, x_move(one_out, nb)
    grad_one, branch_one, grad_mixed, gq_cross, sums_one = before_self(
        grad_two, cross_a, cross_b, unit_one, scale_one, w_cross_q, w_self_out, norm_gain
    )
    three = wide_grad(
        place,
        [(out_self, branch_one, None), (low_one, gq_cross, None), (sources, cross_a, (1, 2)), (sources, cross_b, (1, 2))],
        nb,
    )

    three, cross_a, one = tie(three, cross_a, one)
    three = core_stage(three, nb)
    one_keep, one_out = z_prepare(one)
    one_out, cross_a = tie(one_out, cross_a)
    one = one_keep, z_move(one_out, nb, 0)
    spots = [((), ((0, 384),), ((width, 384),)), ((), ((384, 384),), ((width + 384, 384),))]
    other = grad_rows(place, [cross_a, cross_b], spots, w_cross_kv, None, False)

    other, three, two, grad_mixed = tie(other, three, two, grad_mixed)
    three_out, three = y_prepare(three)
    two_keep, two_out = x_prepare(two)
    three_out, two_out, grad_mixed = tie(three_out, two_out, grad_mixed)
    three = three + (y_move(three_out, nb),)
    two = two_keep, x_move(two_out, nb)
    memory_back = swap(other)
    back = partial(attn_bwd, length, query_self, key_self, value_self, out_self)
    self_a, sums_sa, *four = back(
        grad_mixed, lp_self, True, 0, 3, 2, tokens, place, nb, "early", (sums_one, sums_ca, sums_cb, sums_ffn, bias_sums)
    )

    self_a, four, one, cross_a = tie(self_a, four, one, cross_a)
    four = core_stage(four, nb)
    one_keep, one_out = z_prepare(one)
    one_out, cross_a = tie(one_out, cross_a)
    one = one_keep, z_move(one_out, nb, 1)
    memory_mine = grad_rows(place, [cross_a, cross_b], spots, w_cross_kv, None, True)

    two, four, grad_mixed, memory_mine = tie(two, four, grad_mixed, memory_mine)
    four_out, four = y_prepare(four)
    two_keep, two_out = z_prepare(two)
    two_out, four_out, grad_mixed = tie(two_out, four_out, grad_mixed)
    four = four + (y_move(four_out, nb),)
    two = two_keep, z_move(two_out, nb, 0)
    self_b, sums_sb, *five = back(grad_mixed, lp_self, True, 1, 3, 2, tokens, place, nb)

    self_b, five, three, two, grad_mixed = tie(self_b, five, three, two, grad_mixed)
    five = core_stage(five, nb)
    three_keep, three_out = x_prepare(three)
    two_keep, two_out = z_prepare(two)
    three_out, two_out, grad_mixed = tie(three_out, two_out, grad_mixed)
    three = three_keep, x_move(three_out, nb)
    two = two_keep, z_move(two_out, nb, 1)
    self_c, sums_sc, *six = back(grad_mixed, lp_self, True, 2, 3, 2, tokens, place, nb, "late", (sums_sa, sums_sb))

    self_c, six, five, four, three = tie(self_c, six, five, four, three)
    six = core_stage(six, nb)
    five_out, five = y_prepare(five)
    four_keep, four_out = x_prepare(four)
    three_keep, three_out = z_prepare(three)
    five_out, four_out, three_out, self_c = tie(five_out, four_out, three_out, self_c)
    five = five + (y_move(five_out, nb),)
    four = four_keep, x_move(four_out, nb)
    three = three_keep, z_move(three_out, nb, 0)
    spots = [tuple(tuple((m * width + (i + s) * 128, 128) for s in (0, 3)) for m in range(3)) for i in range(3)]
    other = grad_rows(place, [self_a, self_b, self_c], spots, w_self_qkv, grad_one, False)

    other, six, grad_one = tie(other, six, grad_one)
    six_out, six = y_prepare(six)
    six_out, other, grad_one = tie(six_out, other, grad_one)
    six = six + (y_move(six_out, nb),)
    in_back = swap(other)
    mine = grad_rows(place, [self_a, self_b, self_c], spots, w_self_qkv, grad_one, True)

    mine, six, five, four, three, layer_got, memory_back = tie(mine, six, five, four, three, layer_got, memory_back)
    six_out = after_y(six)
    five_out = after_y(five)
    both = jnp.concatenate([six_out, five_out], axis=2)
    both = direct_z(both, nb)
    four_keep, four_out = z_prepare(four)
    three_keep, three_out = z_prepare(three)
    four = four_keep, z_move(four_out, nb, 0)
    three = three_keep, z_move(three_out, nb, 1)
    layer_out = join_pairs(lax.dynamic_slice_in_dim(layer, x * span, span, 0), layer_got)
    grad_memory = join_pairs(memory_mine, memory_back)
    both = both[0] + x_move(both[1].astype(bf16), nb).astype(f32)
    four_keep, four_out = z_prepare(four)
    four = last_stage((four_keep, z_move(four_out, nb, 1)))
    grad_in = join_pairs(mine, in_back)
    group = last_stage(three)
    grad_ffn_out = last_stage(one)
    grad_ffn_in = last_stage(two)
    unit = width // nb
    ends = unit, both.shape[0] - unit
    thirds = [s.reshape(unit, 3, 128) for s in (four[:unit], both[ends[1] :], both[: ends[0]])]
    grad_self_qkv = jnp.stack(thirds, axis=2).reshape(unit, 9 * 128)
    late = both[ends[0] : ends[0] + 6, :256].reshape(3, 2, 2, 128)
    late = at(late, x, 2).swapaxes(0, 1).reshape(2, half)
    early = lax.dynamic_slice_in_dim(four[unit:], x * 16, 16, 0)
    vectors = jnp.concatenate([late, early[:11]])
    bias_total = early[11 : 11 + bias_sums.shape[1] // width].reshape(-1)
    return (
        layer_out,
        grad_in,
        grad_memory,
        grad_self_qkv,
        group[:, :half],
        group[:, half : 2 * half],
        group[:, 2 * half :],
        grad_ffn_in[:, -half:],
        grad_ffn_in[:, :-half],
        grad_ffn_out,
        vectors[0:7],
        bias_total,
        vectors[7:10],
        vectors[10:13],
    )


def solution(mesh):
    devices = dict(mesh.shape)

    in_specs = (
        P("seq", "batch", None),
        P("seq", "batch", None),
        P("batch"),
        P("seq", "batch", None),
        P(),
        P(),
        P(),
        P(),
        P(),
        P(),
        P(),
        P(),
        P(),
        P(),
        P(),
    )
    out_specs = (
        P("seq", "batch", None),
        P("seq", "batch", None),
        P("seq", "batch", None),
        P("batch", "seq"),
        P("batch", "seq"),
        P("batch", "seq"),
        P("batch", "seq"),
        P("batch", "seq"),
        P("batch", "seq"),
        P("batch", "seq"),
        P(None, "seq"),
        P("seq"),
        P(None, "seq"),
        P(None, "seq"),
    )
    nb, ns = devices["batch"], devices["seq"]

    def per_device(hidden_in, *rest):
        whole = ns == 2 and hidden_in.shape[1] == 2 and nb % 4 == 0 and nb & (nb - 1) == 0
        return (per_device_fast if whole else per_device_general)(hidden_in, *rest)

    return jax.shard_map(
        per_device, mesh=mesh, in_specs=in_specs, out_specs=out_specs, check_vma=False
    )
```

```python
import functools
from functools import partial

import jax
import jax.numpy as jnp
from jax import lax
from jax.experimental import pallas as pl
from jax.experimental.pallas import tpu as pltpu
from jax.sharding import PartitionSpec as P

H = 12


NEGATIVE = -1e30


def from_behind(value, axis, steps):
    count = lax.axis_size(axis)
    pairs = [(source, (source + steps) % count) for source in range(count)]
    return lax.ppermute(value, axis, pairs)


def shifted(block, axis, distance):
    devices = range(lax.axis_size(axis))
    route = [(i - distance, i) for i in devices if i - distance in devices]
    return lax.ppermute(block, axis, route)


def contract_rows(left, right):
    return lax.dot_general(
        left, right, (((0,), (0,)), ((), ())), preferred_element_type=jnp.float32
    )


def times_transposed(grad, weight):
    return lax.dot_general(
        grad, weight, (((1,), (1,)), ((), ())), preferred_element_type=jnp.float32
    )


def norm_forward(value, gain, shift):
    mean = jnp.mean(value, axis=-1, keepdims=True)
    centred = value - mean
    scale = lax.rsqrt(jnp.mean(centred * centred, axis=-1, keepdims=True) + 1e-05)
    unit = centred * scale
    return (unit * gain + shift, unit, scale)


def norm_backward(grad, unit, scale, gain):
    weighted = grad * gain
    inner = (
        weighted
        - jnp.mean(weighted, axis=-1, keepdims=True)
        - unit * jnp.mean(weighted * unit, axis=-1, keepdims=True)
    )
    return (scale * inner, jnp.sum(grad * unit, axis=0), jnp.sum(grad, axis=0))


def allowed_keys(query_pos, key_pos, lengths, causal):
    if causal:
        return (query_pos[:, None] >= key_pos[None, :])[None, None]
    return (key_pos[None, :] < lengths[:, None])[:, None, None, :]


def attend_forward(query, keys, values, lengths, causal, heads):
    span, batch, width = query.shape
    size = width // heads
    query_heads = query.reshape(span, batch, heads, size)
    query_pos = lax.axis_index("seq") * span + lax.iota(jnp.int32, span)

    def block(carry, key_block, value_block, first):
        previous, total, summed = carry
        rows = key_block.shape[0]
        key_pos = first + lax.iota(jnp.int32, rows)
        scores = jnp.einsum(
            "qshd,kshd->shqk",
            query_heads,
            key_block.reshape(rows, batch, heads, size),
            preferred_element_type=jnp.float32,
        )
        allowed = allowed_keys(query_pos, key_pos, lengths, causal)
        top = jnp.maximum(previous, jnp.max(jnp.where(allowed, scores, NEGATIVE), axis=-1))
        weights = jnp.where(allowed, jnp.exp(scores - top[..., None]), 0.0)
        rescale = jnp.exp(previous - top)
        total = total * rescale + jnp.sum(weights, axis=-1)
        summed = summed * rescale[..., None] + jnp.einsum(
            "shqk,kshd->shqd",
            weights.astype(jnp.bfloat16),
            value_block.reshape(rows, batch, heads, size),
            preferred_element_type=jnp.float32,
        )
        return (top, total, summed)

    def fold(carry, piece):
        key_piece, value_piece = piece
        rows = key_piece.shape[0]
        count = rows // span
        firsts = span * lax.iota(jnp.int32, count)

        def inner(state, parts):
            return (block(state, parts[0], parts[1], parts[2]), None)

        carry, unused = lax.scan(
            inner,
            carry,
            (
                key_piece.reshape(count, span, batch, width),
                value_piece.reshape(count, span, batch, width),
                firsts,
            ),
        )
        return carry

    empty = (
        jnp.full((batch, heads, span), NEGATIVE, jnp.float32),
        jnp.zeros((batch, heads, span), jnp.float32),
        jnp.zeros((batch, heads, span, size), jnp.float32),
    )
    if causal:
        top, total, summed = fold(
            empty,
            (
                lax.all_gather(keys, "seq", axis=0, tiled=True),
                lax.all_gather(values, "seq", axis=0, tiled=True),
            ),
        )
    else:
        top, total, summed = fold(
            empty,
            (
                lax.all_gather(keys, "seq", axis=0, tiled=True),
                lax.all_gather(values, "seq", axis=0, tiled=True),
            ),
        )
    mixed = summed / total[..., None]
    mixed = jnp.transpose(mixed, (2, 0, 1, 3)).reshape(span, batch, width)
    return (mixed, top + jnp.log(total))


def block_backward(
    query_heads, grad_heads, delta, logsum, key_block, value_block, allowed, batch, heads, size
):
    span = key_block.shape[0]
    width = heads * size
    key_heads = key_block.reshape(span, batch, heads, size)
    value_heads = value_block.reshape(span, batch, heads, size)
    scores = jnp.einsum(
        "qshd,kshd->shqk", query_heads, key_heads, preferred_element_type=jnp.float32
    )
    weights = jnp.where(allowed, jnp.exp(scores - logsum[..., None]), 0.0)
    grad_weights = jnp.einsum(
        "qshd,kshd->shqk", grad_heads, value_heads, preferred_element_type=jnp.float32
    )
    grad_scores = (weights * (grad_weights - delta[..., None])).astype(jnp.bfloat16)
    grad_query = jnp.einsum(
        "shqk,kshd->qshd", grad_scores, key_heads, preferred_element_type=jnp.float32
    )
    grad_keys = jnp.einsum(
        "shqk,qshd->kshd", grad_scores, query_heads, preferred_element_type=jnp.float32
    ).reshape(span, batch, width)
    grad_values = jnp.einsum(
        "shqk,qshd->kshd",
        weights.astype(jnp.bfloat16),
        grad_heads,
        preferred_element_type=jnp.float32,
    ).reshape(span, batch, width)
    return (grad_query, grad_keys, grad_values)


def attend_backward(query, keys, values, mixed, grad_mixed, logsum, lengths, causal, heads):
    span, batch, width = query.shape
    size = width // heads
    query_heads = query.reshape(span, batch, heads, size)
    grad_heads = grad_mixed.reshape(span, batch, heads, size)
    delta = jnp.sum(
        grad_heads.astype(jnp.float32) * mixed.reshape(span, batch, heads, size), axis=-1
    )
    delta = jnp.transpose(delta, (1, 2, 0))
    devices = lax.axis_size("seq")
    place = lax.axis_index("seq")
    query_pos = place * span + lax.iota(jnp.int32, span)
    grad_query = jnp.zeros((span, batch, heads, size), jnp.float32)
    grad_keys = jnp.zeros((span, batch, width), jnp.float32)
    grad_values = jnp.zeros((span, batch, width), jnp.float32)
    key_block, value_block = (keys, values)
    for step in range(devices):
        owner = (place - step + devices) % devices
        key_pos = owner * span + lax.iota(jnp.int32, span)
        allowed = allowed_keys(query_pos, key_pos, lengths, causal)
        part_query, part_keys, part_values = block_backward(
            query_heads,
            grad_heads,
            delta,
            logsum,
            key_block,
            value_block,
            allowed,
            batch,
            heads,
            size,
        )
        grad_query = grad_query + part_query
        grad_keys = grad_keys + part_keys
        grad_values = grad_values + part_values
        if causal:
            grad_keys, grad_values = (
                from_behind(grad_keys.astype(jnp.bfloat16), "seq", 1).astype(grad_keys.dtype),
                from_behind(grad_values.astype(jnp.bfloat16), "seq", 1).astype(grad_values.dtype),
            )
        else:
            grad_keys, grad_values = (
                from_behind(grad_keys.astype(jnp.bfloat16), "seq", 1).astype(grad_keys.dtype),
                from_behind(grad_values.astype(jnp.bfloat16), "seq", 1).astype(grad_values.dtype),
            )
        if step + 1 < devices:
            if causal:
                key_block, value_block = shifted((key_block, value_block), "seq", 1)
            else:
                key_block, value_block = from_behind((key_block, value_block), "seq", 1)
    return (grad_query.reshape(span, batch, width), grad_keys, grad_values)


def per_device_general(
    hidden_in,
    memory,
    src_len,
    out_grad,
    w_self_qkv,
    w_self_out,
    w_cross_q,
    w_cross_kv,
    w_cross_out,
    w_ffn_in,
    w_ffn_out,
    biases,
    ffn_bias,
    norm_gain,
    norm_shift,
):
    span, batch, width = hidden_in.shape
    heads = H
    rows = span * batch
    layout = (span, batch, width)
    tokens = hidden_in.reshape(rows, width)
    sources = memory.reshape(rows, width)
    joined = jnp.dot(tokens, w_self_qkv, preferred_element_type=jnp.float32)
    query_self = ((joined[:, :width] + biases[0]) * 0.125).astype(jnp.bfloat16)
    key_self = joined[:, width : 2 * width].astype(jnp.bfloat16)
    value_self = (joined[:, 2 * width :] + biases[1]).astype(jnp.bfloat16)
    mixed_self, logsum_self = attend_forward(
        query_self.reshape(layout),
        key_self.reshape(layout),
        value_self.reshape(layout),
        src_len,
        True,
        heads,
    )
    out_self = mixed_self.reshape(rows, width).astype(jnp.bfloat16)
    resid_one = (
        tokens.astype(jnp.float32)
        + jnp.dot(out_self, w_self_out, preferred_element_type=jnp.float32)
        + biases[2]
    )
    normed_one, unit_one, scale_one = norm_forward(resid_one, norm_gain[0], norm_shift[0])
    normed_one_low = normed_one.astype(jnp.bfloat16)
    query_cross = (
        (jnp.dot(normed_one_low, w_cross_q, preferred_element_type=jnp.float32) + biases[3]) * 0.125
    ).astype(jnp.bfloat16)
    pair = jnp.dot(sources, w_cross_kv, preferred_element_type=jnp.float32)
    key_cross = pair[:, :width].astype(jnp.bfloat16)
    value_cross = (pair[:, width:] + biases[4]).astype(jnp.bfloat16)
    mixed_cross, logsum_cross = attend_forward(
        query_cross.reshape(layout),
        key_cross.reshape(layout),
        value_cross.reshape(layout),
        src_len,
        False,
        heads,
    )
    out_cross = mixed_cross.reshape(rows, width).astype(jnp.bfloat16)
    resid_two = (
        normed_one + jnp.dot(out_cross, w_cross_out, preferred_element_type=jnp.float32) + biases[5]
    )
    normed_two, unit_two, scale_two = norm_forward(resid_two, norm_gain[1], norm_shift[1])
    normed_two_low = normed_two.astype(jnp.bfloat16)
    inner = jnp.dot(normed_two_low, w_ffn_in, preferred_element_type=jnp.float32) + ffn_bias
    active = jax.nn.gelu(inner, approximate=False).astype(jnp.bfloat16)
    resid_three = (
        normed_two + jnp.dot(active, w_ffn_out, preferred_element_type=jnp.float32) + biases[6]
    )
    result, unit_three, scale_three = norm_forward(resid_three, norm_gain[2], norm_shift[2])
    layer_out = result.astype(jnp.bfloat16).reshape(layout)
    grad_three, gain_three, shift_three = norm_backward(
        out_grad.reshape(rows, width).astype(jnp.float32), unit_three, scale_three, norm_gain[2]
    )
    branch_three = grad_three.astype(jnp.bfloat16)
    hidden_pre, hidden_act = (inner, active)
    grad_ffn_out = contract_rows(hidden_act, branch_three)
    grad_act = times_transposed(branch_three, w_ffn_out)
    unused, pull = jax.vjp(partial(jax.nn.gelu, approximate=False), hidden_pre)
    grad_pre = pull(grad_act)[0].astype(jnp.bfloat16)
    grad_ffn_in = contract_rows(normed_two_low, grad_pre)
    grad_normed_two = grad_three + times_transposed(grad_pre, w_ffn_in)
    grad_two, gain_two, shift_two = norm_backward(
        grad_normed_two, unit_two, scale_two, norm_gain[1]
    )
    branch_two = grad_two.astype(jnp.bfloat16)
    grad_cross_out = contract_rows(out_cross, branch_two)
    grad_mixed_cross = times_transposed(branch_two, w_cross_out).astype(jnp.bfloat16)
    raw_query, grad_keys, grad_values = attend_backward(
        query_cross.reshape(layout),
        key_cross.reshape(layout),
        value_cross.reshape(layout),
        mixed_cross,
        grad_mixed_cross.reshape(layout),
        logsum_cross,
        src_len,
        False,
        heads,
    )
    grad_query_cross = (raw_query.reshape(rows, width) * 0.125).astype(jnp.bfloat16)
    grad_pair = jnp.concatenate(
        [
            grad_keys.reshape(rows, width).astype(jnp.bfloat16),
            grad_values.reshape(rows, width).astype(jnp.bfloat16),
        ],
        axis=1,
    )
    grad_cross_q = contract_rows(normed_one_low, grad_query_cross)
    grad_cross_kv = contract_rows(sources, grad_pair)
    grad_memory = times_transposed(grad_pair, w_cross_kv).reshape(layout)
    grad_normed_one = grad_two + times_transposed(grad_query_cross, w_cross_q)
    grad_one, gain_one, shift_one = norm_backward(
        grad_normed_one, unit_one, scale_one, norm_gain[0]
    )
    branch_one = grad_one.astype(jnp.bfloat16)
    grad_self_out = contract_rows(out_self, branch_one)
    grad_mixed_self = times_transposed(branch_one, w_self_out).astype(jnp.bfloat16)
    raw_query, grad_keys, grad_values = attend_backward(
        query_self.reshape(layout),
        key_self.reshape(layout),
        value_self.reshape(layout),
        mixed_self,
        grad_mixed_self.reshape(layout),
        logsum_self,
        src_len,
        True,
        heads,
    )
    grad_joined = jnp.concatenate(
        [
            (raw_query.reshape(rows, width) * 0.125).astype(jnp.bfloat16),
            grad_keys.reshape(rows, width).astype(jnp.bfloat16),
            grad_values.reshape(rows, width).astype(jnp.bfloat16),
        ],
        axis=1,
    )
    grad_self_qkv = contract_rows(tokens, grad_joined)
    grad_in = (grad_one + times_transposed(grad_joined, w_self_qkv)).reshape(layout)
    vector_terms = jnp.stack(
        [
            jnp.sum(grad_joined[:, :width].astype(jnp.float32), axis=0),
            jnp.sum(grad_joined[:, 2 * width :].astype(jnp.float32), axis=0),
            jnp.sum(grad_one, axis=0),
            jnp.sum(grad_query_cross.astype(jnp.float32), axis=0),
            jnp.sum(grad_pair[:, width:].astype(jnp.float32), axis=0),
            jnp.sum(grad_two, axis=0),
            jnp.sum(grad_three, axis=0),
            gain_one,
            gain_two,
            gain_three,
            shift_one,
            shift_two,
            shift_three,
        ]
    )
    bias_terms = jnp.sum(grad_pre.astype(jnp.float32), axis=0)[None]
    (
        grad_self_qkv,
        grad_self_out,
        grad_cross_q,
        grad_cross_kv,
        grad_cross_out,
        grad_ffn_in,
        grad_ffn_out,
        vector_terms,
        bias_terms,
    ) = (
        lax.psum_scatter(
            grad_self_qkv.astype(jnp.bfloat16), "seq", scatter_dimension=1, tiled=True
        ).astype(jnp.float32),
        lax.psum_scatter(
            grad_self_out.astype(jnp.bfloat16), "seq", scatter_dimension=1, tiled=True
        ).astype(jnp.float32),
        lax.psum_scatter(
            grad_cross_q.astype(jnp.bfloat16), "seq", scatter_dimension=1, tiled=True
        ).astype(jnp.float32),
        lax.psum_scatter(
            grad_cross_kv.astype(jnp.bfloat16), "seq", scatter_dimension=1, tiled=True
        ).astype(jnp.float32),
        lax.psum_scatter(
            grad_cross_out.astype(jnp.bfloat16), "seq", scatter_dimension=1, tiled=True
        ).astype(jnp.float32),
        lax.psum_scatter(
            grad_ffn_in.astype(jnp.bfloat16), "seq", scatter_dimension=1, tiled=True
        ).astype(jnp.float32),
        lax.psum_scatter(
            grad_ffn_out.astype(jnp.bfloat16), "seq", scatter_dimension=1, tiled=True
        ).astype(jnp.float32),
        lax.psum_scatter(
            vector_terms.astype(jnp.bfloat16), "seq", scatter_dimension=1, tiled=True
        ).astype(jnp.float32),
        lax.psum_scatter(
            bias_terms.astype(jnp.bfloat16), "seq", scatter_dimension=1, tiled=True
        ).astype(jnp.float32),
    )
    (
        grad_self_qkv,
        grad_self_out,
        grad_cross_q,
        grad_cross_kv,
        grad_cross_out,
        grad_ffn_in,
        grad_ffn_out,
    ) = (
        lax.psum_scatter(
            grad_self_qkv.astype(jnp.bfloat16), "batch", scatter_dimension=0, tiled=True
        ).astype(jnp.float32),
        lax.psum_scatter(
            grad_self_out.astype(jnp.bfloat16), "batch", scatter_dimension=0, tiled=True
        ).astype(jnp.float32),
        lax.psum_scatter(
            grad_cross_q.astype(jnp.bfloat16), "batch", scatter_dimension=0, tiled=True
        ).astype(jnp.float32),
        lax.psum_scatter(
            grad_cross_kv.astype(jnp.bfloat16), "batch", scatter_dimension=0, tiled=True
        ).astype(jnp.float32),
        lax.psum_scatter(
            grad_cross_out.astype(jnp.bfloat16), "batch", scatter_dimension=0, tiled=True
        ).astype(jnp.float32),
        lax.psum_scatter(
            grad_ffn_in.astype(jnp.bfloat16), "batch", scatter_dimension=0, tiled=True
        ).astype(jnp.float32),
        lax.psum_scatter(
            grad_ffn_out.astype(jnp.bfloat16), "batch", scatter_dimension=0, tiled=True
        ).astype(jnp.float32),
    )
    vector_terms, bias_terms = lax.psum((vector_terms, bias_terms), "batch")
    return (
        layer_out,
        grad_in,
        grad_memory,
        grad_self_qkv,
        grad_self_out,
        grad_cross_q,
        grad_cross_kv,
        grad_cross_out,
        grad_ffn_in,
        grad_ffn_out,
        vector_terms[0:7],
        bias_terms[0],
        vector_terms[7:10],
        vector_terms[10:13],
    )


LOG2E = 1.4426950408889634
NN = (((1,), (0,)), ((), ()))
NT = (((1,), (1,)), ((), ()))
HD = 64
BIG = -1e30
f32, bf16 = jnp.float32, jnp.bfloat16

def dot(a, b, dims=NN):
    return lax.dot_general(a, b, dims, preferred_element_type=f32)

def lanes(shape):
    return lax.broadcasted_iota(jnp.int32, shape, len(shape) - 1)

def swap_halves(x):
    return jnp.concatenate([x[:, HD:], x[:, :HD]], axis=1)

def fwd_kernel(len_ref, q_ref, k_ref, v_ref, o_ref, lp_ref, acc_ref, *, causal, heads, qb, ahead):
    p = pl.program_id(0)
    n = q_ref.shape[0]
    nk = k_ref.shape[0]
    scaled = q_ref[...].astype(f32) * LOG2E
    hi = scaled.astype(bf16)
    lo = (scaled - hi.astype(f32)).astype(bf16)
    first = lanes((n, 128)) < HD
    hi_s, lo_s = swap_halves(hi), swap_halves(lo)
    q_aug = (jnp.where(first, hi, lo_s), jnp.where(first, hi_s, lo))
    kk = k_ref[...]
    k_s = swap_halves(kk)
    k_aug = [jnp.where(first, kk, k_s), jnp.where(first, k_s, kk)]
    if not causal:
        length = len_ref[0]
        row = lax.broadcasted_iota(jnp.int32, (nk, 128), 0)
        extra = jnp.where((row >= length) & (lanes((nk, 128)) == 0), BIG, 0.0).astype(bf16)
        k_aug = [jnp.concatenate([x, extra], axis=1) for x in k_aug]
        one = (lanes((n, 128)) == 0).astype(bf16)
        q_aug = [jnp.concatenate([x, one], axis=1) for x in q_aug]
    vt = jnp.transpose(v_ref[...])
    ones = jnp.ones((16, nk), bf16)
    va = [jnp.concatenate([vt[h * HD:(h + 1) * HD], ones], axis=0) for h in range(2)]

    def scores(c, h):
        top_k = (c + 1) * qb if causal else nk
        s = dot(k_aug[h][:top_k], q_aug[h][c * qb:(c + 1) * qb], NT)
        if causal:
            r = lax.broadcasted_iota(jnp.int32, (qb, qb), 0)
            d = jnp.where(r <= lanes((qb, qb)), s[c * qb:], BIG)
            s = jnp.concatenate([s[:c * qb], d], axis=0) if c else d
        return s

    steps = [(c, h) for c in range(n // qb) for h in range(2)]
    queue = [scores(*x) for x in steps[:ahead]]
    parts = []
    for i, (c, h) in enumerate(steps):
        if i + ahead < len(steps):
            queue.append(scores(*steps[i + ahead]))
        s = queue.pop(0)
        m = jnp.max(s, axis=0, keepdims=True)
        pt = jnp.exp2(s - m).astype(bf16)
        ot = dot(va[h][:, :s.shape[0]], pt)
        l = ot[HD:HD + 1]
        parts.append(ot[:HD] * (1.0 / l))
        acc_ref[pl.ds(2 * p + h, 1), c * qb:(c + 1) * qb] = m + jnp.log2(l)
        if h == 1:
            o_ref[c * qb:(c + 1) * qb, :] = jnp.transpose(jnp.concatenate(parts, axis=0)).astype(bf16)
            parts = []

    @pl.when(p == pl.num_programs(0) - 1)
    def _():
        rows = acc_ref[...]
        wide = jnp.concatenate([rows, jnp.zeros((128 - rows.shape[0], n), f32)], axis=0)
        cols = jnp.transpose(wide)
        a = cols.astype(bf16)
        cols = cols - a.astype(f32)
        b = cols.astype(bf16)
        c = (cols - b.astype(f32)).astype(bf16)
        lane = lanes((n, 128))
        sh = lambda x, k: jnp.concatenate([jnp.zeros((n, k), bf16), x[:, :128 - k]], axis=1)
        out = jnp.where(lane < 16, a, jnp.where(lane < 32, sh(b, 16), jnp.where(lane < 48, sh(c, 32), jnp.where(lane == 127, 1.0, 0.0).astype(bf16))))
        lp_ref[...] = out

def attn_fwd(length, q, k, v, causal, qb=256, ahead=2):
    n, d = q.shape
    blk = lambda r: pl.BlockSpec((r, 128), lambda p, l: (0, p))
    return pl.pallas_call(
        functools.partial(fwd_kernel, causal=causal, heads=d // HD, qb=qb, ahead=ahead),
        grid_spec=pltpu.PrefetchScalarGridSpec(
            num_scalar_prefetch=1, grid=(d // 128,),
            in_specs=[blk(n), blk(k.shape[0]), blk(k.shape[0])],
            out_specs=[blk(n), pl.BlockSpec((n, 128), lambda p, l: (0, 0))],
            scratch_shapes=[pltpu.VMEM((16, n), f32)]),
        out_shape=[pltpu.HBM((n, d), bf16), pltpu.HBM((n, 128), bf16)],
        compiler_params=params(40),
        cost_estimate=cost((n + 256) * n * 1024 // (2 if causal else 1) * (d // HD), 8 * n * d, n * n * d // HD),
        name="attn_fwd",
    )(length, *hbm(q, k, v))

def side_rows(kind, refs, own):
    if kind == "early":
        one, cross_a, cross_b, ffn, bias = refs
        both = lambda r: jnp.concatenate([cross_a[r : r + 1, :], cross_b[r : r + 1, :]], axis=1)
        rows = [one[2:3, :], both(0), both(1), ffn[5:6, :], ffn[2:3, :], one[0:1, :], ffn[3:4, :], ffn[0:1, :], one[1:2, :], ffn[4:5, :], ffn[1:2, :]]
        half = rows[0].shape[1] // 2
        wide = bias.shape[1] // 2
        sides = []
        for x in range(2):
            sides += [r[:, x * half : (x + 1) * half] for r in rows]
            sides += [bias[0:1, x * wide + c * half : x * wide + (c + 1) * half] for c in range(wide // half)]
            sides += [jnp.zeros((1, half), f32)] * (16 - len(rows) - wide // half)
        return jnp.concatenate(sides, axis=0).astype(bf16)
    rows = [refs[0][0:2, :], refs[1][0:2, :], own[0:2, :], jnp.zeros((10, own.shape[1]), f32)]
    rows = jnp.concatenate(rows, axis=0)
    return jnp.concatenate([rows, jnp.zeros((16, 128), f32)], axis=1).astype(bf16)


def bwd_kernel(len_ref, q_ref, k_ref, v_ref, o_ref, g_ref, lp_ref, *rest, causal, qb, first_pair, stride, unit, kind):
    if unit:
        place, tok_ref, *side, out_ref, sums_ref, send_ref, own_ref = rest
    else:
        out_ref, sums_ref = rest
    p = pl.program_id(0) * stride + first_pair
    n, nk = q_ref.shape[0], k_ref.shape[0]
    first = lanes((n, 128)) < HD
    q = q_ref[...]
    scaled = q.astype(f32) * LOG2E
    hi = scaled.astype(bf16)
    lo = (scaled - hi.astype(f32)).astype(bf16)
    hi_s, lo_s = swap_halves(hi), swap_halves(lo)
    lp = lp_ref[...]
    q_aug = [jnp.concatenate([x, lp], axis=1) for x in (jnp.where(first, hi, lo_s), jnp.where(first, hi_s, lo))]
    kk = k_ref[...]
    k_s = swap_halves(kk)
    v = v_ref[...]
    lane = lanes((nk, 128))
    g = g_ref[...]
    zero = jnp.zeros((), bf16)
    go = g.astype(f32) * o_ref[...].astype(f32)
    go_hi = go.astype(bf16)
    go_lo = (go - go_hi.astype(f32)).astype(bf16)
    br = lax.broadcasted_iota(jnp.int32, (128, 128), 0)
    bl = lanes((128, 128))
    pick = jnp.where(((bl < 3) & (br < HD)) | ((bl >= 3) & (bl < 6) & (br >= HD)), 1.0, 0.0).astype(bf16)
    dl = dot(go_hi, pick) + dot(go_lo, pick)
    da = dl.astype(bf16)
    rest = dl - da.astype(f32)
    db = rest.astype(bf16)
    dc = (rest - db.astype(f32)).astype(bf16)
    part = lanes((n, 128))
    part = jnp.where(part >= 3, part - 3, part)
    dpack = jnp.where(part == 0, da, jnp.where(part == 1, db, dc))
    g_aug = jnp.concatenate([g, dpack], axis=1)
    qt = jnp.transpose(q)
    gt = jnp.transpose(g)
    minus = jnp.full((), -1.0, bf16)
    row = lax.broadcasted_iota(jnp.int32, (nk, 128), 0)
    dq_parts, dkts, dvts = [], [], []
    for h in range(2):
        head = 2 * p + h
        sel = jnp.where((lane < 48) & ((lane & 15) == head), -1.0, 0.0)
        if not causal:
            sel = jnp.where((lane == 127) & (row >= len_ref[0]), BIG, sel)
        k_aug = jnp.concatenate([jnp.where(first, kk, k_s) if h == 0 else jnp.where(first, k_s, kk), sel.astype(bf16)], axis=1)
        dsel = jnp.where((lane >= 3 * h) & (lane < 3 * h + 3), -1.0, 0.0).astype(bf16)
        v_m = jnp.where(first, v, zero) if h == 0 else jnp.where(first, zero, v)
        v_aug = jnp.concatenate([v_m, dsel], axis=1)
        parts = []
        dkt = jnp.zeros((HD, nk), f32)
        dvt = jnp.zeros((HD, nk), f32)
        for c in range(n // qb):
            rows = slice(c * qb, (c + 1) * qb)
            top_k = (c + 1) * qb if causal else nk
            s = dot(q_aug[h][rows], k_aug[:top_k], NT)
            w = jnp.exp2(s)
            if causal:
                r = lax.broadcasted_iota(jnp.int32, (qb, qb), 0)
                dg = jnp.where(r >= lanes((qb, qb)), w[:, c * qb:], 0.0)
                w = jnp.concatenate([w[:, :c * qb], dg], axis=1) if c else dg
            dp = dot(g_aug[rows], v_aug[:top_k], NT)
            ds = (w * dp).astype(bf16)
            wb = w.astype(bf16)
            a = dot(gt[h * HD:(h + 1) * HD, rows], wb)
            b = dot(qt[h * HD:(h + 1) * HD, rows], ds)
            if top_k < nk:
                pad = jnp.zeros((HD, nk - top_k), f32)
                a = jnp.concatenate([a, pad], axis=1)
                b = jnp.concatenate([b, pad], axis=1)
            dvt = dvt + a
            dkt = dkt + b
            parts.append(dot(ds, kk[:top_k]))
        dq_parts.append(parts)
        dkts.append(dkt)
        dvts.append(dvt)
    sums = jnp.zeros((1, 128), f32)
    dqs = []
    for c in range(n // qb):
        rows = slice(c * qb, (c + 1) * qb)
        fl = lanes((qb, 128)) < HD
        dq = (jnp.where(fl, dq_parts[0][c], dq_parts[1][c]) * 0.125).astype(bf16)
        dqs.append(dq)
        sums = sums + jnp.sum(dq.astype(f32), axis=0, keepdims=True)
    dk = jnp.transpose(jnp.concatenate(dkts, axis=0)).astype(bf16)
    dv = jnp.transpose(jnp.concatenate(dvts, axis=0)).astype(bf16)
    v_sums = jnp.sum(dv.astype(f32), axis=0, keepdims=True)
    grads = (jnp.concatenate(dqs, axis=0), dk, dv)
    if not unit:
        sums_ref[...] = jnp.concatenate([sums, v_sums, jnp.zeros((6, 128), f32)], axis=0)
        for m, part in enumerate(grads):
            out_ref[m] = part
        return
    for at in range(2):
        @pl.when(pl.program_id(0) == at)
        def _(at=at):
            cols = slice(at * 128, (at + 1) * 128)
            sums_ref[:, cols] = jnp.concatenate([sums, v_sums, jnp.zeros((6, 128), f32)], axis=0)
            for m, part in enumerate(grads):
                out_ref[m, :, cols] = part

    @pl.when(pl.program_id(0) == 1)
    def _():
        joined = jnp.concatenate([out_ref[0], out_ref[1], out_ref[2]], axis=1)
        store_units(place, dot(tok_ref[...], joined, TN).astype(bf16), unit, send_ref, own_ref)
        if kind:
            rows = side_rows(kind, side, sums_ref[...])
            for ref in (send_ref, own_ref):
                for y in range(2):
                    for x in range(2):
                        for z in range(ref.shape[2]):
                            ref[y, x, z, unit:] = rows


def attn_bwd(length, q, k, v, o, g, lp, causal, first, stride, count, tokens=None, place=None, nb=0, kind="", side=(), qb=256):
    n, d = q.shape
    blk = pl.BlockSpec((n, 128), lambda p, l: (0, first + stride * p))
    ins = [blk] * 5 + [pl.BlockSpec((n, 128), lambda p, l: (0, 0))]
    outs = [pl.BlockSpec((3, n, 128), lambda p, l: (0, 0, p)), pl.BlockSpec((8, 128), lambda p, l: (0, p))]
    shapes = [pltpu.HBM((3, n, count * 128), bf16), pltpu.HBM((8, count * 128), f32)]
    args = hbm(q, k, v, o, g, lp)
    unit = 0
    if tokens is not None:
        unit = d // nb
        rows = unit + {"early": 32, "late": 16, "": 0}[kind]
        ins += [pl.BlockSpec(memory_space=pltpu.SMEM), pl.BlockSpec((n, d), lambda p, l: (0, 0))]
        ins += [pl.BlockSpec(s.shape, lambda p, l: (0, 0)) for s in side]
        args += [place] + hbm(tokens, *side)
        outs = [pl.BlockSpec((3, n, 256), lambda p, l: (0, 0, 0)), pl.BlockSpec((8, 256), lambda p, l: (0, 0))]
        outs += [pl.BlockSpec((2, 2, nb // 4, rows, 384), lambda p, l: (0, 0, 0, 0, 0))] * 2
        shapes += [pltpu.HBM((2, 2, nb // 4, rows, 384), bf16)] * 2
    return pl.pallas_call(
        functools.partial(bwd_kernel, causal=causal, qb=qb, first_pair=first, stride=stride, unit=unit, kind=kind),
        grid_spec=pltpu.PrefetchScalarGridSpec(
            num_scalar_prefetch=1, grid=(count,), in_specs=ins, out_specs=outs),
        out_shape=shapes,
        compiler_params=params(40),
        cost_estimate=cost((n + 256) * n * 2560 // (2 if causal else 1) * count * 2, 16 * n * count * 128, 2 * n * n * count),
        name="attn_bwd",
    )(length, *args)


def cost(flops, moved, exps=0):
    return pl.CostEstimate(flops=int(flops), bytes_accessed=int(moved), transcendentals=int(exps))


def params(mib):
    return pltpu.CompilerParams(vmem_limit_bytes=mib * 2**20)


def hbm(*values):
    return [pltpu.with_memory_space_constraint(v, pltpu.HBM) for v in values]


def whole():
    return pl.BlockSpec(memory_space=pltpu.VMEM)


def fixed(shape):
    return pl.BlockSpec(shape, lambda *_: (0,) * len(shape), pipeline_mode=pl.Buffered(1))


def spread_rows(block):
    return lambda i, *_: (i, 0)


def project_kernel(place, mine, got, weight, biases, *outs, step, plan):
    i = pl.program_id(0)
    x = jnp.where(i // step == place[0], mine[...], got[...])
    outs[0][...] = x
    joined = dot(x, weight[...])
    width = x.shape[1]
    for n, (bias, scale) in enumerate(plan):
        part = joined[:, n * width : (n + 1) * width]
        if bias is not None:
            part = part + biases[bias : bias + 1, :]
        if scale != 1.0:
            part = part * scale
        outs[n + 1][...] = part.astype(bf16)


def project(place, pairs, got, weight, biases, plan, rows=256):
    half, width = got.shape
    step = half // rows
    cols = weight.shape[1]
    block = pl.BlockSpec((rows, width), lambda i, p: (i, 0))
    return pl.pallas_call(
        functools.partial(project_kernel, step=step, plan=plan),
        grid_spec=pltpu.PrefetchScalarGridSpec(
            num_scalar_prefetch=1,
            grid=(2 * step,),
            in_specs=[
                pl.BlockSpec((rows, width), lambda i, p: (i % step, p[0])),
                pl.BlockSpec((rows, width), lambda i, p: (i % step, 0)),
                whole(),
                whole(),
            ],
            out_specs=[block] * (1 + len(plan)),
        ),
        out_shape=[pltpu.HBM((2 * half, width), bf16)] * (1 + len(plan)),
        compiler_params=params(32),
        cost_estimate=cost(4 * half * width * cols, 2 * width * cols + 12 * half * width),
        name="project",
    )(place, *hbm(pairs, got), weight, biases)


def norm_unit(value):
    mean = jnp.mean(value, axis=-1, keepdims=True)
    centred = value - mean
    scale = lax.rsqrt(jnp.mean(centred * centred, axis=-1, keepdims=True) + 1e-05)
    return centred * scale, scale


def norm_back(grad, unit, scale, gain):
    weighted = grad * gain
    return scale * (
        weighted
        - jnp.mean(weighted, axis=-1, keepdims=True)
        - unit * jnp.mean(weighted * unit, axis=-1, keepdims=True)
    )


def row_sum(value):
    return jnp.sum(value, axis=0, keepdims=True)


def after_self_kernel(o, tok, w_out, w_q, biases, gain, shift, unit_ref, scale_ref, low_ref, q_ref):
    resid = tok[...].astype(f32) + dot(o[...], w_out[...]) + biases[2:3, :]
    unit, scale = norm_unit(resid)
    unit_ref[...] = unit
    scale_ref[...] = jnp.broadcast_to(scale, scale_ref.shape)
    low_ = (unit * gain[0:1, :] + shift[0:1, :]).astype(bf16)
    low_ref[...] = low_
    q_ref[...] = ((dot(low_, w_q[...]) + biases[3:4, :]) * 0.125).astype(bf16)


def after_self(o, tok, w_out, w_q, biases, gain, shift, rows=256):
    n, d = o.shape
    block = pl.BlockSpec((rows, d), lambda i: (i, 0))
    return pl.pallas_call(
        after_self_kernel,
        grid=(n // rows,),
        in_specs=[block, block, whole(), whole()] + [whole()] * 3,
        out_specs=[block, pl.BlockSpec((rows, 128), lambda i: (i, 0)), block, block],
        out_shape=[
            pltpu.HBM((n, d), f32),
            pltpu.HBM((n, 128), f32),
            pltpu.HBM((n, d), bf16),
            pltpu.HBM((n, d), bf16),
        ],
        compiler_params=params(32),
        cost_estimate=cost(4 * n * d * d, 4 * d * d + 12 * n * d),
        name="after_self",
    )(*hbm(o, tok), w_out, w_q, biases, gain, shift)


RATE = 0.3275911 * 0.7071067811865476
TAIL = tuple(0.5 * c for c in (0.254829592, -0.284496736, 1.421413741, -1.453152027, 1.061405429))
DENSITY = 0.3989422804014327


def gelu_pair(v):
    size = jnp.abs(v)
    base = 1.0 + RATE * size
    t = pl.reciprocal(base, approx=True)
    t = t * (2.0 - base * t)
    poly = TAIL[4]
    for c in TAIL[3::-1]:
        poly = c + t * poly
    bell = jnp.exp2((v * v) * (-0.5 * LOG2E))
    tail = t * poly * bell
    below = jnp.where(v >= 0.0, 1.0 - tail, tail)
    return v * below, below + v * (DENSITY * bell)


def ffn_kernel(
    o, unit_one, cot, w_co, w_in, w_out, biases, ffn_bias, gain, shift,
    layer_ref, act_ref, pre_ref, low_ref, b3_ref, g2_ref, b2_ref, gm_ref, sums_ref, fsum_ref,
    slope, *, chunk,
):
    i = pl.program_id(0)
    ff = w_in.shape[1]
    n_chunks = ff // chunk

    @pl.when(i == 0)
    def _():
        sums_ref[...] = jnp.zeros_like(sums_ref)
        fsum_ref[...] = jnp.zeros_like(fsum_ref)

    normed_one = unit_one[...] * gain[0:1, :] + shift[0:1, :]
    resid = normed_one + dot(o[...], w_co[...]) + biases[5:6, :]
    unit_two, scale_two = norm_unit(resid)
    normed_two = unit_two * gain[1:2, :] + shift[1:2, :]
    low_two = normed_two.astype(bf16)
    low_ref[...] = low_two

    def inner(j):
        at = slice(j * chunk, (j + 1) * chunk)
        return dot(low_two, w_in[:, at]) + ffn_bias[0:1, at]

    total = normed_two + biases[6:7, :]
    ahead = inner(0)
    for j in range(n_chunks):
        v = ahead
        if j + 1 < n_chunks:
            ahead = inner(j + 1)
        at = slice(j * chunk, (j + 1) * chunk)
        act, grad = gelu_pair(v)
        act = act.astype(bf16)
        act_ref[:, at] = act
        slope[:, at] = grad
        total = total + dot(act, w_out[at, :])
    unit, scale = norm_unit(total)
    layer_ref[...] = (unit * gain[2:3, :] + shift[2:3, :]).astype(bf16)
    g = cot[...].astype(f32)
    grad_three = norm_back(g, unit, scale, gain[2:3, :])
    branch = grad_three.astype(bf16)
    b3_ref[...] = branch
    sums_ref[0:1, :] += row_sum(g * unit)
    sums_ref[1:2, :] += row_sum(g)
    sums_ref[2:3, :] += row_sum(grad_three)

    def back(j):
        return dot(branch, w_out[j * chunk : (j + 1) * chunk, :], NT)

    total = grad_three
    ahead = back(0)
    for j in range(n_chunks):
        v = ahead
        if j + 1 < n_chunks:
            ahead = back(j + 1)
        at = slice(j * chunk, (j + 1) * chunk)
        pre = (v * slope[:, at]).astype(bf16)
        pre_ref[:, at] = pre
        fsum_ref[0:1, at] += row_sum(pre.astype(f32))
        total = total + dot(pre, w_in[:, at], NT)
    grad_two = norm_back(total, unit_two, scale_two, gain[1:2, :])
    g2_ref[...] = grad_two
    branch = grad_two.astype(bf16)
    b2_ref[...] = branch
    sums_ref[3:4, :] += row_sum(total * unit_two)
    sums_ref[4:5, :] += row_sum(total)
    sums_ref[5:6, :] += row_sum(grad_two)
    gm_ref[...] = dot(branch, w_co[...], NT).astype(bf16)


def ffn(o, unit_one, cot, w_co, w_in, w_out, biases, ffn_bias, gain, shift, rows=256, chunk=512):
    n, d = o.shape
    ff = w_in.shape[1]
    block = pl.BlockSpec((rows, d), lambda i: (i, 0))
    wide = pl.BlockSpec((rows, ff), lambda i: (i, 0))
    low_shape = pltpu.HBM((n, d), bf16)
    return pl.pallas_call(
        functools.partial(ffn_kernel, chunk=chunk),
        grid=(n // rows,),
        in_specs=[block, block, block, whole(), whole(), whole()] + [whole()] * 4,
        out_specs=[block, wide, wide, block, block, block, block, block,
                   pl.BlockSpec((8, d), lambda i: (0, 0)), pl.BlockSpec((8, ff), lambda i: (0, 0))],
        out_shape=[
            low_shape,
            pltpu.HBM((n, ff), bf16),
            pltpu.HBM((n, ff), bf16),
            low_shape,
            low_shape,
            pltpu.HBM((n, d), f32),
            low_shape,
            low_shape,
            pltpu.HBM((8, d), f32),
            pltpu.HBM((8, ff), f32),
        ],
        scratch_shapes=[pltpu.VMEM((rows, ff), f32)],
        compiler_params=params(48),
        cost_estimate=cost(8 * n * d * ff + 4 * n * d * d, 4 * d * ff + 4 * n * ff + 20 * n * d, 2 * n * ff),
        name="ffn",
    )(*hbm(o, unit_one, cot), w_co, w_in, w_out, biases, ffn_bias, gain, shift)


def before_self_kernel(g2, gqa, gqb, unit_ref, scale_ref, w_q, w_out, gain, g1_ref, b1_ref, gm_ref, gq_ref, sums_ref):
    @pl.when(pl.program_id(0) == 0)
    def _():
        sums_ref[...] = jnp.zeros_like(sums_ref)

    gq = jnp.concatenate([gqa[0], gqb[0]], axis=1)
    gq_ref[...] = gq
    g = g2[...] + dot(gq, w_q[...], NT)
    unit = unit_ref[...]
    grad = norm_back(g, unit, scale_ref[:, 0:1], gain[0:1, :])
    g1_ref[...] = grad
    branch = grad.astype(bf16)
    b1_ref[...] = branch
    sums_ref[0:1, :] += row_sum(g * unit)
    sums_ref[1:2, :] += row_sum(g)
    sums_ref[2:3, :] += row_sum(grad)
    gm_ref[...] = dot(branch, w_out[...], NT).astype(bf16)


def before_self(g2, gqa, gqb, unit, scale, w_q, w_out, gain, rows=256):
    n, d = g2.shape
    block = pl.BlockSpec((rows, d), lambda i: (i, 0))
    return pl.pallas_call(
        before_self_kernel,
        grid=(n // rows,),
        in_specs=[block, pl.BlockSpec((1, rows, d // 2), lambda i: (0, i, 0)), pl.BlockSpec((1, rows, d // 2), lambda i: (0, i, 0)), block, pl.BlockSpec((rows, 128), lambda i: (i, 0)), whole(), whole(), whole()],
        out_specs=[block, block, block, block, pl.BlockSpec((8, d), lambda i: (0, 0))],
        out_shape=[
            pltpu.HBM((n, d), f32),
            pltpu.HBM((n, d), bf16),
            pltpu.HBM((n, d), bf16),
            pltpu.HBM((n, d), bf16),
            pltpu.HBM((8, d), f32),
        ],
        compiler_params=params(32),
        cost_estimate=cost(4 * n * d * d, 4 * d * d + 18 * n * d),
        name="before_self",
    )(*hbm(g2, gqa, gqb, unit, scale), w_q, w_out, gain)


TN = (((0,), (0,)), ((), ()))


def store_units(place, value, unit, send_ref, own_ref, first=0, z_local=False):
    mx, mz, my, core = place[0], place[1], place[2], place[3]
    half = value.shape[1] // 2
    for mine in range(2):
        @pl.when(core == mine)
        def _():
            for u in range(value.shape[0] // unit):
                ref = own_ref if u % 2 == mine else send_ref
                z = 0 if z_local else jnp.bitwise_xor(u // 4, mz)
                y = jnp.bitwise_xor((u // 2) % 2, my)
                for x in range(2):
                    ref[y, jnp.bitwise_xor(x, mx), z, :unit] = value[u * unit : (u + 1) * unit, x * half : (x + 1) * half]


def store_in_order(value, unit, ref, pieces=1):
    half = value.shape[1] // 2
    part = unit // pieces
    for u in range(value.shape[0] // unit):
        for x in range(2):
            for c in range(pieces):
                top = u * unit + c * part
                ref[x, u, :, c * half : (c + 1) * half] = value[top : top + part, x * half : (x + 1) * half]


def tall_kernel(a, b, out_ref, *, unit, pieces):
    store_in_order(dot(a[...], b[...], TN).astype(bf16), unit, out_ref, pieces)


def tall_grad(a, b, nb, width, steps=4):
    n, rows = a.shape
    cols = b.shape[1]
    pieces = rows // cols
    unit = rows // nb
    return pl.pallas_call(
        functools.partial(tall_kernel, unit=unit, pieces=pieces),
        grid=(steps,),
        in_specs=[pl.BlockSpec((n, rows // steps), lambda s: (0, s)), pl.BlockSpec((n, cols), lambda s: (0, 0))],
        out_specs=pl.BlockSpec((2, nb // steps, unit // pieces, pieces * cols // 2), lambda s: (0, s, 0, 0)),
        out_shape=pltpu.HBM((2, nb, unit // pieces, width), bf16),
        compiler_params=params(32),
        cost_estimate=cost(2 * n * rows * cols, 2 * (n * rows + n * cols + rows * cols)),
        name="tall_grad",
    )(*hbm(a, b))


def wide_kernel(place, *refs, steps, unit, into):
    send_ref, own_ref = refs[-2:]
    j = pl.program_id(0)
    for a_at, left, right, first, count in steps:
        @pl.when((j >= first) & (j < first + count))
        def _(a_at=a_at, left=left, right=right):
            flat = lambda r: refs[r][...].reshape(refs[r].shape[-2:])
            value = dot(refs[a_at][...], jnp.concatenate([flat(left), flat(right)], axis=1), TN).astype(bf16)
            if into:
                store_in_order(value, unit, own_ref)
            else:
                store_units(place, value, unit, send_ref, own_ref)


def wide_grad(place, terms, nb, block=384, into=None):
    n, rows = terms[0][0].shape
    unit = rows // nb
    arrays, specs, steps, first = [], [], [], 0
    whole_a = pl.BlockSpec((n, rows), lambda j, p: (0, 0))
    for a, b, leads in terms:
        if not any(a is other for other in arrays):
            arrays.append(a)
            specs.append(whole_a)
        a_at = next(i for i, other in enumerate(arrays) if other is a)
        count = b.shape[-1] // block // (1 if leads else 2)
        for side in range(2):
            def where(j, p, first=first, count=count, side=side, leads=leads):
                inside = jnp.clip(j - first, 0, count - 1)
                return (leads[side], 0, inside) if leads else (0, side * count + inside)
            arrays.append(b)
            specs.append(pl.BlockSpec((1, n, block) if leads else (n, block), where))
        steps.append((a_at, len(arrays) - 2, len(arrays) - 1, first, count))
        first += count
    steps = [(a, l, r, f, c) for a, l, r, f, c in steps]
    if into is None:
        out = [pltpu.HBM((2, 2, nb // 4, unit, first * block), bf16)] * 2
        out_specs = [pl.BlockSpec((2, 2, nb // 4, unit, block), lambda j, p: (0, 0, 0, 0, j))] * 2
        aliases = {}
    else:
        start = into.shape[-1] // block - first
        out = [pltpu.HBM(into.shape, bf16)]
        out_specs = [pl.BlockSpec((2, nb, unit, block), lambda j, p: (0, 0, 0, start + j))]
        aliases = {1 + len(arrays): 0}
        arrays.append(into)
        specs.append(pl.BlockSpec(memory_space=pl.ANY))
    return pl.pallas_call(
        functools.partial(wide_kernel, steps=steps, unit=unit, into=into is not None),
        grid_spec=pltpu.PrefetchScalarGridSpec(num_scalar_prefetch=1, grid=(first,), in_specs=specs, out_specs=out_specs),
        out_shape=out,
        input_output_aliases=aliases,
        compiler_params=params(40),
        cost_estimate=cost(4 * n * rows * first * block, 4 * rows * first * block + 4 * n * first * block),
        name="wide_grad",
    )(place, *hbm(*arrays))


def grad_rows_kernel(place, *refs, columns, based):
    gs, weight = refs[: len(columns)], refs[len(columns)]
    out_ref = refs[-1]
    value = None
    for g, chunks in zip(gs, columns):
        for m, starts in enumerate(chunks):
            if not starts:
                continue
            w = [weight[:, s : s + size] for s, size in starts]
            w = w[0] if len(w) == 1 else jnp.concatenate(w, axis=1)
            term = dot(g[m], w, NT)
            value = term if value is None else value + term
    if based:
        value = value + refs[len(columns) + 1][...]

    out_ref[...] = value.astype(out_ref.dtype)


def grad_rows(place, terms, columns, weight, base, mine, rows=256):
    n = terms[0].shape[1]
    d, k = weight.shape
    steps = n // 2 // rows
    half = lambda i, p: (p[0] if mine else 1 - p[0]) * steps + i
    ins = [pl.BlockSpec((t.shape[0], rows, t.shape[2]), lambda i, p: (0, half(i, p), 0)) for t in terms] + [whole()]
    args = hbm(*terms) + [weight]
    if base is not None:
        ins.append(pl.BlockSpec((rows, d), lambda i, p: (half(i, p), 0)))
        args += hbm(base)
    return pl.pallas_call(
        functools.partial(grad_rows_kernel, columns=columns, based=base is not None),
        grid_spec=pltpu.PrefetchScalarGridSpec(
            num_scalar_prefetch=1,
            grid=(steps,),
            in_specs=ins,
            out_specs=pl.BlockSpec((rows, d), lambda i, p: (i, 0)),
        ),
        out_shape=pltpu.HBM((n // 2, d), f32 if mine else bf16),
        compiler_params=params(40),
        cost_estimate=cost(n * k * d, n * k + 2 * k * d + 4 * n * d),
        name="grad_rows",
    )(place, *args)


def route(nb, move):
    dz, dy, dc, dx = move
    pairs = []
    for b in range(nb):
        z, y, core = b // 4, (b // 2) % 2, b % 2
        for x in range(2):
            target = (z ^ dz) * 4 + (y ^ dy) * 2 + (core ^ dc)
            pairs.append((b * 2 + x, target * 2 + (x ^ dx)))
    return pairs


def send(value, nb, move):
    return lax.ppermute(value, ("batch", "seq"), route(nb, move))


def core_stage(buffers, nb):
    to_send, own = buffers
    return own, send(to_send, nb, (0, 0, 1, 0))


def y_prepare(state):
    own, got = state
    return (own[1].astype(f32) + got[1].astype(f32)).astype(bf16), (own, got)


def y_move(value, nb):
    return send(value, nb, (0, 1, 0, 0))


def x_prepare(state):
    own, got, more = state
    total = own[0].astype(f32) + got[0].astype(f32) + more.astype(f32)
    return total[0].astype(bf16), total[1].astype(bf16)


def x_move(value, nb):
    return send(value, nb, (0, 0, 0, 1))


def z_prepare(state):
    kept, got = state
    total = kept.astype(f32) + got.astype(f32)
    return total[0::2].astype(bf16), total[1::2].astype(bf16)


def z_move(value, nb, bit):
    return send(value, nb, (1 << bit, 0, 0, 0))


def after_y(state):
    own, got, more = state
    return (own[0].astype(f32) + got[0].astype(f32) + more.astype(f32)).astype(bf16)


def direct_z(total, nb):
    result = total[:, 0].astype(f32)
    for d in range(1, nb // 4):
        result = result + send(total[:, d], nb, (d, 0, 0, 0)).astype(f32)
    return result


def at(value, index, axis):
    return lax.dynamic_index_in_dim(value, index, axis, keepdims=False)


def last_stage(state):
    kept, got = state
    return (kept.astype(f32) + got.astype(f32))[0]


def tie(*values):
    return lax.optimization_barrier(values)


def swap(value):
    return lax.ppermute(value, "seq", [(0, 1), (1, 0)])


def split_pairs(local):
    positions, _, width = local.shape
    pairs = local.reshape(positions, 2 * width)
    x = lax.axis_index("seq")
    return pairs, lax.dynamic_slice(pairs, (0, (1 - x) * width), (positions, width))


def join_pairs(mine, got):
    x = lax.axis_index("seq")
    got = got.astype(mine.dtype)
    both = jnp.concatenate([jnp.where(x == 0, mine, got), jnp.where(x == 0, got, mine)], axis=1)
    return both.reshape(mine.shape[0], 2, mine.shape[1])


def whole_sequence(pairs, got):
    x = lax.axis_index("seq")
    width = got.shape[1]
    mine = lax.dynamic_slice(pairs, (0, x * width), got.shape)
    return jnp.where(x == 0, jnp.concatenate([mine, got]), jnp.concatenate([got, mine]))


def per_device_fast(
    hidden_in,
    memory,
    src_len,
    out_grad,
    w_self_qkv,
    w_self_out,
    w_cross_q,
    w_cross_kv,
    w_cross_out,
    w_ffn_in,
    w_ffn_out,
    biases,
    ffn_bias,
    norm_gain,
    norm_shift,
):
    nb = lax.axis_size("batch")
    width = hidden_in.shape[2]
    half = width // 2
    x, b = lax.axis_index("seq"), lax.axis_index("batch")
    place = jnp.stack([x, b // 4, (b // 2) % 2, b % 2]).astype(jnp.int32)
    length = lax.dynamic_slice_in_dim(src_len, x, 1)

    pairs, other = split_pairs(hidden_in)
    got = swap(other)
    memory_pairs, memory_other = split_pairs(memory)
    memory_got = swap(memory_other)
    cot_pairs, cot_other = split_pairs(out_grad)
    tokens, query_self, key_self, value_self = project(
        place, pairs, got, w_self_qkv, biases, ((0, 0.125), (None, 1.0), (1, 1.0))
    )
    query_self, cot_other = tie(query_self, cot_other)
    cot_got = swap(cot_other)
    out_self, lp_self = attn_fwd(length, query_self, key_self, value_self, True)
    unit_one, scale_one, low_one, query_cross = after_self(
        out_self, tokens, w_self_out, w_cross_q, biases, norm_gain, norm_shift
    )
    sources, key_cross, value_cross = project(
        place, memory_pairs, memory_got, w_cross_kv, biases, ((None, 1.0), (4, 1.0))
    )
    out_cross, lp_cross = attn_fwd(length, query_cross, key_cross, value_cross, False)
    cotangent = whole_sequence(cot_pairs, cot_got)
    layer, active, grad_pre, low_two, branch_three, grad_two, branch_two, grad_mixed, sums_ffn, bias_sums = ffn(
        out_cross, unit_one, cotangent, w_cross_out, w_ffn_in, w_ffn_out, biases, ffn_bias[None], norm_gain, norm_shift
    )
    span = layer.shape[0] // 2

    ff = active.shape[1]
    one = tall_grad(active, branch_three, nb, 2 * (ff // 2) + half)
    one, low_two = tie(one, low_two)
    (one,) = wide_grad(place, [(low_two, grad_pre, None), (out_cross, branch_two, None)], nb, into=one)

    one, grad_mixed = tie(one, grad_mixed)
    one = lax.psum_scatter(one.reshape(-1, one.shape[-1]), ("seq", "batch"), scatter_dimension=0, tiled=True)
    back = partial(attn_bwd, length, query_cross, key_cross, value_cross, out_cross)
    cross_a, sums_ca = back(grad_mixed, lp_cross, False, 0, 1, 3)

    cross_a, grad_mixed = tie(cross_a, grad_mixed)
    layer_other = lax.dynamic_slice_in_dim(layer, (1 - x) * span, span, 0)
    layer_other, grad_mixed = tie(layer_other, grad_mixed)
    layer_got = swap(layer_other)
    cross_b, sums_cb = back(grad_mixed, lp_cross, False, 3, 1, 3)

    cross_b, layer_got = tie(cross_b, layer_got)
    grad_one, branch_one, grad_mixed, gq_cross, sums_one = before_self(
        grad_two, cross_a, cross_b, unit_one, scale_one, w_cross_q, w_self_out, norm_gain
    )
    three = wide_grad(
        place,
        [(out_self, branch_one, None), (low_one, gq_cross, None), (sources, cross_a, (1, 2)), (sources, cross_b, (1, 2))],
        nb,
    )

    three, cross_a = tie(three, cross_a)
    three = core_stage(three, nb)
    spots = [((), ((0, 384),), ((width, 384),)), ((), ((384, 384),), ((width + 384, 384),))]
    other = grad_rows(place, [cross_a, cross_b], spots, w_cross_kv, None, False)

    other, three, grad_mixed = tie(other, three, grad_mixed)
    three_out, three = y_prepare(three)
    three_out, grad_mixed = tie(three_out, grad_mixed)
    three = three + (y_move(three_out, nb),)
    memory_back = swap(other)
    back = partial(attn_bwd, length, query_self, key_self, value_self, out_self)
    self_a, sums_sa, *four = back(
        grad_mixed, lp_self, True, 0, 3, 2, tokens, place, nb, "early", (sums_one, sums_ca, sums_cb, sums_ffn, bias_sums)
    )

    self_a, four, cross_a, memory_back = tie(self_a, four, cross_a, memory_back)
    four = core_stage(four, nb)
    memory_mine = grad_rows(place, [cross_a, cross_b], spots, w_cross_kv, None, True)

    four, three, grad_mixed, memory_mine = tie(four, three, grad_mixed, memory_mine)
    four_out, four = y_prepare(four)
    three_keep, three_out = x_prepare(three)
    four_out, three_out, grad_mixed = tie(four_out, three_out, grad_mixed)
    four = four + (y_move(four_out, nb),)
    three = three_keep, x_move(three_out, nb)
    self_b, sums_sb, *five = back(grad_mixed, lp_self, True, 1, 3, 2, tokens, place, nb)

    self_b, five, four, three, grad_mixed = tie(self_b, five, four, three, grad_mixed)
    five = core_stage(five, nb)
    four_keep, four_out = x_prepare(four)
    three_keep, three_out = z_prepare(three)
    four_out, three_out, grad_mixed = tie(four_out, three_out, grad_mixed)
    four = four_keep, x_move(four_out, nb)
    three = three_keep, z_move(three_out, nb, 0)
    self_c, sums_sc, *six = back(grad_mixed, lp_self, True, 2, 3, 2, tokens, place, nb, "late", (sums_sa, sums_sb))

    self_c, six, five, four, three = tie(self_c, six, five, four, three)
    six = core_stage(six, nb)
    five_out, five = y_prepare(five)
    four_keep, four_out = z_prepare(four)
    three_keep, three_out = z_prepare(three)
    five_out, four_out, three_out, self_c = tie(five_out, four_out, three_out, self_c)
    five = five + (y_move(five_out, nb),)
    four = four_keep, z_move(four_out, nb, 0)
    three = three_keep, z_move(three_out, nb, 1)
    spots = [tuple(tuple((m * width + (i + s) * 128, 128) for s in (0, 3)) for m in range(3)) for i in range(3)]
    other = grad_rows(place, [self_a, self_b, self_c], spots, w_self_qkv, grad_one, False)

    other, six, grad_one = tie(other, six, grad_one)
    six_out, six = y_prepare(six)
    six_out, other, grad_one = tie(six_out, other, grad_one)
    six = six + (y_move(six_out, nb),)
    in_back = swap(other)
    mine = grad_rows(place, [self_a, self_b, self_c], spots, w_self_qkv, grad_one, True)

    mine, six, five, four, three, layer_got, memory_back = tie(mine, six, five, four, three, layer_got, memory_back)
    both = direct_z(jnp.concatenate([after_y(six), after_y(five)], axis=2), nb)
    four_keep, four_out = z_prepare(four)
    four = four_keep, z_move(four_out, nb, 1)
    layer_out = join_pairs(lax.dynamic_slice_in_dim(layer, x * span, span, 0), layer_got)
    grad_memory = join_pairs(memory_mine, memory_back)
    both = both[0] + x_move(both[1].astype(bf16), nb).astype(f32)
    four = last_stage(four)
    grad_in = join_pairs(mine, in_back)
    group = last_stage(three)
    one = one.astype(f32)
    pieces = ff // width
    grad_ffn_out = jnp.concatenate([one[:, c * half : (c + 1) * half] for c in range(pieces)], axis=0)
    grad_ffn_in = one[:, pieces * half :]
    unit = width // nb
    ends = unit, both.shape[0] - unit
    thirds = [s.reshape(unit, 3, 128) for s in (four[:unit], both[ends[1] :], both[: ends[0]])]
    grad_self_qkv = jnp.stack(thirds, axis=2).reshape(unit, 9 * 128)
    late = both[ends[0] : ends[0] + 6, :256].reshape(3, 2, 2, 128)
    late = at(late, x, 2).swapaxes(0, 1).reshape(2, half)
    early = lax.dynamic_slice_in_dim(four[unit:], x * 16, 16, 0)
    vectors = jnp.concatenate([late, early[:11]])
    bias_total = early[11 : 11 + bias_sums.shape[1] // width].reshape(-1)
    return (
        layer_out,
        grad_in,
        grad_memory,
        grad_self_qkv,
        group[:, :half],
        group[:, half : 2 * half],
        group[:, 2 * half :],
        grad_ffn_in[:, -half:],
        grad_ffn_in[:, :-half],
        grad_ffn_out,
        vectors[0:7],
        bias_total,
        vectors[7:10],
        vectors[10:13],
    )


def solution(mesh):
    devices = dict(mesh.shape)

    in_specs = (
        P("seq", "batch", None),
        P("seq", "batch", None),
        P("batch"),
        P("seq", "batch", None),
        P(),
        P(),
        P(),
        P(),
        P(),
        P(),
        P(),
        P(),
        P(),
        P(),
        P(),
    )
    out_specs = (
        P("seq", "batch", None),
        P("seq", "batch", None),
        P("seq", "batch", None),
        P("batch", "seq"),
        P("batch", "seq"),
        P("batch", "seq"),
        P("batch", "seq"),
        P("batch", "seq"),
        P("batch", "seq"),
        P("batch", "seq"),
        P(None, "seq"),
        P("seq"),
        P(None, "seq"),
        P(None, "seq"),
    )
    nb, ns = devices["batch"], devices["seq"]

    def per_device(hidden_in, *rest):
        whole = ns == 2 and hidden_in.shape[1] == 2 and nb % 4 == 0 and nb & (nb - 1) == 0
        return (per_device_fast if whole else per_device_general)(hidden_in, *rest)

    return jax.shard_map(
        per_device, mesh=mesh, in_specs=in_specs, out_specs=out_specs, check_vma=False
    )
```

```python
import functools
from functools import partial

import jax
import jax.numpy as jnp
from jax import lax
from jax.experimental import pallas as pl
from jax.experimental.pallas import tpu as pltpu
from jax.sharding import PartitionSpec as P

H = 12


NEGATIVE = -1e30


def from_behind(value, axis, steps):
    count = lax.axis_size(axis)
    pairs = [(source, (source + steps) % count) for source in range(count)]
    return lax.ppermute(value, axis, pairs)


def shifted(block, axis, distance):
    devices = range(lax.axis_size(axis))
    route = [(i - distance, i) for i in devices if i - distance in devices]
    return lax.ppermute(block, axis, route)


def contract_rows(left, right):
    return lax.dot_general(
        left, right, (((0,), (0,)), ((), ())), preferred_element_type=jnp.float32
    )


def times_transposed(grad, weight):
    return lax.dot_general(
        grad, weight, (((1,), (1,)), ((), ())), preferred_element_type=jnp.float32
    )


def norm_forward(value, gain, shift):
    mean = jnp.mean(value, axis=-1, keepdims=True)
    centred = value - mean
    scale = lax.rsqrt(jnp.mean(centred * centred, axis=-1, keepdims=True) + 1e-05)
    unit = centred * scale
    return (unit * gain + shift, unit, scale)


def norm_backward(grad, unit, scale, gain):
    weighted = grad * gain
    inner = (
        weighted
        - jnp.mean(weighted, axis=-1, keepdims=True)
        - unit * jnp.mean(weighted * unit, axis=-1, keepdims=True)
    )
    return (scale * inner, jnp.sum(grad * unit, axis=0), jnp.sum(grad, axis=0))


def allowed_keys(query_pos, key_pos, lengths, causal):
    if causal:
        return (query_pos[:, None] >= key_pos[None, :])[None, None]
    return (key_pos[None, :] < lengths[:, None])[:, None, None, :]


def attend_forward(query, keys, values, lengths, causal, heads):
    span, batch, width = query.shape
    size = width // heads
    query_heads = query.reshape(span, batch, heads, size)
    query_pos = lax.axis_index("seq") * span + lax.iota(jnp.int32, span)

    def block(carry, key_block, value_block, first):
        previous, total, summed = carry
        rows = key_block.shape[0]
        key_pos = first + lax.iota(jnp.int32, rows)
        scores = jnp.einsum(
            "qshd,kshd->shqk",
            query_heads,
            key_block.reshape(rows, batch, heads, size),
            preferred_element_type=jnp.float32,
        )
        allowed = allowed_keys(query_pos, key_pos, lengths, causal)
        top = jnp.maximum(previous, jnp.max(jnp.where(allowed, scores, NEGATIVE), axis=-1))
        weights = jnp.where(allowed, jnp.exp(scores - top[..., None]), 0.0)
        rescale = jnp.exp(previous - top)
        total = total * rescale + jnp.sum(weights, axis=-1)
        summed = summed * rescale[..., None] + jnp.einsum(
            "shqk,kshd->shqd",
            weights.astype(jnp.bfloat16),
            value_block.reshape(rows, batch, heads, size),
            preferred_element_type=jnp.float32,
        )
        return (top, total, summed)

    def fold(carry, piece):
        key_piece, value_piece = piece
        rows = key_piece.shape[0]
        count = rows // span
        firsts = span * lax.iota(jnp.int32, count)

        def inner(state, parts):
            return (block(state, parts[0], parts[1], parts[2]), None)

        carry, unused = lax.scan(
            inner,
            carry,
            (
                key_piece.reshape(count, span, batch, width),
                value_piece.reshape(count, span, batch, width),
                firsts,
            ),
        )
        return carry

    empty = (
        jnp.full((batch, heads, span), NEGATIVE, jnp.float32),
        jnp.zeros((batch, heads, span), jnp.float32),
        jnp.zeros((batch, heads, span, size), jnp.float32),
    )
    if causal:
        top, total, summed = fold(
            empty,
            (
                lax.all_gather(keys, "seq", axis=0, tiled=True),
                lax.all_gather(values, "seq", axis=0, tiled=True),
            ),
        )
    else:
        top, total, summed = fold(
            empty,
            (
                lax.all_gather(keys, "seq", axis=0, tiled=True),
                lax.all_gather(values, "seq", axis=0, tiled=True),
            ),
        )
    mixed = summed / total[..., None]
    mixed = jnp.transpose(mixed, (2, 0, 1, 3)).reshape(span, batch, width)
    return (mixed, top + jnp.log(total))


def block_backward(
    query_heads, grad_heads, delta, logsum, key_block, value_block, allowed, batch, heads, size
):
    span = key_block.shape[0]
    width = heads * size
    key_heads = key_block.reshape(span, batch, heads, size)
    value_heads = value_block.reshape(span, batch, heads, size)
    scores = jnp.einsum(
        "qshd,kshd->shqk", query_heads, key_heads, preferred_element_type=jnp.float32
    )
    weights = jnp.where(allowed, jnp.exp(scores - logsum[..., None]), 0.0)
    grad_weights = jnp.einsum(
        "qshd,kshd->shqk", grad_heads, value_heads, preferred_element_type=jnp.float32
    )
    grad_scores = (weights * (grad_weights - delta[..., None])).astype(jnp.bfloat16)
    grad_query = jnp.einsum(
        "shqk,kshd->qshd", grad_scores, key_heads, preferred_element_type=jnp.float32
    )
    grad_keys = jnp.einsum(
        "shqk,qshd->kshd", grad_scores, query_heads, preferred_element_type=jnp.float32
    ).reshape(span, batch, width)
    grad_values = jnp.einsum(
        "shqk,qshd->kshd",
        weights.astype(jnp.bfloat16),
        grad_heads,
        preferred_element_type=jnp.float32,
    ).reshape(span, batch, width)
    return (grad_query, grad_keys, grad_values)


def attend_backward(query, keys, values, mixed, grad_mixed, logsum, lengths, causal, heads):
    span, batch, width = query.shape
    size = width // heads
    query_heads = query.reshape(span, batch, heads, size)
    grad_heads = grad_mixed.reshape(span, batch, heads, size)
    delta = jnp.sum(
        grad_heads.astype(jnp.float32) * mixed.reshape(span, batch, heads, size), axis=-1
    )
    delta = jnp.transpose(delta, (1, 2, 0))
    devices = lax.axis_size("seq")
    place = lax.axis_index("seq")
    query_pos = place * span + lax.iota(jnp.int32, span)
    grad_query = jnp.zeros((span, batch, heads, size), jnp.float32)
    grad_keys = jnp.zeros((span, batch, width), jnp.float32)
    grad_values = jnp.zeros((span, batch, width), jnp.float32)
    key_block, value_block = (keys, values)
    for step in range(devices):
        owner = (place - step + devices) % devices
        key_pos = owner * span + lax.iota(jnp.int32, span)
        allowed = allowed_keys(query_pos, key_pos, lengths, causal)
        part_query, part_keys, part_values = block_backward(
            query_heads,
            grad_heads,
            delta,
            logsum,
            key_block,
            value_block,
            allowed,
            batch,
            heads,
            size,
        )
        grad_query = grad_query + part_query
        grad_keys = grad_keys + part_keys
        grad_values = grad_values + part_values
        if causal:
            grad_keys, grad_values = (
                from_behind(grad_keys.astype(jnp.bfloat16), "seq", 1).astype(grad_keys.dtype),
                from_behind(grad_values.astype(jnp.bfloat16), "seq", 1).astype(grad_values.dtype),
            )
        else:
            grad_keys, grad_values = (
                from_behind(grad_keys.astype(jnp.bfloat16), "seq", 1).astype(grad_keys.dtype),
                from_behind(grad_values.astype(jnp.bfloat16), "seq", 1).astype(grad_values.dtype),
            )
        if step + 1 < devices:
            if causal:
                key_block, value_block = shifted((key_block, value_block), "seq", 1)
            else:
                key_block, value_block = from_behind((key_block, value_block), "seq", 1)
    return (grad_query.reshape(span, batch, width), grad_keys, grad_values)


def per_device_general(
    hidden_in,
    memory,
    src_len,
    out_grad,
    w_self_qkv,
    w_self_out,
    w_cross_q,
    w_cross_kv,
    w_cross_out,
    w_ffn_in,
    w_ffn_out,
    biases,
    ffn_bias,
    norm_gain,
    norm_shift,
):
    span, batch, width = hidden_in.shape
    heads = H
    rows = span * batch
    layout = (span, batch, width)
    tokens = hidden_in.reshape(rows, width)
    sources = memory.reshape(rows, width)
    joined = jnp.dot(tokens, w_self_qkv, preferred_element_type=jnp.float32)
    query_self = ((joined[:, :width] + biases[0]) * 0.125).astype(jnp.bfloat16)
    key_self = joined[:, width : 2 * width].astype(jnp.bfloat16)
    value_self = (joined[:, 2 * width :] + biases[1]).astype(jnp.bfloat16)
    mixed_self, logsum_self = attend_forward(
        query_self.reshape(layout),
        key_self.reshape(layout),
        value_self.reshape(layout),
        src_len,
        True,
        heads,
    )
    out_self = mixed_self.reshape(rows, width).astype(jnp.bfloat16)
    resid_one = (
        tokens.astype(jnp.float32)
        + jnp.dot(out_self, w_self_out, preferred_element_type=jnp.float32)
        + biases[2]
    )
    normed_one, unit_one, scale_one = norm_forward(resid_one, norm_gain[0], norm_shift[0])
    normed_one_low = normed_one.astype(jnp.bfloat16)
    query_cross = (
        (jnp.dot(normed_one_low, w_cross_q, preferred_element_type=jnp.float32) + biases[3]) * 0.125
    ).astype(jnp.bfloat16)
    pair = jnp.dot(sources, w_cross_kv, preferred_element_type=jnp.float32)
    key_cross = pair[:, :width].astype(jnp.bfloat16)
    value_cross = (pair[:, width:] + biases[4]).astype(jnp.bfloat16)
    mixed_cross, logsum_cross = attend_forward(
        query_cross.reshape(layout),
        key_cross.reshape(layout),
        value_cross.reshape(layout),
        src_len,
        False,
        heads,
    )
    out_cross = mixed_cross.reshape(rows, width).astype(jnp.bfloat16)
    resid_two = (
        normed_one + jnp.dot(out_cross, w_cross_out, preferred_element_type=jnp.float32) + biases[5]
    )
    normed_two, unit_two, scale_two = norm_forward(resid_two, norm_gain[1], norm_shift[1])
    normed_two_low = normed_two.astype(jnp.bfloat16)
    inner = jnp.dot(normed_two_low, w_ffn_in, preferred_element_type=jnp.float32) + ffn_bias
    active = jax.nn.gelu(inner, approximate=False).astype(jnp.bfloat16)
    resid_three = (
        normed_two + jnp.dot(active, w_ffn_out, preferred_element_type=jnp.float32) + biases[6]
    )
    result, unit_three, scale_three = norm_forward(resid_three, norm_gain[2], norm_shift[2])
    layer_out = result.astype(jnp.bfloat16).reshape(layout)
    grad_three, gain_three, shift_three = norm_backward(
        out_grad.reshape(rows, width).astype(jnp.float32), unit_three, scale_three, norm_gain[2]
    )
    branch_three = grad_three.astype(jnp.bfloat16)
    hidden_pre, hidden_act = (inner, active)
    grad_ffn_out = contract_rows(hidden_act, branch_three)
    grad_act = times_transposed(branch_three, w_ffn_out)
    unused, pull = jax.vjp(partial(jax.nn.gelu, approximate=False), hidden_pre)
    grad_pre = pull(grad_act)[0].astype(jnp.bfloat16)
    grad_ffn_in = contract_rows(normed_two_low, grad_pre)
    grad_normed_two = grad_three + times_transposed(grad_pre, w_ffn_in)
    grad_two, gain_two, shift_two = norm_backward(
        grad_normed_two, unit_two, scale_two, norm_gain[1]
    )
    branch_two = grad_two.astype(jnp.bfloat16)
    grad_cross_out = contract_rows(out_cross, branch_two)
    grad_mixed_cross = times_transposed(branch_two, w_cross_out).astype(jnp.bfloat16)
    raw_query, grad_keys, grad_values = attend_backward(
        query_cross.reshape(layout),
        key_cross.reshape(layout),
        value_cross.reshape(layout),
        mixed_cross,
        grad_mixed_cross.reshape(layout),
        logsum_cross,
        src_len,
        False,
        heads,
    )
    grad_query_cross = (raw_query.reshape(rows, width) * 0.125).astype(jnp.bfloat16)
    grad_pair = jnp.concatenate(
        [
            grad_keys.reshape(rows, width).astype(jnp.bfloat16),
            grad_values.reshape(rows, width).astype(jnp.bfloat16),
        ],
        axis=1,
    )
    grad_cross_q = contract_rows(normed_one_low, grad_query_cross)
    grad_cross_kv = contract_rows(sources, grad_pair)
    grad_memory = times_transposed(grad_pair, w_cross_kv).reshape(layout)
    grad_normed_one = grad_two + times_transposed(grad_query_cross, w_cross_q)
    grad_one, gain_one, shift_one = norm_backward(
        grad_normed_one, unit_one, scale_one, norm_gain[0]
    )
    branch_one = grad_one.astype(jnp.bfloat16)
    grad_self_out = contract_rows(out_self, branch_one)
    grad_mixed_self = times_transposed(branch_one, w_self_out).astype(jnp.bfloat16)
    raw_query, grad_keys, grad_values = attend_backward(
        query_self.reshape(layout),
        key_self.reshape(layout),
        value_self.reshape(layout),
        mixed_self,
        grad_mixed_self.reshape(layout),
        logsum_self,
        src_len,
        True,
        heads,
    )
    grad_joined = jnp.concatenate(
        [
            (raw_query.reshape(rows, width) * 0.125).astype(jnp.bfloat16),
            grad_keys.reshape(rows, width).astype(jnp.bfloat16),
            grad_values.reshape(rows, width).astype(jnp.bfloat16),
        ],
        axis=1,
    )
    grad_self_qkv = contract_rows(tokens, grad_joined)
    grad_in = (grad_one + times_transposed(grad_joined, w_self_qkv)).reshape(layout)
    vector_terms = jnp.stack(
        [
            jnp.sum(grad_joined[:, :width].astype(jnp.float32), axis=0),
            jnp.sum(grad_joined[:, 2 * width :].astype(jnp.float32), axis=0),
            jnp.sum(grad_one, axis=0),
            jnp.sum(grad_query_cross.astype(jnp.float32), axis=0),
            jnp.sum(grad_pair[:, width:].astype(jnp.float32), axis=0),
            jnp.sum(grad_two, axis=0),
            jnp.sum(grad_three, axis=0),
            gain_one,
            gain_two,
            gain_three,
            shift_one,
            shift_two,
            shift_three,
        ]
    )
    bias_terms = jnp.sum(grad_pre.astype(jnp.float32), axis=0)[None]
    (
        grad_self_qkv,
        grad_self_out,
        grad_cross_q,
        grad_cross_kv,
        grad_cross_out,
        grad_ffn_in,
        grad_ffn_out,
        vector_terms,
        bias_terms,
    ) = (
        lax.psum_scatter(
            grad_self_qkv.astype(jnp.bfloat16), "seq", scatter_dimension=1, tiled=True
        ).astype(jnp.float32),
        lax.psum_scatter(
            grad_self_out.astype(jnp.bfloat16), "seq", scatter_dimension=1, tiled=True
        ).astype(jnp.float32),
        lax.psum_scatter(
            grad_cross_q.astype(jnp.bfloat16), "seq", scatter_dimension=1, tiled=True
        ).astype(jnp.float32),
        lax.psum_scatter(
            grad_cross_kv.astype(jnp.bfloat16), "seq", scatter_dimension=1, tiled=True
        ).astype(jnp.float32),
        lax.psum_scatter(
            grad_cross_out.astype(jnp.bfloat16), "seq", scatter_dimension=1, tiled=True
        ).astype(jnp.float32),
        lax.psum_scatter(
            grad_ffn_in.astype(jnp.bfloat16), "seq", scatter_dimension=1, tiled=True
        ).astype(jnp.float32),
        lax.psum_scatter(
            grad_ffn_out.astype(jnp.bfloat16), "seq", scatter_dimension=1, tiled=True
        ).astype(jnp.float32),
        lax.psum_scatter(
            vector_terms.astype(jnp.bfloat16), "seq", scatter_dimension=1, tiled=True
        ).astype(jnp.float32),
        lax.psum_scatter(
            bias_terms.astype(jnp.bfloat16), "seq", scatter_dimension=1, tiled=True
        ).astype(jnp.float32),
    )
    (
        grad_self_qkv,
        grad_self_out,
        grad_cross_q,
        grad_cross_kv,
        grad_cross_out,
        grad_ffn_in,
        grad_ffn_out,
    ) = (
        lax.psum_scatter(
            grad_self_qkv.astype(jnp.bfloat16), "batch", scatter_dimension=0, tiled=True
        ).astype(jnp.float32),
        lax.psum_scatter(
            grad_self_out.astype(jnp.bfloat16), "batch", scatter_dimension=0, tiled=True
        ).astype(jnp.float32),
        lax.psum_scatter(
            grad_cross_q.astype(jnp.bfloat16), "batch", scatter_dimension=0, tiled=True
        ).astype(jnp.float32),
        lax.psum_scatter(
            grad_cross_kv.astype(jnp.bfloat16), "batch", scatter_dimension=0, tiled=True
        ).astype(jnp.float32),
        lax.psum_scatter(
            grad_cross_out.astype(jnp.bfloat16), "batch", scatter_dimension=0, tiled=True
        ).astype(jnp.float32),
        lax.psum_scatter(
            grad_ffn_in.astype(jnp.bfloat16), "batch", scatter_dimension=0, tiled=True
        ).astype(jnp.float32),
        lax.psum_scatter(
            grad_ffn_out.astype(jnp.bfloat16), "batch", scatter_dimension=0, tiled=True
        ).astype(jnp.float32),
    )
    vector_terms, bias_terms = lax.psum((vector_terms, bias_terms), "batch")
    return (
        layer_out,
        grad_in,
        grad_memory,
        grad_self_qkv,
        grad_self_out,
        grad_cross_q,
        grad_cross_kv,
        grad_cross_out,
        grad_ffn_in,
        grad_ffn_out,
        vector_terms[0:7],
        bias_terms[0],
        vector_terms[7:10],
        vector_terms[10:13],
    )


LOG2E = 1.4426950408889634
NN = (((1,), (0,)), ((), ()))
NT = (((1,), (1,)), ((), ()))
HD = 64
BIG = -1e30
f32, bf16 = jnp.float32, jnp.bfloat16

def dot(a, b, dims=NN):
    return lax.dot_general(a, b, dims, preferred_element_type=f32)

def lanes(shape):
    return lax.broadcasted_iota(jnp.int32, shape, len(shape) - 1)

def swap_halves(x):
    return jnp.concatenate([x[:, HD:], x[:, :HD]], axis=1)

def fwd_kernel(len_ref, q_ref, k_ref, v_ref, o_ref, lp_ref, acc_ref, *, causal, heads, qb, ahead):
    p = pl.program_id(0)
    n = q_ref.shape[0]
    nk = k_ref.shape[0]
    scaled = q_ref[...].astype(f32) * LOG2E
    hi = scaled.astype(bf16)
    lo = (scaled - hi.astype(f32)).astype(bf16)
    first = lanes((n, 128)) < HD
    hi_s, lo_s = swap_halves(hi), swap_halves(lo)
    q_aug = (jnp.where(first, hi, lo_s), jnp.where(first, hi_s, lo))
    kk = k_ref[...]
    k_s = swap_halves(kk)
    k_aug = [jnp.where(first, kk, k_s), jnp.where(first, k_s, kk)]
    if not causal:
        length = len_ref[0]
        row = lax.broadcasted_iota(jnp.int32, (nk, 128), 0)
        extra = jnp.where((row >= length) & (lanes((nk, 128)) == 0), BIG, 0.0).astype(bf16)
        k_aug = [jnp.concatenate([x, extra], axis=1) for x in k_aug]
        one = (lanes((n, 128)) == 0).astype(bf16)
        q_aug = [jnp.concatenate([x, one], axis=1) for x in q_aug]
    vt = jnp.transpose(v_ref[...])
    ones = jnp.ones((16, nk), bf16)
    va = [jnp.concatenate([vt[h * HD:(h + 1) * HD], ones], axis=0) for h in range(2)]

    def scores(c, h):
        top_k = (c + 1) * qb if causal else nk
        s = dot(k_aug[h][:top_k], q_aug[h][c * qb:(c + 1) * qb], NT)
        if causal:
            r = lax.broadcasted_iota(jnp.int32, (qb, qb), 0)
            d = jnp.where(r <= lanes((qb, qb)), s[c * qb:], BIG)
            s = jnp.concatenate([s[:c * qb], d], axis=0) if c else d
        return s

    steps = [(c, h) for c in range(n // qb) for h in range(2)]
    queue = [scores(*x) for x in steps[:ahead]]
    parts = []
    for i, (c, h) in enumerate(steps):
        if i + ahead < len(steps):
            queue.append(scores(*steps[i + ahead]))
        s = queue.pop(0)
        m = jnp.max(s, axis=0, keepdims=True)
        pt = jnp.exp2(s - m).astype(bf16)
        ot = dot(va[h][:, :s.shape[0]], pt)
        l = ot[HD:HD + 1]
        parts.append(ot[:HD] * (1.0 / l))
        acc_ref[pl.ds(2 * p + h, 1), c * qb:(c + 1) * qb] = m + jnp.log2(l)
        if h == 1:
            o_ref[c * qb:(c + 1) * qb, :] = jnp.transpose(jnp.concatenate(parts, axis=0)).astype(bf16)
            parts = []

    @pl.when(p == pl.num_programs(0) - 1)
    def _():
        rows = acc_ref[...]
        wide = jnp.concatenate([rows, jnp.zeros((128 - rows.shape[0], n), f32)], axis=0)
        cols = jnp.transpose(wide)
        a = cols.astype(bf16)
        cols = cols - a.astype(f32)
        b = cols.astype(bf16)
        c = (cols - b.astype(f32)).astype(bf16)
        lane = lanes((n, 128))
        sh = lambda x, k: jnp.concatenate([jnp.zeros((n, k), bf16), x[:, :128 - k]], axis=1)
        out = jnp.where(lane < 16, a, jnp.where(lane < 32, sh(b, 16), jnp.where(lane < 48, sh(c, 32), jnp.where(lane == 127, 1.0, 0.0).astype(bf16))))
        lp_ref[...] = out

def attn_fwd(length, q, k, v, causal, qb=256, ahead=2):
    n, d = q.shape
    blk = lambda r: pl.BlockSpec((r, 128), lambda p, l: (0, p))
    return pl.pallas_call(
        functools.partial(fwd_kernel, causal=causal, heads=d // HD, qb=qb, ahead=ahead),
        grid_spec=pltpu.PrefetchScalarGridSpec(
            num_scalar_prefetch=1, grid=(d // 128,),
            in_specs=[blk(n), blk(k.shape[0]), blk(k.shape[0])],
            out_specs=[blk(n), pl.BlockSpec((n, 128), lambda p, l: (0, 0))],
            scratch_shapes=[pltpu.VMEM((16, n), f32)]),
        out_shape=[pltpu.HBM((n, d), bf16), pltpu.HBM((n, 128), bf16)],
        compiler_params=params(40),
        cost_estimate=cost((n + 256) * n * 1024 // (2 if causal else 1) * (d // HD), 8 * n * d, n * n * d // HD),
        name="attn_fwd",
    )(length, *hbm(q, k, v))

def side_rows(kind, refs, own):
    if kind == "early":
        one, cross_a, cross_b, ffn, bias = refs
        both = lambda r: jnp.concatenate([cross_a[r : r + 1, :], cross_b[r : r + 1, :]], axis=1)
        rows = [one[2:3, :], both(0), both(1), ffn[5:6, :], ffn[2:3, :], one[0:1, :], ffn[3:4, :], ffn[0:1, :], one[1:2, :], ffn[4:5, :], ffn[1:2, :]]
        half = rows[0].shape[1] // 2
        wide = bias.shape[1] // 2
        sides = []
        for x in range(2):
            sides += [r[:, x * half : (x + 1) * half] for r in rows]
            sides += [bias[0:1, x * wide + c * half : x * wide + (c + 1) * half] for c in range(wide // half)]
            sides += [jnp.zeros((1, half), f32)] * (16 - len(rows) - wide // half)
        return jnp.concatenate(sides, axis=0).astype(bf16)
    rows = [refs[0][0:2, :], refs[1][0:2, :], own[0:2, :], jnp.zeros((10, own.shape[1]), f32)]
    rows = jnp.concatenate(rows, axis=0)
    return jnp.concatenate([rows, jnp.zeros((16, 128), f32)], axis=1).astype(bf16)


def bwd_kernel(len_ref, q_ref, k_ref, v_ref, o_ref, g_ref, lp_ref, *rest, causal, qb, first_pair, stride, unit, kind):
    if unit:
        place, tok_ref, *side, out_ref, sums_ref, send_ref, own_ref = rest
    else:
        out_ref, sums_ref = rest
    p = pl.program_id(0) * stride + first_pair
    n, nk = q_ref.shape[0], k_ref.shape[0]
    first = lanes((n, 128)) < HD
    q = q_ref[...]
    scaled = q.astype(f32) * LOG2E
    hi = scaled.astype(bf16)
    lo = (scaled - hi.astype(f32)).astype(bf16)
    hi_s, lo_s = swap_halves(hi), swap_halves(lo)
    lp = lp_ref[...]
    q_aug = [jnp.concatenate([x, lp], axis=1) for x in (jnp.where(first, hi, lo_s), jnp.where(first, hi_s, lo))]
    kk = k_ref[...]
    k_s = swap_halves(kk)
    v = v_ref[...]
    lane = lanes((nk, 128))
    g = g_ref[...]
    zero = jnp.zeros((), bf16)
    go = g.astype(f32) * o_ref[...].astype(f32)
    go_hi = go.astype(bf16)
    go_lo = (go - go_hi.astype(f32)).astype(bf16)
    br = lax.broadcasted_iota(jnp.int32, (128, 128), 0)
    bl = lanes((128, 128))
    pick = jnp.where(((bl < 3) & (br < HD)) | ((bl >= 3) & (bl < 6) & (br >= HD)), 1.0, 0.0).astype(bf16)
    dl = dot(go_hi, pick) + dot(go_lo, pick)
    da = dl.astype(bf16)
    rest = dl - da.astype(f32)
    db = rest.astype(bf16)
    dc = (rest - db.astype(f32)).astype(bf16)
    part = lanes((n, 128))
    part = jnp.where(part >= 3, part - 3, part)
    dpack = jnp.where(part == 0, da, jnp.where(part == 1, db, dc))
    g_aug = jnp.concatenate([g, dpack], axis=1)
    qt = jnp.transpose(q)
    gt = jnp.transpose(g)
    minus = jnp.full((), -1.0, bf16)
    row = lax.broadcasted_iota(jnp.int32, (nk, 128), 0)
    dq_parts, dkts, dvts = [], [], []
    for h in range(2):
        head = 2 * p + h
        sel = jnp.where((lane < 48) & ((lane & 15) == head), -1.0, 0.0)
        if not causal:
            sel = jnp.where((lane == 127) & (row >= len_ref[0]), BIG, sel)
        k_aug = jnp.concatenate([jnp.where(first, kk, k_s) if h == 0 else jnp.where(first, k_s, kk), sel.astype(bf16)], axis=1)
        dsel = jnp.where((lane >= 3 * h) & (lane < 3 * h + 3), -1.0, 0.0).astype(bf16)
        v_m = jnp.where(first, v, zero) if h == 0 else jnp.where(first, zero, v)
        v_aug = jnp.concatenate([v_m, dsel], axis=1)
        parts = []
        dkt = jnp.zeros((HD, nk), f32)
        dvt = jnp.zeros((HD, nk), f32)
        for c in range(n // qb):
            rows = slice(c * qb, (c + 1) * qb)
            top_k = (c + 1) * qb if causal else nk
            s = dot(q_aug[h][rows], k_aug[:top_k], NT)
            w = jnp.exp2(s)
            if causal:
                r = lax.broadcasted_iota(jnp.int32, (qb, qb), 0)
                dg = jnp.where(r >= lanes((qb, qb)), w[:, c * qb:], 0.0)
                w = jnp.concatenate([w[:, :c * qb], dg], axis=1) if c else dg
            dp = dot(g_aug[rows], v_aug[:top_k], NT)
            ds = (w * dp).astype(bf16)
            wb = w.astype(bf16)
            a = dot(gt[h * HD:(h + 1) * HD, rows], wb)
            b = dot(qt[h * HD:(h + 1) * HD, rows], ds)
            if top_k < nk:
                pad = jnp.zeros((HD, nk - top_k), f32)
                a = jnp.concatenate([a, pad], axis=1)
                b = jnp.concatenate([b, pad], axis=1)
            dvt = dvt + a
            dkt = dkt + b
            parts.append(dot(ds, kk[:top_k]))
        dq_parts.append(parts)
        dkts.append(dkt)
        dvts.append(dvt)
    sums = jnp.zeros((1, 128), f32)
    dqs = []
    for c in range(n // qb):
        rows = slice(c * qb, (c + 1) * qb)
        fl = lanes((qb, 128)) < HD
        dq = (jnp.where(fl, dq_parts[0][c], dq_parts[1][c]) * 0.125).astype(bf16)
        dqs.append(dq)
        sums = sums + jnp.sum(dq.astype(f32), axis=0, keepdims=True)
    dk = jnp.transpose(jnp.concatenate(dkts, axis=0)).astype(bf16)
    dv = jnp.transpose(jnp.concatenate(dvts, axis=0)).astype(bf16)
    v_sums = jnp.sum(dv.astype(f32), axis=0, keepdims=True)
    grads = (jnp.concatenate(dqs, axis=0), dk, dv)
    if not unit:
        sums_ref[...] = jnp.concatenate([sums, v_sums, jnp.zeros((6, 128), f32)], axis=0)
        for m, part in enumerate(grads):
            out_ref[m] = part
        return
    for at in range(2):
        @pl.when(pl.program_id(0) == at)
        def _(at=at):
            cols = slice(at * 128, (at + 1) * 128)
            sums_ref[:, cols] = jnp.concatenate([sums, v_sums, jnp.zeros((6, 128), f32)], axis=0)
            for m, part in enumerate(grads):
                out_ref[m, :, cols] = part

    @pl.when(pl.program_id(0) == 1)
    def _():
        joined = jnp.concatenate([out_ref[0], out_ref[1], out_ref[2]], axis=1)
        store_units(place, dot(tok_ref[...], joined, TN).astype(bf16), unit, send_ref, own_ref)
        if kind:
            rows = side_rows(kind, side, sums_ref[...])
            for ref in (send_ref, own_ref):
                for y in range(2):
                    for x in range(2):
                        for z in range(ref.shape[2]):
                            ref[y, x, z, unit:] = rows


def attn_bwd(length, q, k, v, o, g, lp, causal, first, stride, count, tokens=None, place=None, nb=0, kind="", side=(), qb=256):
    n, d = q.shape
    blk = pl.BlockSpec((n, 128), lambda p, l: (0, first + stride * p))
    ins = [blk] * 5 + [pl.BlockSpec((n, 128), lambda p, l: (0, 0))]
    outs = [pl.BlockSpec((3, n, 128), lambda p, l: (0, 0, p)), pl.BlockSpec((8, 128), lambda p, l: (0, p))]
    shapes = [pltpu.HBM((3, n, count * 128), bf16), pltpu.HBM((8, count * 128), f32)]
    args = hbm(q, k, v, o, g, lp)
    unit = 0
    if tokens is not None:
        unit = d // nb
        rows = unit + {"early": 32, "late": 16, "": 0}[kind]
        ins += [pl.BlockSpec(memory_space=pltpu.SMEM), pl.BlockSpec((n, d), lambda p, l: (0, 0))]
        ins += [pl.BlockSpec(s.shape, lambda p, l: (0, 0)) for s in side]
        args += [place] + hbm(tokens, *side)
        outs = [pl.BlockSpec((3, n, 256), lambda p, l: (0, 0, 0)), pl.BlockSpec((8, 256), lambda p, l: (0, 0))]
        outs += [pl.BlockSpec((2, 2, nb // 4, rows, 384), lambda p, l: (0, 0, 0, 0, 0))] * 2
        shapes += [pltpu.HBM((2, 2, nb // 4, rows, 384), bf16)] * 2
    return pl.pallas_call(
        functools.partial(bwd_kernel, causal=causal, qb=qb, first_pair=first, stride=stride, unit=unit, kind=kind),
        grid_spec=pltpu.PrefetchScalarGridSpec(
            num_scalar_prefetch=1, grid=(count,), in_specs=ins, out_specs=outs),
        out_shape=shapes,
        compiler_params=params(40),
        cost_estimate=cost((n + 256) * n * 2560 // (2 if causal else 1) * count * 2, 16 * n * count * 128, 2 * n * n * count),
        name="attn_bwd",
    )(length, *args)


TN = (((0,), (0,)), ((), ()))


def cost(flops, moved, exps=0):
    return pl.CostEstimate(flops=int(flops), bytes_accessed=int(moved), transcendentals=int(exps))


def params(mib):
    return pltpu.CompilerParams(vmem_limit_bytes=mib * 2**20)


def hbm(*values):
    return [pltpu.with_memory_space_constraint(v, pltpu.HBM) for v in values]


def whole():
    return pl.BlockSpec(memory_space=pltpu.VMEM)


def fixed(shape):
    return pl.BlockSpec(shape, lambda *_: (0,) * len(shape), pipeline_mode=pl.Buffered(1))


def spread_rows(block):
    return lambda i, *_: (i, 0)


def project_kernel(place, mine, got, weight, biases, *outs, step, plan):
    i = pl.program_id(0)
    x = jnp.where(i // step == place[0], mine[...], got[...])
    outs[0][...] = x
    joined = dot(x, weight[...])
    width = x.shape[1]
    for n, (bias, scale) in enumerate(plan):
        part = joined[:, n * width : (n + 1) * width]
        if bias is not None:
            part = part + biases[bias : bias + 1, :]
        if scale != 1.0:
            part = part * scale
        outs[n + 1][...] = part.astype(bf16)


def project(place, pairs, got, weight, biases, plan, rows=256):
    half, width = got.shape
    step = half // rows
    cols = weight.shape[1]
    block = pl.BlockSpec((rows, width), lambda i, p: (i, 0))
    return pl.pallas_call(
        functools.partial(project_kernel, step=step, plan=plan),
        grid_spec=pltpu.PrefetchScalarGridSpec(
            num_scalar_prefetch=1,
            grid=(2 * step,),
            in_specs=[
                pl.BlockSpec((rows, width), lambda i, p: (i % step, p[0])),
                pl.BlockSpec((rows, width), lambda i, p: (i % step, 0)),
                whole(),
                whole(),
            ],
            out_specs=[block] * (1 + len(plan)),
        ),
        out_shape=[pltpu.HBM((2 * half, width), bf16)] * (1 + len(plan)),
        compiler_params=params(32),
        cost_estimate=cost(4 * half * width * cols, 2 * width * cols + 12 * half * width),
        name="project",
    )(place, *hbm(pairs, got), weight, biases)


def norm_unit(value):
    mean = jnp.mean(value, axis=-1, keepdims=True)
    centred = value - mean
    scale = lax.rsqrt(jnp.mean(centred * centred, axis=-1, keepdims=True) + 1e-05)
    return centred * scale, scale


def norm_back(grad, unit, scale, gain):
    weighted = grad * gain
    return scale * (
        weighted
        - jnp.mean(weighted, axis=-1, keepdims=True)
        - unit * jnp.mean(weighted * unit, axis=-1, keepdims=True)
    )


def row_sum(value):
    return jnp.sum(value, axis=0, keepdims=True)


def after_self_kernel(o, tok, w_out, w_q, biases, gain, shift, unit_ref, scale_ref, low_ref, q_ref):
    resid = tok[...].astype(f32) + dot(o[...], w_out[...]) + biases[2:3, :]
    unit, scale = norm_unit(resid)
    unit_ref[...] = unit
    scale_ref[...] = jnp.broadcast_to(scale, scale_ref.shape)
    low_ = (unit * gain[0:1, :] + shift[0:1, :]).astype(bf16)
    low_ref[...] = low_
    q_ref[...] = ((dot(low_, w_q[...]) + biases[3:4, :]) * 0.125).astype(bf16)


def after_self(o, tok, w_out, w_q, biases, gain, shift, rows=256):
    n, d = o.shape
    block = pl.BlockSpec((rows, d), lambda i: (i, 0))
    return pl.pallas_call(
        after_self_kernel,
        grid=(n // rows,),
        in_specs=[block, block, whole(), whole()] + [whole()] * 3,
        out_specs=[block, pl.BlockSpec((rows, 128), lambda i: (i, 0)), block, block],
        out_shape=[
            pltpu.HBM((n, d), f32),
            pltpu.HBM((n, 128), f32),
            pltpu.HBM((n, d), bf16),
            pltpu.HBM((n, d), bf16),
        ],
        compiler_params=params(32),
        cost_estimate=cost(4 * n * d * d, 4 * d * d + 12 * n * d),
        name="after_self",
    )(*hbm(o, tok), w_out, w_q, biases, gain, shift)


RATE = 0.3275911 * 0.7071067811865476
TAIL = tuple(0.5 * c for c in (0.254829592, -0.284496736, 1.421413741, -1.453152027, 1.061405429))
DENSITY = 0.3989422804014327


def gelu_pair(v):
    size = jnp.abs(v)
    base = 1.0 + RATE * size
    t = pl.reciprocal(base, approx=True)
    t = t * (2.0 - base * t)
    poly = TAIL[4]
    for c in TAIL[3::-1]:
        poly = c + t * poly
    bell = jnp.exp2((v * v) * (-0.5 * LOG2E))
    tail = t * poly * bell
    below = jnp.where(v >= 0.0, 1.0 - tail, tail)
    return v * below, below + v * (DENSITY * bell)


def ffn_kernel(
    o, unit_one, cot, w_co, w_in, w_out, biases, ffn_bias, gain, shift,
    layer_ref, g2_ref, gm_ref, sums_ref, fsum_ref, grads_ref,
    slope, act_all, pre_all, b3_all, b2_all, low_turned, o_turned, *, blocks, nz,
):
    i = pl.program_id(0)
    rows, d = o.shape
    n_chunks, _, chunk = act_all.shape

    @pl.when(i == 0)
    def _():
        sums_ref[...] = jnp.zeros_like(sums_ref)
        fsum_ref[...] = jnp.zeros_like(fsum_ref)

    @pl.when(i < blocks)
    def _():
        here = pl.ds(pl.multiple_of(i * rows, rows), rows)
        o_turned[:, here] = jnp.transpose(o[...])
        normed_one = unit_one[...] * gain[0:1, :] + shift[0:1, :]
        resid = normed_one + dot(o[...], w_co[...]) + biases[5:6, :]
        unit_two, scale_two = norm_unit(resid)
        normed_two = unit_two * gain[1:2, :] + shift[1:2, :]
        low_two = normed_two.astype(bf16)
        low_turned[:, here] = jnp.transpose(low_two)

        def inner(j):
            at = slice(j * chunk, (j + 1) * chunk)
            return dot(low_two, w_in[:, at]) + ffn_bias[0:1, at]

        total = normed_two + biases[6:7, :]
        ahead = inner(0)
        for j in range(n_chunks):
            v = ahead
            if j + 1 < n_chunks:
                ahead = inner(j + 1)
            act, grad = gelu_pair(v)
            act = act.astype(bf16)
            act_all[j, here, :] = act
            slope[:, j * chunk : (j + 1) * chunk] = grad
            total = total + dot(act, w_out[j * chunk : (j + 1) * chunk, :])
        unit, scale = norm_unit(total)
        layer_ref[...] = (unit * gain[2:3, :] + shift[2:3, :]).astype(bf16)
        g = cot[...].astype(f32)
        grad_three = norm_back(g, unit, scale, gain[2:3, :])
        branch = grad_three.astype(bf16)
        b3_all[here, :] = branch
        sums_ref[0:1, :] += row_sum(g * unit)
        sums_ref[1:2, :] += row_sum(g)
        sums_ref[2:3, :] += row_sum(grad_three)

        def back(j):
            return dot(branch, w_out[j * chunk : (j + 1) * chunk, :], NT)

        total = grad_three
        ahead = back(0)
        for j in range(n_chunks):
            v = ahead
            if j + 1 < n_chunks:
                ahead = back(j + 1)
            at = slice(j * chunk, (j + 1) * chunk)
            pre = (v * slope[:, at]).astype(bf16)
            pre_all[j, here, :] = pre
            fsum_ref[0:1, at] += row_sum(pre.astype(f32))
            total = total + dot(pre, w_in[:, at], NT)
        grad_two = norm_back(total, unit_two, scale_two, gain[1:2, :])
        g2_ref[...] = grad_two
        branch = grad_two.astype(bf16)
        b2_all[here, :] = branch
        sums_ref[3:4, :] += row_sum(total * unit_two)
        sums_ref[4:5, :] += row_sum(total)
        sums_ref[5:6, :] += row_sum(grad_two)
        gm_ref[...] = dot(branch, w_co[...], NT).astype(bf16)

    @pl.when(i >= blocks)
    def _():
        z = i - blocks
        half = d // 2
        count = grads_ref.shape[1]
        unit = grads_ref.shape[2]
        value = dot(act_all[z], b3_all[...], TN).astype(bf16)
        pieces = value.shape[0] // (count * unit)
        for u in range(count):
            for c in range(pieces):
                top = (u * pieces + c) * unit
                for x in range(2):
                    grads_ref[x, u, :, c * half : (c + 1) * half] = value[top : top + unit, x * half : (x + 1) * half]
        start = pieces * half
        own = pl.ds(pl.multiple_of(z * count * unit, count * unit), count * unit)
        a = low_turned[own, :]
        for j in range(n_chunks):
            value = dot(a, pre_all[j]).astype(bf16)
            x, left = divmod(j, n_chunks // 2)
            for u in range(count):
                grads_ref[x, u, :, start + left * chunk : start + (left + 1) * chunk] = value[u * unit : (u + 1) * unit]
        start += n_chunks // 2 * chunk
        value = dot(o_turned[own, :], b2_all[...]).astype(bf16)
        for u in range(count):
            for x in range(2):
                grads_ref[x, u, :, start : start + half] = value[u * unit : (u + 1) * unit, x * half : (x + 1) * half]


def ffn(o, unit_one, cot, w_co, w_in, w_out, biases, ffn_bias, gain, shift, nb, rows=256):
    n, d = o.shape
    ff = w_in.shape[1]
    blocks = n // rows
    nz = ff // d
    unit = d // nb
    block = pl.BlockSpec((rows, d), lambda i: (jnp.minimum(i, blocks - 1), 0))
    width = ff + d // 2
    return pl.pallas_call(
        functools.partial(ffn_kernel, blocks=blocks, nz=nz),
        grid=(blocks + nz,),
        in_specs=[block, block, block] + [whole()] * 7,
        out_specs=[block, block, block,
                   pl.BlockSpec((8, d), lambda i: (0, 0)), pl.BlockSpec((8, ff), lambda i: (0, 0)),
                   pl.BlockSpec((2, nb // nz, unit, width), lambda i: (0, jnp.maximum(i - blocks, 0), 0, 0))],
        out_shape=[
            pltpu.HBM((n, d), bf16),
            pltpu.HBM((n, d), f32),
            pltpu.HBM((n, d), bf16),
            pltpu.HBM((8, d), f32),
            pltpu.HBM((8, ff), f32),
            pltpu.HBM((2, nb, unit, width), bf16),
        ],
        scratch_shapes=[
            pltpu.VMEM((rows, ff), f32),
            pltpu.VMEM((nz, n, d), bf16),
            pltpu.VMEM((nz, n, d), bf16),
            pltpu.VMEM((n, d), bf16),
            pltpu.VMEM((n, d), bf16),
            pltpu.VMEM((d, n), bf16),
            pltpu.VMEM((d, n), bf16),
        ],
        compiler_params=params(60),
        cost_estimate=cost(12 * n * d * ff + 6 * n * d * d, 8 * d * ff + 20 * n * d, 2 * n * ff),
        name="ffn",
    )(*hbm(o, unit_one, cot), w_co, w_in, w_out, biases, ffn_bias, gain, shift)


def before_self_kernel(g2, gqa, gqb, unit_ref, scale_ref, w_q, w_out, gain, g1_ref, b1_ref, gm_ref, gq_ref, sums_ref):
    @pl.when(pl.program_id(0) == 0)
    def _():
        sums_ref[...] = jnp.zeros_like(sums_ref)

    gq = jnp.concatenate([gqa[0], gqb[0]], axis=1)
    gq_ref[...] = gq
    g = g2[...] + dot(gq, w_q[...], NT)
    unit = unit_ref[...]
    grad = norm_back(g, unit, scale_ref[:, 0:1], gain[0:1, :])
    g1_ref[...] = grad
    branch = grad.astype(bf16)
    b1_ref[...] = branch
    sums_ref[0:1, :] += row_sum(g * unit)
    sums_ref[1:2, :] += row_sum(g)
    sums_ref[2:3, :] += row_sum(grad)
    gm_ref[...] = dot(branch, w_out[...], NT).astype(bf16)


def before_self(g2, gqa, gqb, unit, scale, w_q, w_out, gain, rows=256):
    n, d = g2.shape
    block = pl.BlockSpec((rows, d), lambda i: (i, 0))
    return pl.pallas_call(
        before_self_kernel,
        grid=(n // rows,),
        in_specs=[block, pl.BlockSpec((1, rows, d // 2), lambda i: (0, i, 0)), pl.BlockSpec((1, rows, d // 2), lambda i: (0, i, 0)), block, pl.BlockSpec((rows, 128), lambda i: (i, 0)), whole(), whole(), whole()],
        out_specs=[block, block, block, block, pl.BlockSpec((8, d), lambda i: (0, 0))],
        out_shape=[
            pltpu.HBM((n, d), f32),
            pltpu.HBM((n, d), bf16),
            pltpu.HBM((n, d), bf16),
            pltpu.HBM((n, d), bf16),
            pltpu.HBM((8, d), f32),
        ],
        compiler_params=params(32),
        cost_estimate=cost(4 * n * d * d, 4 * d * d + 18 * n * d),
        name="before_self",
    )(*hbm(g2, gqa, gqb, unit, scale), w_q, w_out, gain)


def store_units(place, value, unit, send_ref, own_ref, first=0, z_local=False):
    mx, mz, my, core = place[0], place[1], place[2], place[3]
    half = value.shape[1] // 2
    for mine in range(2):
        @pl.when(core == mine)
        def _():
            for u in range(value.shape[0] // unit):
                ref = own_ref if u % 2 == mine else send_ref
                z = 0 if z_local else jnp.bitwise_xor(u // 4, mz)
                y = jnp.bitwise_xor((u // 2) % 2, my)
                for x in range(2):
                    ref[y, jnp.bitwise_xor(x, mx), z, :unit] = value[u * unit : (u + 1) * unit, x * half : (x + 1) * half]


def wide_kernel(place, *refs, steps, unit):
    send_ref, own_ref = refs[-2:]
    j = pl.program_id(0)
    for a_at, left, right, first, count in steps:
        @pl.when((j >= first) & (j < first + count))
        def _(a_at=a_at, left=left, right=right):
            flat = lambda r: refs[r][...].reshape(refs[r].shape[-2:])
            value = dot(refs[a_at][...], jnp.concatenate([flat(left), flat(right)], axis=1), TN).astype(bf16)
            store_units(place, value, unit, send_ref, own_ref)


def wide_grad(place, terms, nb, block=384):
    n, rows = terms[0][0].shape
    unit = rows // nb
    arrays, specs, steps, first = [], [], [], 0
    whole_a = pl.BlockSpec((n, rows), lambda j, p: (0, 0))
    for a, b, leads in terms:
        if not any(a is other for other in arrays):
            arrays.append(a)
            specs.append(whole_a)
        a_at = next(i for i, other in enumerate(arrays) if other is a)
        count = b.shape[-1] // block // (1 if leads else 2)
        for side in range(2):
            def where(j, p, first=first, count=count, side=side, leads=leads):
                inside = jnp.clip(j - first, 0, count - 1)
                return (leads[side], 0, inside) if leads else (0, side * count + inside)
            arrays.append(b)
            specs.append(pl.BlockSpec((1, n, block) if leads else (n, block), where))
        steps.append((a_at, len(arrays) - 2, len(arrays) - 1, first, count))
        first += count
    steps = [(a, l, r, f, c) for a, l, r, f, c in steps]
    out = [pltpu.HBM((2, 2, nb // 4, unit, first * block), bf16)] * 2
    out_specs = [pl.BlockSpec((2, 2, nb // 4, unit, block), lambda j, p: (0, 0, 0, 0, j))] * 2
    return pl.pallas_call(
        functools.partial(wide_kernel, steps=steps, unit=unit),
        grid_spec=pltpu.PrefetchScalarGridSpec(num_scalar_prefetch=1, grid=(first,), in_specs=specs, out_specs=out_specs),
        out_shape=out,
        compiler_params=params(40),
        cost_estimate=cost(4 * n * rows * first * block, 4 * rows * first * block + 4 * n * first * block),
        name="wide_grad",
    )(place, *hbm(*arrays))


def grad_rows_kernel(place, *refs, columns, based):
    gs, weight = refs[: len(columns)], refs[len(columns)]
    out_ref = refs[-1]
    value = None
    for g, chunks in zip(gs, columns):
        for m, starts in enumerate(chunks):
            if not starts:
                continue
            w = [weight[:, s : s + size] for s, size in starts]
            w = w[0] if len(w) == 1 else jnp.concatenate(w, axis=1)
            term = dot(g[m], w, NT)
            value = term if value is None else value + term
    if based:
        value = value + refs[len(columns) + 1][...]

    out_ref[...] = value.astype(out_ref.dtype)


def grad_rows(place, terms, columns, weight, base, mine, rows=256):
    n = terms[0].shape[1]
    d, k = weight.shape
    steps = n // 2 // rows
    half = lambda i, p: (p[0] if mine else 1 - p[0]) * steps + i
    ins = [pl.BlockSpec((t.shape[0], rows, t.shape[2]), lambda i, p: (0, half(i, p), 0)) for t in terms] + [whole()]
    args = hbm(*terms) + [weight]
    if base is not None:
        ins.append(pl.BlockSpec((rows, d), lambda i, p: (half(i, p), 0)))
        args += hbm(base)
    return pl.pallas_call(
        functools.partial(grad_rows_kernel, columns=columns, based=base is not None),
        grid_spec=pltpu.PrefetchScalarGridSpec(
            num_scalar_prefetch=1,
            grid=(steps,),
            in_specs=ins,
            out_specs=pl.BlockSpec((rows, d), lambda i, p: (i, 0)),
        ),
        out_shape=pltpu.HBM((n // 2, d), f32 if mine else bf16),
        compiler_params=params(40),
        cost_estimate=cost(n * k * d, n * k + 2 * k * d + 4 * n * d),
        name="grad_rows",
    )(place, *args)


def route(nb, move):
    dz, dy, dc, dx = move
    pairs = []
    for b in range(nb):
        z, y, core = b // 4, (b // 2) % 2, b % 2
        for x in range(2):
            target = (z ^ dz) * 4 + (y ^ dy) * 2 + (core ^ dc)
            pairs.append((b * 2 + x, target * 2 + (x ^ dx)))
    return pairs


def send(value, nb, move):
    return lax.ppermute(value, ("z", "y", "core", "seq"), route(nb, move))


def core_stage(buffers, nb):
    to_send, own = buffers
    return own, send(to_send, nb, (0, 0, 1, 0))


def y_prepare(state):
    own, got = state
    return (own[1].astype(f32) + got[1].astype(f32)).astype(bf16), (own, got)


def y_move(value, nb):
    return send(value, nb, (0, 1, 0, 0))


def x_prepare(state):
    own, got, more = state
    total = own[0].astype(f32) + got[0].astype(f32) + more.astype(f32)
    return total[0].astype(bf16), total[1].astype(bf16)


def x_move(value, nb):
    return send(value, nb, (0, 0, 0, 1))


def z_prepare(state):
    kept, got = state
    total = kept.astype(f32) + got.astype(f32)
    return total[0::2].astype(bf16), total[1::2].astype(bf16)


def z_move(value, nb, bit):
    return send(value, nb, (1 << bit, 0, 0, 0))


def halves_first(state):
    own, got = state
    h = own.shape[2] // 2
    over_y = own[1, :, :h].astype(f32) + got[1, :, :h].astype(f32)
    over_x = own[:, 1, h:].astype(f32) + got[:, 1, h:].astype(f32)
    return over_y.astype(bf16), over_x.astype(bf16)


def halves_move(values, nb, turn):
    a, b = ((0, 0, 0, 1), (0, 1, 0, 0)) if turn else ((0, 1, 0, 0), (0, 0, 0, 1))
    return send(values[0], nb, a), send(values[1], nb, b)


def halves_second(state):
    (own, got), (from_y, from_x) = state
    h = own.shape[2] // 2
    a = own[0, :, :h].astype(f32) + got[0, :, :h].astype(f32) + from_y.astype(f32)
    b = own[:, 0, h:].astype(f32) + got[:, 0, h:].astype(f32) + from_x.astype(f32)
    return (a[0].astype(bf16), b[0].astype(bf16)), (a[1].astype(bf16), b[1].astype(bf16))


def halves_third(state):
    kept, got = state
    total = jnp.concatenate([k.astype(f32) + g.astype(f32) for k, g in zip(kept, got)], axis=0)
    return total[0::2].astype(bf16), total[1::2].astype(bf16)


def after_y(state):
    own, got, more = state
    return (own[0].astype(f32) + got[0].astype(f32) + more.astype(f32)).astype(bf16)


def direct_z(total, nb):
    result = total[:, 0].astype(f32)
    for d in range(1, nb // 4):
        result = result + send(total[:, d], nb, (d, 0, 0, 0)).astype(f32)
    return result


def at(value, index, axis):
    return lax.dynamic_index_in_dim(value, index, axis, keepdims=False)


def last_stage(state):
    kept, got = state
    return (kept.astype(f32) + got.astype(f32))[0]


def tie(*values):
    return lax.optimization_barrier(values)


def swap(value):
    return lax.ppermute(value, "seq", [(0, 1), (1, 0)])


def split_pairs(local):
    positions, _, width = local.shape
    pairs = local.reshape(positions, 2 * width)
    x = lax.axis_index("seq")
    return pairs, lax.dynamic_slice(pairs, (0, (1 - x) * width), (positions, width))


def join_pairs(mine, got):
    x = lax.axis_index("seq")
    got = got.astype(mine.dtype)
    both = jnp.concatenate([jnp.where(x == 0, mine, got), jnp.where(x == 0, got, mine)], axis=1)
    return both.reshape(mine.shape[0], 2, mine.shape[1])


def whole_sequence(pairs, got):
    x = lax.axis_index("seq")
    width = got.shape[1]
    mine = lax.dynamic_slice(pairs, (0, x * width), got.shape)
    return jnp.where(x == 0, jnp.concatenate([mine, got]), jnp.concatenate([got, mine]))


def per_device_fast(
    hidden_in,
    memory,
    src_len,
    out_grad,
    w_self_qkv,
    w_self_out,
    w_cross_q,
    w_cross_kv,
    w_cross_out,
    w_ffn_in,
    w_ffn_out,
    biases,
    ffn_bias,
    norm_gain,
    norm_shift,
):
    nb = lax.axis_size(("z", "y", "core"))
    width = hidden_in.shape[2]
    half = width // 2
    x, b = lax.axis_index("seq"), lax.axis_index(("z", "y", "core"))
    place = jnp.stack([x, b // 4, (b // 2) % 2, b % 2]).astype(jnp.int32)
    length = lax.dynamic_slice_in_dim(src_len, x, 1)

    pairs, other = split_pairs(hidden_in)
    got = swap(other)
    memory_pairs, memory_other = split_pairs(memory)
    memory_got = swap(memory_other)
    cot_pairs, cot_other = split_pairs(out_grad)
    tokens, query_self, key_self, value_self = project(
        place, pairs, got, w_self_qkv, biases, ((0, 0.125), (None, 1.0), (1, 1.0))
    )
    query_self, cot_other = tie(query_self, cot_other)
    cot_got = swap(cot_other)
    out_self, lp_self = attn_fwd(length, query_self, key_self, value_self, True)
    unit_one, scale_one, low_one, query_cross = after_self(
        out_self, tokens, w_self_out, w_cross_q, biases, norm_gain, norm_shift
    )
    sources, key_cross, value_cross = project(
        place, memory_pairs, memory_got, w_cross_kv, biases, ((None, 1.0), (4, 1.0))
    )
    out_cross, lp_cross = attn_fwd(length, query_cross, key_cross, value_cross, False)
    cotangent = whole_sequence(cot_pairs, cot_got)
    layer, grad_two, grad_mixed, sums_ffn, bias_sums, one = ffn(
        out_cross, unit_one, cotangent, w_cross_out, w_ffn_in, w_ffn_out, biases, ffn_bias[None], norm_gain, norm_shift, nb
    )
    span = layer.shape[0] // 2

    ff = w_ffn_in.shape[1]
    layer_other = lax.dynamic_slice_in_dim(layer, (1 - x) * span, span, 0)
    one, layer_other, grad_mixed = tie(one, layer_other, grad_mixed)
    one = lax.psum_scatter(one.reshape(-1, one.shape[-1]), ("seq", "z", "y", "core"), scatter_dimension=0, tiled=True)
    layer_got = swap(layer_other)
    back = partial(attn_bwd, length, query_cross, key_cross, value_cross, out_cross)
    cross_a, sums_ca = back(grad_mixed, lp_cross, False, 0, 1, 3)

    cross_a, grad_mixed, layer_got = tie(cross_a, grad_mixed, layer_got)
    cross_b, sums_cb = back(grad_mixed, lp_cross, False, 3, 1, 3)

    grad_one, branch_one, grad_mixed, gq_cross, sums_one = before_self(
        grad_two, cross_a, cross_b, unit_one, scale_one, w_cross_q, w_self_out, norm_gain
    )
    three = wide_grad(
        place,
        [(out_self, branch_one, None), (low_one, gq_cross, None), (sources, cross_a, (1, 2)), (sources, cross_b, (1, 2))],
        nb,
    )

    three, cross_a = tie(three, cross_a)
    three = core_stage(three, nb)
    spots = [((), ((0, 384),), ((width, 384),)), ((), ((384, 384),), ((width + 384, 384),))]
    other = grad_rows(place, [cross_a, cross_b], spots, w_cross_kv, None, False)

    other, three, grad_mixed = tie(other, three, grad_mixed)
    three_out = halves_first(three)
    three_out, grad_mixed = tie(three_out, grad_mixed)
    three = three, halves_move(three_out, nb, False)
    memory_back = swap(other)
    back = partial(attn_bwd, length, query_self, key_self, value_self, out_self)
    self_a, sums_sa, *four = back(
        grad_mixed, lp_self, True, 0, 3, 2, tokens, place, nb, "early", (sums_one, sums_ca, sums_cb, sums_ffn, bias_sums)
    )

    self_a, four, cross_a = tie(self_a, four, cross_a)
    four = core_stage(four, nb)
    memory_mine = grad_rows(place, [cross_a, cross_b], spots, w_cross_kv, None, True)

    four, three, grad_mixed, memory_mine = tie(four, three, grad_mixed, memory_mine)
    four_out, four = y_prepare(four)
    three_keep, three_out = halves_second(three)
    four_out, three_out, grad_mixed = tie(four_out, three_out, grad_mixed)
    four = four + (y_move(four_out, nb),)
    three = three_keep, halves_move(three_out, nb, True)
    self_b, sums_sb, *five = back(grad_mixed, lp_self, True, 1, 3, 2, tokens, place, nb)

    self_b, five, four, three, grad_mixed, memory_back = tie(self_b, five, four, three, grad_mixed, memory_back)
    five = core_stage(five, nb)
    four_keep, four_out = x_prepare(four)
    three_keep, three_out = halves_third(three)
    four_out, three_out, grad_mixed = tie(four_out, three_out, grad_mixed)
    four = four_keep, x_move(four_out, nb)
    three = three_keep, z_move(three_out, nb, 0)
    self_c, sums_sc, *six = back(grad_mixed, lp_self, True, 2, 3, 2, tokens, place, nb, "late", (sums_sa, sums_sb))

    self_c, six, five, four, three = tie(self_c, six, five, four, three)
    six = core_stage(six, nb)
    five_out, five = y_prepare(five)
    four_keep, four_out = z_prepare(four)
    three_keep, three_out = z_prepare(three)
    five_out, four_out, three_out, self_c = tie(five_out, four_out, three_out, self_c)
    five = five + (y_move(five_out, nb),)
    four = four_keep, z_move(four_out, nb, 0)
    three = three_keep, z_move(three_out, nb, 1)
    spots = [tuple(tuple((m * width + (i + s) * 128, 128) for s in (0, 3)) for m in range(3)) for i in range(3)]
    other = grad_rows(place, [self_a, self_b, self_c], spots, w_self_qkv, grad_one, False)

    other, six, grad_one = tie(other, six, grad_one)
    six_out, six = y_prepare(six)
    six_out, other, grad_one = tie(six_out, other, grad_one)
    six = six + (y_move(six_out, nb),)
    in_back = swap(other)
    mine = grad_rows(place, [self_a, self_b, self_c], spots, w_self_qkv, grad_one, True)

    mine, four, layer_got, one = tie(mine, four, layer_got, one)
    layer_out = join_pairs(lax.dynamic_slice_in_dim(layer, x * span, span, 0), layer_got)
    four_keep, four_out = z_prepare(four)
    four = four_keep, z_move(four_out, nb, 1)
    layer_out, mine, six, five, three, memory_back = tie(layer_out, mine, six, five, three, memory_back)
    both = jnp.concatenate([after_y(six), after_y(five)], axis=2)
    both, memory_back = tie(both, memory_back)
    moved = [send(both[:, d], nb, (d, 0, 0, 0)) for d in range(1, nb // 4)]
    grad_memory = join_pairs(memory_mine, memory_back)
    grad_memory, moved, one, four = tie(grad_memory, moved, one, four)
    both = both[:, 0].astype(f32)
    for value in moved:
        both = both + value.astype(f32)
    last = both[1].astype(bf16)
    last, one, in_back = tie(last, one, in_back)
    last = x_move(last, nb)
    grad_in = join_pairs(mine, in_back)
    one = one.astype(f32)
    pieces = ff // width
    grad_ffn_out = jnp.concatenate([one[:, c * half : (c + 1) * half] for c in range(pieces)], axis=0)
    grad_ffn_in = one[:, pieces * half :]
    group = last_stage(three)
    four = last_stage(four)
    last, grad_in, grad_ffn_in, grad_ffn_out, group, four = tie(last, grad_in, grad_ffn_in, grad_ffn_out, group, four)
    both = both[0] + last.astype(f32)
    unit = width // nb
    ends = unit, both.shape[0] - unit
    thirds = [s.reshape(unit, 3, 128) for s in (four[:unit], both[ends[1] :], both[: ends[0]])]
    grad_self_qkv = jnp.stack(thirds, axis=2).reshape(unit, 9 * 128)
    late = both[ends[0] : ends[0] + 6, :256].reshape(3, 2, 2, 128)
    late = at(late, x, 2).swapaxes(0, 1).reshape(2, half)
    early = lax.dynamic_slice_in_dim(four[unit:], x * 16, 16, 0)
    vectors = jnp.concatenate([late, early[:11]])
    bias_total = early[11 : 11 + bias_sums.shape[1] // width].reshape(-1)
    return (
        layer_out,
        grad_in,
        grad_memory,
        grad_self_qkv,
        group[:, :half],
        group[:, half : 2 * half],
        group[:, 2 * half :],
        grad_ffn_in[:, -half:],
        grad_ffn_in[:, :-half],
        grad_ffn_out,
        vectors[0:7],
        bias_total,
        vectors[7:10],
        vectors[10:13],
    )


def solution(mesh):
    devices = dict(mesh.shape)

    in_specs = (
        P("seq", "batch", None),
        P("seq", "batch", None),
        P("batch"),
        P("seq", "batch", None),
        P(),
        P(),
        P(),
        P(),
        P(),
        P(),
        P(),
        P(),
        P(),
        P(),
        P(),
    )
    out_specs = (
        P("seq", "batch", None),
        P("seq", "batch", None),
        P("seq", "batch", None),
        P("batch", "seq"),
        P("batch", "seq"),
        P("batch", "seq"),
        P("batch", "seq"),
        P("batch", "seq"),
        P("batch", "seq"),
        P("batch", "seq"),
        P(None, "seq"),
        P("seq"),
        P(None, "seq"),
        P(None, "seq"),
    )
    nb, ns = devices["batch"], devices["seq"]

    def program(hidden_in, *rest):
        whole = ns == 2 and hidden_in.shape[1] == 2 * nb and nb % 8 == 0 and nb & (nb - 1) == 0
        if not whole:
            general = jax.shard_map(
                per_device_general, mesh=mesh, in_specs=in_specs, out_specs=out_specs, check_vma=False
            )
            return general(hidden_in, *rest)
        parts = jax.sharding.Mesh(mesh.devices.reshape(nb // 4, 2, 2, ns), ("z", "y", "core", "seq"))
        split = lambda spec: P(*(("z", "y", "core") if axis == "batch" else axis for axis in spec))
        fast = jax.shard_map(
            per_device_fast,
            mesh=parts,
            in_specs=tuple(split(spec) for spec in in_specs),
            out_specs=tuple(split(spec) for spec in out_specs),
            check_vma=False,
        )
        return fast(hidden_in, *rest)

    return program
```

```python
import functools
from functools import partial

import jax
import jax.numpy as jnp
from jax import lax
from jax.experimental import pallas as pl
from jax.experimental.pallas import tpu as pltpu
from jax.sharding import PartitionSpec as P

H = 12


NEGATIVE = -1e30


def from_behind(value, axis, steps):
    count = lax.axis_size(axis)
    pairs = [(source, (source + steps) % count) for source in range(count)]
    return lax.ppermute(value, axis, pairs)


def shifted(block, axis, distance):
    devices = range(lax.axis_size(axis))
    route = [(i - distance, i) for i in devices if i - distance in devices]
    return lax.ppermute(block, axis, route)


def contract_rows(left, right):
    return lax.dot_general(
        left, right, (((0,), (0,)), ((), ())), preferred_element_type=jnp.float32
    )


def times_transposed(grad, weight):
    return lax.dot_general(
        grad, weight, (((1,), (1,)), ((), ())), preferred_element_type=jnp.float32
    )


def norm_forward(value, gain, shift):
    mean = jnp.mean(value, axis=-1, keepdims=True)
    centred = value - mean
    scale = lax.rsqrt(jnp.mean(centred * centred, axis=-1, keepdims=True) + 1e-05)
    unit = centred * scale
    return (unit * gain + shift, unit, scale)


def norm_backward(grad, unit, scale, gain):
    weighted = grad * gain
    inner = (
        weighted
        - jnp.mean(weighted, axis=-1, keepdims=True)
        - unit * jnp.mean(weighted * unit, axis=-1, keepdims=True)
    )
    return (scale * inner, jnp.sum(grad * unit, axis=0), jnp.sum(grad, axis=0))


def allowed_keys(query_pos, key_pos, lengths, causal):
    if causal:
        return (query_pos[:, None] >= key_pos[None, :])[None, None]
    return (key_pos[None, :] < lengths[:, None])[:, None, None, :]


def attend_forward(query, keys, values, lengths, causal, heads):
    span, batch, width = query.shape
    size = width // heads
    query_heads = query.reshape(span, batch, heads, size)
    query_pos = lax.axis_index("seq") * span + lax.iota(jnp.int32, span)

    def block(carry, key_block, value_block, first):
        previous, total, summed = carry
        rows = key_block.shape[0]
        key_pos = first + lax.iota(jnp.int32, rows)
        scores = jnp.einsum(
            "qshd,kshd->shqk",
            query_heads,
            key_block.reshape(rows, batch, heads, size),
            preferred_element_type=jnp.float32,
        )
        allowed = allowed_keys(query_pos, key_pos, lengths, causal)
        top = jnp.maximum(previous, jnp.max(jnp.where(allowed, scores, NEGATIVE), axis=-1))
        weights = jnp.where(allowed, jnp.exp(scores - top[..., None]), 0.0)
        rescale = jnp.exp(previous - top)
        total = total * rescale + jnp.sum(weights, axis=-1)
        summed = summed * rescale[..., None] + jnp.einsum(
            "shqk,kshd->shqd",
            weights.astype(jnp.bfloat16),
            value_block.reshape(rows, batch, heads, size),
            preferred_element_type=jnp.float32,
        )
        return (top, total, summed)

    def fold(carry, piece):
        key_piece, value_piece = piece
        rows = key_piece.shape[0]
        count = rows // span
        firsts = span * lax.iota(jnp.int32, count)

        def inner(state, parts):
            return (block(state, parts[0], parts[1], parts[2]), None)

        carry, unused = lax.scan(
            inner,
            carry,
            (
                key_piece.reshape(count, span, batch, width),
                value_piece.reshape(count, span, batch, width),
                firsts,
            ),
        )
        return carry

    empty = (
        jnp.full((batch, heads, span), NEGATIVE, jnp.float32),
        jnp.zeros((batch, heads, span), jnp.float32),
        jnp.zeros((batch, heads, span, size), jnp.float32),
    )
    if causal:
        top, total, summed = fold(
            empty,
            (
                lax.all_gather(keys, "seq", axis=0, tiled=True),
                lax.all_gather(values, "seq", axis=0, tiled=True),
            ),
        )
    else:
        top, total, summed = fold(
            empty,
            (
                lax.all_gather(keys, "seq", axis=0, tiled=True),
                lax.all_gather(values, "seq", axis=0, tiled=True),
            ),
        )
    mixed = summed / total[..., None]
    mixed = jnp.transpose(mixed, (2, 0, 1, 3)).reshape(span, batch, width)
    return (mixed, top + jnp.log(total))


def block_backward(
    query_heads, grad_heads, delta, logsum, key_block, value_block, allowed, batch, heads, size
):
    span = key_block.shape[0]
    width = heads * size
    key_heads = key_block.reshape(span, batch, heads, size)
    value_heads = value_block.reshape(span, batch, heads, size)
    scores = jnp.einsum(
        "qshd,kshd->shqk", query_heads, key_heads, preferred_element_type=jnp.float32
    )
    weights = jnp.where(allowed, jnp.exp(scores - logsum[..., None]), 0.0)
    grad_weights = jnp.einsum(
        "qshd,kshd->shqk", grad_heads, value_heads, preferred_element_type=jnp.float32
    )
    grad_scores = (weights * (grad_weights - delta[..., None])).astype(jnp.bfloat16)
    grad_query = jnp.einsum(
        "shqk,kshd->qshd", grad_scores, key_heads, preferred_element_type=jnp.float32
    )
    grad_keys = jnp.einsum(
        "shqk,qshd->kshd", grad_scores, query_heads, preferred_element_type=jnp.float32
    ).reshape(span, batch, width)
    grad_values = jnp.einsum(
        "shqk,qshd->kshd",
        weights.astype(jnp.bfloat16),
        grad_heads,
        preferred_element_type=jnp.float32,
    ).reshape(span, batch, width)
    return (grad_query, grad_keys, grad_values)


def attend_backward(query, keys, values, mixed, grad_mixed, logsum, lengths, causal, heads):
    span, batch, width = query.shape
    size = width // heads
    query_heads = query.reshape(span, batch, heads, size)
    grad_heads = grad_mixed.reshape(span, batch, heads, size)
    delta = jnp.sum(
        grad_heads.astype(jnp.float32) * mixed.reshape(span, batch, heads, size), axis=-1
    )
    delta = jnp.transpose(delta, (1, 2, 0))
    devices = lax.axis_size("seq")
    place = lax.axis_index("seq")
    query_pos = place * span + lax.iota(jnp.int32, span)
    grad_query = jnp.zeros((span, batch, heads, size), jnp.float32)
    grad_keys = jnp.zeros((span, batch, width), jnp.float32)
    grad_values = jnp.zeros((span, batch, width), jnp.float32)
    key_block, value_block = (keys, values)
    for step in range(devices):
        owner = (place - step + devices) % devices
        key_pos = owner * span + lax.iota(jnp.int32, span)
        allowed = allowed_keys(query_pos, key_pos, lengths, causal)
        part_query, part_keys, part_values = block_backward(
            query_heads,
            grad_heads,
            delta,
            logsum,
            key_block,
            value_block,
            allowed,
            batch,
            heads,
            size,
        )
        grad_query = grad_query + part_query
        grad_keys = grad_keys + part_keys
        grad_values = grad_values + part_values
        if causal:
            grad_keys, grad_values = (
                from_behind(grad_keys.astype(jnp.bfloat16), "seq", 1).astype(grad_keys.dtype),
                from_behind(grad_values.astype(jnp.bfloat16), "seq", 1).astype(grad_values.dtype),
            )
        else:
            grad_keys, grad_values = (
                from_behind(grad_keys.astype(jnp.bfloat16), "seq", 1).astype(grad_keys.dtype),
                from_behind(grad_values.astype(jnp.bfloat16), "seq", 1).astype(grad_values.dtype),
            )
        if step + 1 < devices:
            if causal:
                key_block, value_block = shifted((key_block, value_block), "seq", 1)
            else:
                key_block, value_block = from_behind((key_block, value_block), "seq", 1)
    return (grad_query.reshape(span, batch, width), grad_keys, grad_values)


def per_device_general(
    hidden_in,
    memory,
    src_len,
    out_grad,
    w_self_qkv,
    w_self_out,
    w_cross_q,
    w_cross_kv,
    w_cross_out,
    w_ffn_in,
    w_ffn_out,
    biases,
    ffn_bias,
    norm_gain,
    norm_shift,
):
    span, batch, width = hidden_in.shape
    heads = H
    rows = span * batch
    layout = (span, batch, width)
    tokens = hidden_in.reshape(rows, width)
    sources = memory.reshape(rows, width)
    joined = jnp.dot(tokens, w_self_qkv, preferred_element_type=jnp.float32)
    query_self = ((joined[:, :width] + biases[0]) * 0.125).astype(jnp.bfloat16)
    key_self = joined[:, width : 2 * width].astype(jnp.bfloat16)
    value_self = (joined[:, 2 * width :] + biases[1]).astype(jnp.bfloat16)
    mixed_self, logsum_self = attend_forward(
        query_self.reshape(layout),
        key_self.reshape(layout),
        value_self.reshape(layout),
        src_len,
        True,
        heads,
    )
    out_self = mixed_self.reshape(rows, width).astype(jnp.bfloat16)
    resid_one = (
        tokens.astype(jnp.float32)
        + jnp.dot(out_self, w_self_out, preferred_element_type=jnp.float32)
        + biases[2]
    )
    normed_one, unit_one, scale_one = norm_forward(resid_one, norm_gain[0], norm_shift[0])
    normed_one_low = normed_one.astype(jnp.bfloat16)
    query_cross = (
        (jnp.dot(normed_one_low, w_cross_q, preferred_element_type=jnp.float32) + biases[3]) * 0.125
    ).astype(jnp.bfloat16)
    pair = jnp.dot(sources, w_cross_kv, preferred_element_type=jnp.float32)
    key_cross = pair[:, :width].astype(jnp.bfloat16)
    value_cross = (pair[:, width:] + biases[4]).astype(jnp.bfloat16)
    mixed_cross, logsum_cross = attend_forward(
        query_cross.reshape(layout),
        key_cross.reshape(layout),
        value_cross.reshape(layout),
        src_len,
        False,
        heads,
    )
    out_cross = mixed_cross.reshape(rows, width).astype(jnp.bfloat16)
    resid_two = (
        normed_one + jnp.dot(out_cross, w_cross_out, preferred_element_type=jnp.float32) + biases[5]
    )
    normed_two, unit_two, scale_two = norm_forward(resid_two, norm_gain[1], norm_shift[1])
    normed_two_low = normed_two.astype(jnp.bfloat16)
    inner = jnp.dot(normed_two_low, w_ffn_in, preferred_element_type=jnp.float32) + ffn_bias
    active = jax.nn.gelu(inner, approximate=False).astype(jnp.bfloat16)
    resid_three = (
        normed_two + jnp.dot(active, w_ffn_out, preferred_element_type=jnp.float32) + biases[6]
    )
    result, unit_three, scale_three = norm_forward(resid_three, norm_gain[2], norm_shift[2])
    layer_out = result.astype(jnp.bfloat16).reshape(layout)
    grad_three, gain_three, shift_three = norm_backward(
        out_grad.reshape(rows, width).astype(jnp.float32), unit_three, scale_three, norm_gain[2]
    )
    branch_three = grad_three.astype(jnp.bfloat16)
    hidden_pre, hidden_act = (inner, active)
    grad_ffn_out = contract_rows(hidden_act, branch_three)
    grad_act = times_transposed(branch_three, w_ffn_out)
    unused, pull = jax.vjp(partial(jax.nn.gelu, approximate=False), hidden_pre)
    grad_pre = pull(grad_act)[0].astype(jnp.bfloat16)
    grad_ffn_in = contract_rows(normed_two_low, grad_pre)
    grad_normed_two = grad_three + times_transposed(grad_pre, w_ffn_in)
    grad_two, gain_two, shift_two = norm_backward(
        grad_normed_two, unit_two, scale_two, norm_gain[1]
    )
    branch_two = grad_two.astype(jnp.bfloat16)
    grad_cross_out = contract_rows(out_cross, branch_two)
    grad_mixed_cross = times_transposed(branch_two, w_cross_out).astype(jnp.bfloat16)
    raw_query, grad_keys, grad_values = attend_backward(
        query_cross.reshape(layout),
        key_cross.reshape(layout),
        value_cross.reshape(layout),
        mixed_cross,
        grad_mixed_cross.reshape(layout),
        logsum_cross,
        src_len,
        False,
        heads,
    )
    grad_query_cross = (raw_query.reshape(rows, width) * 0.125).astype(jnp.bfloat16)
    grad_pair = jnp.concatenate(
        [
            grad_keys.reshape(rows, width).astype(jnp.bfloat16),
            grad_values.reshape(rows, width).astype(jnp.bfloat16),
        ],
        axis=1,
    )
    grad_cross_q = contract_rows(normed_one_low, grad_query_cross)
    grad_cross_kv = contract_rows(sources, grad_pair)
    grad_memory = times_transposed(grad_pair, w_cross_kv).reshape(layout)
    grad_normed_one = grad_two + times_transposed(grad_query_cross, w_cross_q)
    grad_one, gain_one, shift_one = norm_backward(
        grad_normed_one, unit_one, scale_one, norm_gain[0]
    )
    branch_one = grad_one.astype(jnp.bfloat16)
    grad_self_out = contract_rows(out_self, branch_one)
    grad_mixed_self = times_transposed(branch_one, w_self_out).astype(jnp.bfloat16)
    raw_query, grad_keys, grad_values = attend_backward(
        query_self.reshape(layout),
        key_self.reshape(layout),
        value_self.reshape(layout),
        mixed_self,
        grad_mixed_self.reshape(layout),
        logsum_self,
        src_len,
        True,
        heads,
    )
    grad_joined = jnp.concatenate(
        [
            (raw_query.reshape(rows, width) * 0.125).astype(jnp.bfloat16),
            grad_keys.reshape(rows, width).astype(jnp.bfloat16),
            grad_values.reshape(rows, width).astype(jnp.bfloat16),
        ],
        axis=1,
    )
    grad_self_qkv = contract_rows(tokens, grad_joined)
    grad_in = (grad_one + times_transposed(grad_joined, w_self_qkv)).reshape(layout)
    vector_terms = jnp.stack(
        [
            jnp.sum(grad_joined[:, :width].astype(jnp.float32), axis=0),
            jnp.sum(grad_joined[:, 2 * width :].astype(jnp.float32), axis=0),
            jnp.sum(grad_one, axis=0),
            jnp.sum(grad_query_cross.astype(jnp.float32), axis=0),
            jnp.sum(grad_pair[:, width:].astype(jnp.float32), axis=0),
            jnp.sum(grad_two, axis=0),
            jnp.sum(grad_three, axis=0),
            gain_one,
            gain_two,
            gain_three,
            shift_one,
            shift_two,
            shift_three,
        ]
    )
    bias_terms = jnp.sum(grad_pre.astype(jnp.float32), axis=0)[None]
    (
        grad_self_qkv,
        grad_self_out,
        grad_cross_q,
        grad_cross_kv,
        grad_cross_out,
        grad_ffn_in,
        grad_ffn_out,
        vector_terms,
        bias_terms,
    ) = (
        lax.psum_scatter(
            grad_self_qkv.astype(jnp.bfloat16), "seq", scatter_dimension=1, tiled=True
        ).astype(jnp.float32),
        lax.psum_scatter(
            grad_self_out.astype(jnp.bfloat16), "seq", scatter_dimension=1, tiled=True
        ).astype(jnp.float32),
        lax.psum_scatter(
            grad_cross_q.astype(jnp.bfloat16), "seq", scatter_dimension=1, tiled=True
        ).astype(jnp.float32),
        lax.psum_scatter(
            grad_cross_kv.astype(jnp.bfloat16), "seq", scatter_dimension=1, tiled=True
        ).astype(jnp.float32),
        lax.psum_scatter(
            grad_cross_out.astype(jnp.bfloat16), "seq", scatter_dimension=1, tiled=True
        ).astype(jnp.float32),
        lax.psum_scatter(
            grad_ffn_in.astype(jnp.bfloat16), "seq", scatter_dimension=1, tiled=True
        ).astype(jnp.float32),
        lax.psum_scatter(
            grad_ffn_out.astype(jnp.bfloat16), "seq", scatter_dimension=1, tiled=True
        ).astype(jnp.float32),
        lax.psum_scatter(
            vector_terms.astype(jnp.bfloat16), "seq", scatter_dimension=1, tiled=True
        ).astype(jnp.float32),
        lax.psum_scatter(
            bias_terms.astype(jnp.bfloat16), "seq", scatter_dimension=1, tiled=True
        ).astype(jnp.float32),
    )
    (
        grad_self_qkv,
        grad_self_out,
        grad_cross_q,
        grad_cross_kv,
        grad_cross_out,
        grad_ffn_in,
        grad_ffn_out,
    ) = (
        lax.psum_scatter(
            grad_self_qkv.astype(jnp.bfloat16), "batch", scatter_dimension=0, tiled=True
        ).astype(jnp.float32),
        lax.psum_scatter(
            grad_self_out.astype(jnp.bfloat16), "batch", scatter_dimension=0, tiled=True
        ).astype(jnp.float32),
        lax.psum_scatter(
            grad_cross_q.astype(jnp.bfloat16), "batch", scatter_dimension=0, tiled=True
        ).astype(jnp.float32),
        lax.psum_scatter(
            grad_cross_kv.astype(jnp.bfloat16), "batch", scatter_dimension=0, tiled=True
        ).astype(jnp.float32),
        lax.psum_scatter(
            grad_cross_out.astype(jnp.bfloat16), "batch", scatter_dimension=0, tiled=True
        ).astype(jnp.float32),
        lax.psum_scatter(
            grad_ffn_in.astype(jnp.bfloat16), "batch", scatter_dimension=0, tiled=True
        ).astype(jnp.float32),
        lax.psum_scatter(
            grad_ffn_out.astype(jnp.bfloat16), "batch", scatter_dimension=0, tiled=True
        ).astype(jnp.float32),
    )
    vector_terms, bias_terms = lax.psum((vector_terms, bias_terms), "batch")
    return (
        layer_out,
        grad_in,
        grad_memory,
        grad_self_qkv,
        grad_self_out,
        grad_cross_q,
        grad_cross_kv,
        grad_cross_out,
        grad_ffn_in,
        grad_ffn_out,
        vector_terms[0:7],
        bias_terms[0],
        vector_terms[7:10],
        vector_terms[10:13],
    )


LOG2E = 1.4426950408889634
NN = (((1,), (0,)), ((), ()))
NT = (((1,), (1,)), ((), ()))
HD = 64
BIG = -1e30
f32, bf16 = jnp.float32, jnp.bfloat16

def dot(a, b, dims=NN):
    return lax.dot_general(a, b, dims, preferred_element_type=f32)

def lanes(shape):
    return lax.broadcasted_iota(jnp.int32, shape, len(shape) - 1)

def swap_halves(x):
    return jnp.concatenate([x[:, HD:], x[:, :HD]], axis=1)

def fwd_kernel(len_ref, q_ref, k_ref, v_ref, o_ref, lp_ref, acc_ref, *, causal, heads, qb, ahead):
    p = pl.program_id(0)
    n = q_ref.shape[0]
    nk = k_ref.shape[0]
    scaled = q_ref[...].astype(f32) * LOG2E
    hi = scaled.astype(bf16)
    lo = (scaled - hi.astype(f32)).astype(bf16)
    first = lanes((n, 128)) < HD
    hi_s, lo_s = swap_halves(hi), swap_halves(lo)
    q_aug = (jnp.where(first, hi, lo_s), jnp.where(first, hi_s, lo))
    kk = k_ref[...]
    k_s = swap_halves(kk)
    k_aug = [jnp.where(first, kk, k_s), jnp.where(first, k_s, kk)]
    if not causal:
        length = len_ref[0]
        row = lax.broadcasted_iota(jnp.int32, (nk, 128), 0)
        extra = jnp.where((row >= length) & (lanes((nk, 128)) == 0), BIG, 0.0).astype(bf16)
        k_aug = [jnp.concatenate([x, extra], axis=1) for x in k_aug]
        one = (lanes((n, 128)) == 0).astype(bf16)
        q_aug = [jnp.concatenate([x, one], axis=1) for x in q_aug]
    vt = jnp.transpose(v_ref[...])
    ones = jnp.ones((16, nk), bf16)
    va = [jnp.concatenate([vt[h * HD:(h + 1) * HD], ones], axis=0) for h in range(2)]

    def scores(c, h):
        top_k = (c + 1) * qb if causal else nk
        s = dot(k_aug[h][:top_k], q_aug[h][c * qb:(c + 1) * qb], NT)
        if causal:
            r = lax.broadcasted_iota(jnp.int32, (qb, qb), 0)
            d = jnp.where(r <= lanes((qb, qb)), s[c * qb:], BIG)
            s = jnp.concatenate([s[:c * qb], d], axis=0) if c else d
        return s

    steps = [(c, h) for c in range(n // qb) for h in range(2)]
    queue = [scores(*x) for x in steps[:ahead]]
    parts = []
    for i, (c, h) in enumerate(steps):
        if i + ahead < len(steps):
            queue.append(scores(*steps[i + ahead]))
        s = queue.pop(0)
        m = jnp.max(s, axis=0, keepdims=True)
        pt = jnp.exp2(s - m).astype(bf16)
        ot = dot(va[h][:, :s.shape[0]], pt)
        l = ot[HD:HD + 1]
        parts.append(ot[:HD] * (1.0 / l))
        acc_ref[pl.ds(2 * p + h, 1), c * qb:(c + 1) * qb] = m + jnp.log2(l)
        if h == 1:
            o_ref[c * qb:(c + 1) * qb, :] = jnp.transpose(jnp.concatenate(parts, axis=0)).astype(bf16)
            parts = []

    @pl.when(p == pl.num_programs(0) - 1)
    def _():
        rows = acc_ref[...]
        wide = jnp.concatenate([rows, jnp.zeros((128 - rows.shape[0], n), f32)], axis=0)
        cols = jnp.transpose(wide)
        a = cols.astype(bf16)
        cols = cols - a.astype(f32)
        b = cols.astype(bf16)
        c = (cols - b.astype(f32)).astype(bf16)
        lane = lanes((n, 128))
        sh = lambda x, k: jnp.concatenate([jnp.zeros((n, k), bf16), x[:, :128 - k]], axis=1)
        out = jnp.where(lane < 16, a, jnp.where(lane < 32, sh(b, 16), jnp.where(lane < 48, sh(c, 32), jnp.where(lane == 127, 1.0, 0.0).astype(bf16))))
        lp_ref[...] = out

def attn_fwd(length, q, k, v, causal, qb=256, ahead=4):
    n, d = q.shape
    blk = lambda r: pl.BlockSpec((r, 128), lambda p, l: (0, p))
    return pl.pallas_call(
        functools.partial(fwd_kernel, causal=causal, heads=d // HD, qb=qb, ahead=ahead),
        grid_spec=pltpu.PrefetchScalarGridSpec(
            num_scalar_prefetch=1, grid=(d // 128,),
            in_specs=[blk(n), blk(k.shape[0]), blk(k.shape[0])],
            out_specs=[blk(n), pl.BlockSpec((n, 128), lambda p, l: (0, 0))],
            scratch_shapes=[pltpu.VMEM((16, n), f32)]),
        out_shape=[pltpu.HBM((n, d), bf16), pltpu.HBM((n, 128), bf16)],
        compiler_params=params(40),
        cost_estimate=cost((n + 256) * n * 1024 // (2 if causal else 1) * (d // HD), 8 * n * d, n * n * d // HD),
        name="attn_fwd",
    )(length, *hbm(q, k, v))

def side_rows(kind, refs, own):
    if kind == "early":
        one, cross_a, cross_b, ffn, bias = refs
        both = lambda r: jnp.concatenate([cross_a[r : r + 1, :], cross_b[r : r + 1, :]], axis=1)
        rows = [one[2:3, :], both(0), both(1), ffn[5:6, :], ffn[2:3, :], one[0:1, :], ffn[3:4, :], ffn[0:1, :], one[1:2, :], ffn[4:5, :], ffn[1:2, :]]
        half = rows[0].shape[1] // 2
        wide = bias.shape[1] // 2
        sides = []
        for x in range(2):
            sides += [r[:, x * half : (x + 1) * half] for r in rows]
            sides += [bias[0:1, x * wide + c * half : x * wide + (c + 1) * half] for c in range(wide // half)]
            sides += [jnp.zeros((1, half), f32)] * (16 - len(rows) - wide // half)
        return jnp.concatenate(sides, axis=0).astype(bf16)
    rows = [refs[0][0:2, :], refs[1][0:2, :], own[0:2, :], jnp.zeros((10, own.shape[1]), f32)]
    rows = jnp.concatenate(rows, axis=0)
    return jnp.concatenate([rows, jnp.zeros((16, 128), f32)], axis=1).astype(bf16)


def bwd_kernel(len_ref, q_ref, k_ref, v_ref, o_ref, g_ref, lp_ref, *rest, causal, qb, first_pair, stride, unit, kind):
    if unit:
        place, tok_ref, *side, out_ref, sums_ref, send_ref, own_ref = rest
    else:
        out_ref, sums_ref = rest
    p = pl.program_id(0) * stride + first_pair
    n, nk = q_ref.shape[0], k_ref.shape[0]
    first = lanes((n, 128)) < HD
    q = q_ref[...]
    scaled = q.astype(f32) * LOG2E
    hi = scaled.astype(bf16)
    lo = (scaled - hi.astype(f32)).astype(bf16)
    hi_s, lo_s = swap_halves(hi), swap_halves(lo)
    lp = lp_ref[...]
    q_aug = [jnp.concatenate([x, lp], axis=1) for x in (jnp.where(first, hi, lo_s), jnp.where(first, hi_s, lo))]
    kk = k_ref[...]
    k_s = swap_halves(kk)
    v = v_ref[...]
    lane = lanes((nk, 128))
    g = g_ref[...]
    zero = jnp.zeros((), bf16)
    go = g.astype(f32) * o_ref[...].astype(f32)
    go_hi = go.astype(bf16)
    go_lo = (go - go_hi.astype(f32)).astype(bf16)
    br = lax.broadcasted_iota(jnp.int32, (128, 128), 0)
    bl = lanes((128, 128))
    pick = jnp.where(((bl < 3) & (br < HD)) | ((bl >= 3) & (bl < 6) & (br >= HD)), 1.0, 0.0).astype(bf16)
    dl = dot(go_hi, pick) + dot(go_lo, pick)
    da = dl.astype(bf16)
    rest = dl - da.astype(f32)
    db = rest.astype(bf16)
    dc = (rest - db.astype(f32)).astype(bf16)
    part = lanes((n, 128))
    part = jnp.where(part >= 3, part - 3, part)
    dpack = jnp.where(part == 0, da, jnp.where(part == 1, db, dc))
    g_aug = jnp.concatenate([g, dpack], axis=1)
    qt = jnp.transpose(q)
    gt = jnp.transpose(g)
    minus = jnp.full((), -1.0, bf16)
    row = lax.broadcasted_iota(jnp.int32, (nk, 128), 0)
    k_augs, v_augs = [], []
    for h in range(2):
        head = 2 * p + h
        sel = jnp.where((lane < 48) & ((lane & 15) == head), -1.0, 0.0)
        if not causal:
            sel = jnp.where((lane == 127) & (row >= len_ref[0]), BIG, sel)
        k_augs.append(jnp.concatenate([jnp.where(first, kk, k_s) if h == 0 else jnp.where(first, k_s, kk), sel.astype(bf16)], axis=1))
        dsel = jnp.where((lane >= 3 * h) & (lane < 3 * h + 3), -1.0, 0.0).astype(bf16)
        v_m = jnp.where(first, v, zero) if h == 0 else jnp.where(first, zero, v)
        v_augs.append(jnp.concatenate([v_m, dsel], axis=1))

    def products(c, h):
        rows = slice(c * qb, (c + 1) * qb)
        top_k = (c + 1) * qb if causal else nk
        return dot(q_aug[h][rows], k_augs[h][:top_k], NT), dot(g_aug[rows], v_augs[h][:top_k], NT)

    def weigh(c, s, dp):
        w = jnp.exp2(s)
        if causal:
            r = lax.broadcasted_iota(jnp.int32, (qb, qb), 0)
            dg = jnp.where(r >= lanes((qb, qb)), w[:, c * qb:], 0.0)
            w = jnp.concatenate([w[:, :c * qb], dg], axis=1) if c else dg
        return w.astype(bf16), (w * dp).astype(bf16)

    def collect(c, h, wb, ds):
        rows = slice(c * qb, (c + 1) * qb)
        top_k = ds.shape[1]
        grow = lambda total, part: part + total if top_k == nk else jnp.concatenate([total[:, :top_k] + part, total[:, top_k:]], axis=1)
        dvts[h] = grow(dvts[h], dot(gt[h * HD:(h + 1) * HD, rows], wb))
        dkts[h] = grow(dkts[h], dot(qt[h * HD:(h + 1) * HD, rows], ds))
        dq_parts[h][c] = dot(ds, kk[:top_k])

    dkts = [jnp.zeros((HD, nk), f32)] * 2
    dvts = [jnp.zeros((HD, nk), f32)] * 2
    dq_parts = [{}, {}]
    steps = [(c, h) for h in range(2) for c in range(n // qb)]
    ahead = products(*steps[0])
    for i, (c, h) in enumerate(steps):
        s, dp = ahead
        if i + 1 < len(steps):
            ahead = products(*steps[i + 1])
        collect(c, h, *weigh(c, s, dp))
    sums = jnp.zeros((1, 128), f32)
    dqs = []
    for c in range(n // qb):
        rows = slice(c * qb, (c + 1) * qb)
        fl = lanes((qb, 128)) < HD
        dq = (jnp.where(fl, dq_parts[0][c], dq_parts[1][c]) * 0.125).astype(bf16)
        dqs.append(dq)
        sums = sums + jnp.sum(dq.astype(f32), axis=0, keepdims=True)
    dk = jnp.transpose(jnp.concatenate(dkts, axis=0)).astype(bf16)
    dv = jnp.transpose(jnp.concatenate(dvts, axis=0)).astype(bf16)
    v_sums = jnp.sum(dv.astype(f32), axis=0, keepdims=True)
    grads = (jnp.concatenate(dqs, axis=0), dk, dv)
    if not unit:
        sums_ref[...] = jnp.concatenate([sums, v_sums, jnp.zeros((6, 128), f32)], axis=0)
        for m, part in enumerate(grads):
            out_ref[m] = part
        return
    for at in range(2):
        @pl.when(pl.program_id(0) == at)
        def _(at=at):
            cols = slice(at * 128, (at + 1) * 128)
            sums_ref[:, cols] = jnp.concatenate([sums, v_sums, jnp.zeros((6, 128), f32)], axis=0)
            for m, part in enumerate(grads):
                out_ref[m, :, cols] = part

    @pl.when(pl.program_id(0) == 1)
    def _():
        joined = jnp.concatenate([out_ref[0], out_ref[1], out_ref[2]], axis=1)
        store_units(place, dot(tok_ref[...], joined, TN).astype(bf16), unit, send_ref, own_ref)
        if kind:
            rows = side_rows(kind, side, sums_ref[...])
            for ref in (send_ref, own_ref):
                for y in range(2):
                    for x in range(2):
                        for z in range(ref.shape[2]):
                            ref[y, x, z, unit:] = rows


def attn_bwd(length, q, k, v, o, g, lp, causal, first, stride, count, tokens=None, place=None, nb=0, kind="", side=(), qb=256):
    n, d = q.shape
    blk = pl.BlockSpec((n, 128), lambda p, l: (0, first + stride * p))
    ins = [blk] * 5 + [pl.BlockSpec((n, 128), lambda p, l: (0, 0))]
    outs = [pl.BlockSpec((3, n, 128), lambda p, l: (0, 0, p)), pl.BlockSpec((8, 128), lambda p, l: (0, p))]
    shapes = [pltpu.HBM((3, n, count * 128), bf16), pltpu.HBM((8, count * 128), f32)]
    args = hbm(q, k, v, o, g, lp)
    unit = 0
    if tokens is not None:
        unit = d // nb
        rows = unit + {"early": 32, "late": 16, "": 0}[kind]
        ins += [pl.BlockSpec(memory_space=pltpu.SMEM), pl.BlockSpec((n, d), lambda p, l: (0, 0))]
        ins += [pl.BlockSpec(s.shape, lambda p, l: (0, 0)) for s in side]
        args += [place] + hbm(tokens, *side)
        outs = [pl.BlockSpec((3, n, 256), lambda p, l: (0, 0, 0)), pl.BlockSpec((8, 256), lambda p, l: (0, 0))]
        outs += [pl.BlockSpec((2, 2, nb // 4, rows, 384), lambda p, l: (0, 0, 0, 0, 0))] * 2
        shapes += [pltpu.HBM((2, 2, nb // 4, rows, 384), bf16)] * 2
    return pl.pallas_call(
        functools.partial(bwd_kernel, causal=causal, qb=qb, first_pair=first, stride=stride, unit=unit, kind=kind),
        grid_spec=pltpu.PrefetchScalarGridSpec(
            num_scalar_prefetch=1, grid=(count,), in_specs=ins, out_specs=outs),
        out_shape=shapes,
        compiler_params=params(40),
        cost_estimate=cost((n + 256) * n * 2560 // (2 if causal else 1) * count * 2, 16 * n * count * 128, 2 * n * n * count),
        name="attn_bwd",
    )(length, *args)


TN = (((0,), (0,)), ((), ()))


def cost(flops, moved, exps=0):
    return pl.CostEstimate(flops=int(flops), bytes_accessed=int(moved), transcendentals=int(exps))


def params(mib):
    return pltpu.CompilerParams(vmem_limit_bytes=mib * 2**20)


def hbm(*values):
    return [pltpu.with_memory_space_constraint(v, pltpu.HBM) for v in values]


def whole():
    return pl.BlockSpec(memory_space=pltpu.VMEM)


def fixed(shape):
    return pl.BlockSpec(shape, lambda *_: (0,) * len(shape), pipeline_mode=pl.Buffered(1))


def spread_rows(block):
    return lambda i, *_: (i, 0)


def project_kernel(place, mine, got, weight, biases, *outs, step, plan):
    i = pl.program_id(0)
    x = jnp.where(i // step == place[0], mine[...], got[...])
    outs[0][...] = x
    joined = dot(x, weight[...])
    width = x.shape[1]
    for n, (bias, scale) in enumerate(plan):
        part = joined[:, n * width : (n + 1) * width]
        if bias is not None:
            part = part + biases[bias : bias + 1, :]
        if scale != 1.0:
            part = part * scale
        outs[n + 1][...] = part.astype(bf16)


def project(place, pairs, got, weight, biases, plan, rows=256):
    half, width = got.shape
    step = half // rows
    cols = weight.shape[1]
    block = pl.BlockSpec((rows, width), lambda i, p: (i, 0))
    return pl.pallas_call(
        functools.partial(project_kernel, step=step, plan=plan),
        grid_spec=pltpu.PrefetchScalarGridSpec(
            num_scalar_prefetch=1,
            grid=(2 * step,),
            in_specs=[
                pl.BlockSpec((rows, width), lambda i, p: (i % step, p[0])),
                pl.BlockSpec((rows, width), lambda i, p: (i % step, 0)),
                whole(),
                whole(),
            ],
            out_specs=[block] * (1 + len(plan)),
        ),
        out_shape=[pltpu.HBM((2 * half, width), bf16)] * (1 + len(plan)),
        compiler_params=params(32),
        cost_estimate=cost(4 * half * width * cols, 2 * width * cols + 12 * half * width),
        name="project",
    )(place, *hbm(pairs, got), weight, biases)


def norm_unit(value):
    mean = jnp.mean(value, axis=-1, keepdims=True)
    centred = value - mean
    scale = lax.rsqrt(jnp.mean(centred * centred, axis=-1, keepdims=True) + 1e-05)
    return centred * scale, scale


def norm_back(grad, unit, scale, gain):
    weighted = grad * gain
    return scale * (
        weighted
        - jnp.mean(weighted, axis=-1, keepdims=True)
        - unit * jnp.mean(weighted * unit, axis=-1, keepdims=True)
    )


def row_sum(value):
    return jnp.sum(value, axis=0, keepdims=True)


def after_self_kernel(o, tok, w_out, w_q, biases, gain, shift, unit_ref, scale_ref, low_ref, q_ref):
    resid = tok[...].astype(f32) + dot(o[...], w_out[...]) + biases[2:3, :]
    unit, scale = norm_unit(resid)
    unit_ref[...] = unit
    scale_ref[...] = jnp.broadcast_to(scale, scale_ref.shape)
    low_ = (unit * gain[0:1, :] + shift[0:1, :]).astype(bf16)
    low_ref[...] = low_
    q_ref[...] = ((dot(low_, w_q[...]) + biases[3:4, :]) * 0.125).astype(bf16)


def after_self(o, tok, w_out, w_q, biases, gain, shift, rows=256):
    n, d = o.shape
    block = pl.BlockSpec((rows, d), lambda i: (i, 0))
    return pl.pallas_call(
        after_self_kernel,
        grid=(n // rows,),
        in_specs=[block, block, whole(), whole()] + [whole()] * 3,
        out_specs=[block, pl.BlockSpec((rows, 128), lambda i: (i, 0)), block, block],
        out_shape=[
            pltpu.HBM((n, d), f32),
            pltpu.HBM((n, 128), f32),
            pltpu.HBM((n, d), bf16),
            pltpu.HBM((n, d), bf16),
        ],
        compiler_params=params(32),
        cost_estimate=cost(4 * n * d * d, 4 * d * d + 12 * n * d),
        name="after_self",
    )(*hbm(o, tok), w_out, w_q, biases, gain, shift)


RATE = 0.3275911 * 0.7071067811865476
TAIL = tuple(0.5 * c for c in (0.254829592, -0.284496736, 1.421413741, -1.453152027, 1.061405429))
DENSITY = 0.3989422804014327


def gelu_pair(v):
    size = jnp.abs(v)
    base = 1.0 + RATE * size
    t = pl.reciprocal(base, approx=True)
    t = t * (2.0 - base * t)
    poly = TAIL[4]
    for c in TAIL[3::-1]:
        poly = c + t * poly
    bell = jnp.exp2((v * v) * (-0.5 * LOG2E))
    tail = t * poly * bell
    below = jnp.where(v >= 0.0, 1.0 - tail, tail)
    return v * below, below + v * (DENSITY * bell)


def ffn_kernel(
    o, unit_one, cot, w_co, w_in, w_out, biases, ffn_bias, gain, shift,
    layer_ref, g2_ref, gm_ref, sums_ref, fsum_ref, grads_ref,
    slope, act_all, pre_all, b3_all, b2_all, low_turned, o_turned, *, blocks, nz,
):
    i = pl.program_id(0)
    rows, d = o.shape
    n_chunks, _, chunk = act_all.shape

    @pl.when(i == 0)
    def _():
        sums_ref[...] = jnp.zeros_like(sums_ref)
        fsum_ref[...] = jnp.zeros_like(fsum_ref)

    @pl.when(i < blocks)
    def _():
        here = pl.ds(pl.multiple_of(i * rows, rows), rows)
        o_turned[:, here] = jnp.transpose(o[...])
        normed_one = unit_one[...] * gain[0:1, :] + shift[0:1, :]
        resid = normed_one + dot(o[...], w_co[...]) + biases[5:6, :]
        unit_two, scale_two = norm_unit(resid)
        normed_two = unit_two * gain[1:2, :] + shift[1:2, :]
        low_two = normed_two.astype(bf16)
        low_turned[:, here] = jnp.transpose(low_two)

        def inner(j):
            at = slice(j * chunk, (j + 1) * chunk)
            return dot(low_two, w_in[:, at]) + ffn_bias[0:1, at]

        total = normed_two + biases[6:7, :]
        ahead = inner(0)
        for j in range(n_chunks):
            v = ahead
            if j + 1 < n_chunks:
                ahead = inner(j + 1)
            act, grad = gelu_pair(v)
            act = act.astype(bf16)
            act_all[j, here, :] = act
            slope[:, j * chunk : (j + 1) * chunk] = grad
            total = total + dot(act, w_out[j * chunk : (j + 1) * chunk, :])
        unit, scale = norm_unit(total)
        layer_ref[...] = (unit * gain[2:3, :] + shift[2:3, :]).astype(bf16)
        g = cot[...].astype(f32)
        grad_three = norm_back(g, unit, scale, gain[2:3, :])
        branch = grad_three.astype(bf16)
        b3_all[here, :] = branch
        sums_ref[0:1, :] += row_sum(g * unit)
        sums_ref[1:2, :] += row_sum(g)
        sums_ref[2:3, :] += row_sum(grad_three)

        def back(j):
            return dot(branch, w_out[j * chunk : (j + 1) * chunk, :], NT)

        total = grad_three
        ahead = back(0)
        for j in range(n_chunks):
            v = ahead
            if j + 1 < n_chunks:
                ahead = back(j + 1)
            at = slice(j * chunk, (j + 1) * chunk)
            pre = (v * slope[:, at]).astype(bf16)
            pre_all[j, here, :] = pre
            fsum_ref[0:1, at] += row_sum(pre.astype(f32))
            total = total + dot(pre, w_in[:, at], NT)
        grad_two = norm_back(total, unit_two, scale_two, gain[1:2, :])
        g2_ref[...] = grad_two
        branch = grad_two.astype(bf16)
        b2_all[here, :] = branch
        sums_ref[3:4, :] += row_sum(total * unit_two)
        sums_ref[4:5, :] += row_sum(total)
        sums_ref[5:6, :] += row_sum(grad_two)
        gm_ref[...] = dot(branch, w_co[...], NT).astype(bf16)

    @pl.when(i >= blocks)
    def _():
        z = i - blocks
        half = d // 2
        count = grads_ref.shape[1]
        unit = grads_ref.shape[2]
        value = dot(act_all[z], b3_all[...], TN).astype(bf16)
        pieces = value.shape[0] // (count * unit)
        for u in range(count):
            for c in range(pieces):
                top = (u * pieces + c) * unit
                for x in range(2):
                    grads_ref[x, u, :, c * half : (c + 1) * half] = value[top : top + unit, x * half : (x + 1) * half]
        start = pieces * half
        own = pl.ds(pl.multiple_of(z * count * unit, count * unit), count * unit)
        a = low_turned[own, :]
        for j in range(n_chunks):
            value = dot(a, pre_all[j]).astype(bf16)
            x, left = divmod(j, n_chunks // 2)
            for u in range(count):
                grads_ref[x, u, :, start + left * chunk : start + (left + 1) * chunk] = value[u * unit : (u + 1) * unit]
        start += n_chunks // 2 * chunk
        value = dot(o_turned[own, :], b2_all[...]).astype(bf16)
        for u in range(count):
            for x in range(2):
                grads_ref[x, u, :, start : start + half] = value[u * unit : (u + 1) * unit, x * half : (x + 1) * half]


def ffn(o, unit_one, cot, w_co, w_in, w_out, biases, ffn_bias, gain, shift, nb, rows=256):
    n, d = o.shape
    ff = w_in.shape[1]
    blocks = n // rows
    nz = ff // d
    unit = d // nb
    block = pl.BlockSpec((rows, d), lambda i: (jnp.minimum(i, blocks - 1), 0))
    width = ff + d // 2
    return pl.pallas_call(
        functools.partial(ffn_kernel, blocks=blocks, nz=nz),
        grid=(blocks + nz,),
        in_specs=[block, block, block] + [whole()] * 7,
        out_specs=[block, block, block,
                   pl.BlockSpec((8, d), lambda i: (0, 0)), pl.BlockSpec((8, ff), lambda i: (0, 0)),
                   pl.BlockSpec((2, nb // nz, unit, width), lambda i: (0, jnp.maximum(i - blocks, 0), 0, 0))],
        out_shape=[
            pltpu.HBM((n, d), bf16),
            pltpu.HBM((n, d), f32),
            pltpu.HBM((n, d), bf16),
            pltpu.HBM((8, d), f32),
            pltpu.HBM((8, ff), f32),
            pltpu.HBM((2, nb, unit, width), bf16),
        ],
        scratch_shapes=[
            pltpu.VMEM((rows, ff), f32),
            pltpu.VMEM((nz, n, d), bf16),
            pltpu.VMEM((nz, n, d), bf16),
            pltpu.VMEM((n, d), bf16),
            pltpu.VMEM((n, d), bf16),
            pltpu.VMEM((d, n), bf16),
            pltpu.VMEM((d, n), bf16),
        ],
        compiler_params=params(60),
        cost_estimate=cost(12 * n * d * ff + 6 * n * d * d, 8 * d * ff + 20 * n * d, 2 * n * ff),
        name="ffn",
    )(*hbm(o, unit_one, cot), w_co, w_in, w_out, biases, ffn_bias, gain, shift)


def store_units(place, value, unit, send_ref, own_ref, first=0, z_local=False):
    mx, mz, my, core = place[0], place[1], place[2], place[3]
    half = value.shape[1] // 2
    for mine in range(2):
        @pl.when(core == mine)
        def _():
            for u in range(value.shape[0] // unit):
                ref = own_ref if u % 2 == mine else send_ref
                z = 0 if z_local else jnp.bitwise_xor(u // 4, mz)
                y = jnp.bitwise_xor((u // 2) % 2, my)
                for x in range(2):
                    ref[y, jnp.bitwise_xor(x, mx), z, :unit] = value[u * unit : (u + 1) * unit, x * half : (x + 1) * half]


def middle_kernel(
    place, g2, unit_ref, scale_ref, grad_a, grad_b, out_self, low_one, sources, w_q, w_out, w_kv, gain,
    g1_ref, gm_ref, sums_ref, other_ref, mine_ref, send_ref, own_ref, gq_all, b1_all, *, blocks, unit,
):
    i = pl.program_id(0)
    rows, d = g2.shape

    @pl.when(i == 0)
    def _():
        sums_ref[...] = jnp.zeros_like(sums_ref)

    @pl.when(i < blocks)
    def _():
        half = blocks // 2
        mine = i >= half
        at = jnp.where(mine, place[0] * half + i - half, (1 - place[0]) * half + i)
        here = pl.ds(pl.multiple_of(at * rows, rows), rows)
        gq = jnp.concatenate([grad_a[0, here, :], grad_b[0, here, :]], axis=1)
        gq_all[here, :] = gq
        g = g2[...] + dot(gq, w_q[...], NT)
        unit_one = unit_ref[...]
        grad = norm_back(g, unit_one, scale_ref[:, 0:1], gain[0:1, :])
        g1_ref[...] = grad
        branch = grad.astype(bf16)
        b1_all[here, :] = branch
        sums_ref[0:1, :] += row_sum(g * unit_one)
        sums_ref[1:2, :] += row_sum(g)
        sums_ref[2:3, :] += row_sum(grad)
        gm_ref[...] = dot(branch, w_out[...], NT).astype(bf16)
        pair = jnp.concatenate([r[m, here, :] for m in (1, 2) for r in (grad_a, grad_b)], axis=1)
        value = dot(pair, w_kv[...], NT)

        @pl.when(mine)
        def _():
            mine_ref[...] = value

        @pl.when(jnp.logical_not(mine))
        def _():
            other_ref[...] = value.astype(bf16)

    def store(value):
        store_units(place, value.astype(bf16), unit, send_ref, own_ref)

    @pl.when(i == blocks)
    def _():
        store(dot(out_self[...], b1_all[...], TN))

    @pl.when(i == blocks + 1)
    def _():
        store(dot(low_one[...], gq_all[...], TN))

    for step, grads in ((2, grad_a), (3, grad_b)):
        @pl.when(i == blocks + step)
        def _(grads=grads):
            store(dot(sources[...], jnp.concatenate([grads[1], grads[2]], axis=1), TN))


def middle(place, g2, unit_one, scale, grad_a, grad_b, out_self, low_one, sources, w_q, w_out, w_kv, gain, nb, rows=256):
    n, d = g2.shape
    blocks = n // rows
    unit = d // nb
    half = blocks // 2

    def block_at(i, p):
        i = jnp.minimum(i, blocks - 1)
        return (jnp.where(i < half, (1 - p[0]) * half + i, p[0] * half + i - half), 0)

    block = pl.BlockSpec((rows, d), block_at)
    fixed_block = lambda shape: pl.BlockSpec(shape, lambda i, p: (0,) * len(shape), pipeline_mode=pl.Buffered(1))
    piece = pl.BlockSpec((2, 2, nb // 4, unit, d // 2), lambda i, p: (0, 0, 0, 0, jnp.maximum(i - blocks, 0)))
    big = pltpu.HBM((2, 2, nb // 4, unit, 2 * d), bf16)
    return pl.pallas_call(
        functools.partial(middle_kernel, blocks=blocks, unit=unit),
        grid_spec=pltpu.PrefetchScalarGridSpec(
            num_scalar_prefetch=1,
            grid=(blocks + 4,),
            in_specs=[block, block, pl.BlockSpec((rows, 128), block_at), fixed_block(grad_a.shape), fixed_block(grad_b.shape)]
            + [fixed_block((n, d))] * 3 + [whole()] * 4,
            out_specs=[
                block,
                block,
                pl.BlockSpec((8, d), lambda i, p: (0, 0)),
                pl.BlockSpec((rows, d), lambda i, p: (jnp.minimum(i, half - 1), 0)),
                pl.BlockSpec((rows, d), lambda i, p: (jnp.clip(i - half, 0, half - 1), 0)),
                piece,
                piece,
            ],
            scratch_shapes=[pltpu.VMEM((n, d), bf16), pltpu.VMEM((n, d), bf16)],
        ),
        out_shape=[
            pltpu.HBM((n, d), f32),
            pltpu.HBM((n, d), bf16),
            pltpu.HBM((8, d), f32),
            pltpu.HBM((n // 2, d), bf16),
            pltpu.HBM((n // 2, d), f32),
            big,
            big,
        ],
        compiler_params=params(48),
        cost_estimate=cost(16 * n * d * d, 40 * n * d),
        name="middle",
    )(place, *hbm(g2, unit_one, scale, grad_a, grad_b, out_self, low_one, sources), w_q, w_out, w_kv, gain)


def grad_rows_kernel(place, *refs, columns, based):
    gs, weight = refs[: len(columns)], refs[len(columns)]
    out_ref = refs[-1]
    value = None
    for g, chunks in zip(gs, columns):
        for m, starts in enumerate(chunks):
            if not starts:
                continue
            w = [weight[:, s : s + size] for s, size in starts]
            w = w[0] if len(w) == 1 else jnp.concatenate(w, axis=1)
            term = dot(g[m], w, NT)
            value = term if value is None else value + term
    if based:
        value = value + refs[len(columns) + 1][...]

    out_ref[...] = value.astype(out_ref.dtype)


def grad_rows(place, terms, columns, weight, base, mine, rows=256):
    n = terms[0].shape[1]
    d, k = weight.shape
    steps = n // 2 // rows
    half = lambda i, p: (p[0] if mine else 1 - p[0]) * steps + i
    ins = [pl.BlockSpec((t.shape[0], rows, t.shape[2]), lambda i, p: (0, half(i, p), 0)) for t in terms] + [whole()]
    args = hbm(*terms) + [weight]
    if base is not None:
        ins.append(pl.BlockSpec((rows, d), lambda i, p: (half(i, p), 0)))
        args += hbm(base)
    return pl.pallas_call(
        functools.partial(grad_rows_kernel, columns=columns, based=base is not None),
        grid_spec=pltpu.PrefetchScalarGridSpec(
            num_scalar_prefetch=1,
            grid=(steps,),
            in_specs=ins,
            out_specs=pl.BlockSpec((rows, d), lambda i, p: (i, 0)),
        ),
        out_shape=pltpu.HBM((n // 2, d), f32 if mine else bf16),
        compiler_params=params(40),
        cost_estimate=cost(n * k * d, n * k + 2 * k * d + 4 * n * d),
        name="grad_rows",
    )(place, *args)


def route(nb, move):
    dz, dy, dc, dx = move
    pairs = []
    for b in range(nb):
        z, y, core = b // 4, (b // 2) % 2, b % 2
        for x in range(2):
            target = (z ^ dz) * 4 + (y ^ dy) * 2 + (core ^ dc)
            pairs.append((b * 2 + x, target * 2 + (x ^ dx)))
    return pairs


def send(value, nb, move):
    return lax.ppermute(value, ("z", "y", "core", "seq"), route(nb, move))


def core_stage(buffers, nb):
    to_send, own = buffers
    return own, send(to_send, nb, (0, 0, 1, 0))


def y_prepare(state):
    own, got = state
    return (own[1].astype(f32) + got[1].astype(f32)).astype(bf16), (own, got)


def y_move(value, nb):
    return send(value, nb, (0, 1, 0, 0))


def x_prepare(state):
    own, got, more = state
    total = own[0].astype(f32) + got[0].astype(f32) + more.astype(f32)
    return total[0].astype(bf16), total[1].astype(bf16)


def x_move(value, nb):
    return send(value, nb, (0, 0, 0, 1))


def z_prepare(state):
    kept, got = state
    total = kept.astype(f32) + got.astype(f32)
    return total[0::2].astype(bf16), total[1::2].astype(bf16)


def z_move(value, nb, bit):
    return send(value, nb, (1 << bit, 0, 0, 0))


def halves_first(state):
    own, got = state
    h = own.shape[2] // 2
    over_y = own[1, :, :h].astype(f32) + got[1, :, :h].astype(f32)
    over_x = own[:, 1, h:].astype(f32) + got[:, 1, h:].astype(f32)
    return over_y.astype(bf16), over_x.astype(bf16)


def halves_move(values, nb, turn):
    a, b = ((0, 0, 0, 1), (0, 1, 0, 0)) if turn else ((0, 1, 0, 0), (0, 0, 0, 1))
    return send(values[0], nb, a), send(values[1], nb, b)


def halves_second(state):
    (own, got), (from_y, from_x) = state
    h = own.shape[2] // 2
    a = own[0, :, :h].astype(f32) + got[0, :, :h].astype(f32) + from_y.astype(f32)
    b = own[:, 0, h:].astype(f32) + got[:, 0, h:].astype(f32) + from_x.astype(f32)
    return (a[0].astype(bf16), b[0].astype(bf16)), (a[1].astype(bf16), b[1].astype(bf16))


def halves_third(state):
    kept, got = state
    total = jnp.concatenate([k.astype(f32) + g.astype(f32) for k, g in zip(kept, got)], axis=0)
    return total[0::2].astype(bf16), total[1::2].astype(bf16)


def after_y(state):
    own, got, more = state
    return (own[0].astype(f32) + got[0].astype(f32) + more.astype(f32)).astype(bf16)


def direct_z(total, nb):
    result = total[:, 0].astype(f32)
    for d in range(1, nb // 4):
        result = result + send(total[:, d], nb, (d, 0, 0, 0)).astype(f32)
    return result


def at(value, index, axis):
    return lax.dynamic_index_in_dim(value, index, axis, keepdims=False)


def last_stage(state):
    kept, got = state
    return (kept.astype(f32) + got.astype(f32))[0]


def last_part(state, start, end):
    kept, got = state
    return (kept[:, :, start:end].astype(f32) + got[:, :, start:end].astype(f32))[0]


def tie(*values):
    return lax.optimization_barrier(values)


def swap(value):
    return lax.ppermute(value, "seq", [(0, 1), (1, 0)])


def split_pairs(local):
    positions, _, width = local.shape
    pairs = local.reshape(positions, 2 * width)
    x = lax.axis_index("seq")
    return pairs, lax.dynamic_slice(pairs, (0, (1 - x) * width), (positions, width))


def join_pairs(mine, got):
    x = lax.axis_index("seq")
    got = got.astype(mine.dtype)
    both = jnp.concatenate([jnp.where(x == 0, mine, got), jnp.where(x == 0, got, mine)], axis=1)
    return both.reshape(mine.shape[0], 2, mine.shape[1])


def whole_sequence(pairs, got):
    x = lax.axis_index("seq")
    width = got.shape[1]
    mine = lax.dynamic_slice(pairs, (0, x * width), got.shape)
    return jnp.where(x == 0, jnp.concatenate([mine, got]), jnp.concatenate([got, mine]))


def per_device_fast(
    hidden_in,
    memory,
    src_len,
    out_grad,
    w_self_qkv,
    w_self_out,
    w_cross_q,
    w_cross_kv,
    w_cross_out,
    w_ffn_in,
    w_ffn_out,
    biases,
    ffn_bias,
    norm_gain,
    norm_shift,
):
    nb = lax.axis_size(("z", "y", "core"))
    width = hidden_in.shape[2]
    half = width // 2
    x, b = lax.axis_index("seq"), lax.axis_index(("z", "y", "core"))
    place = jnp.stack([x, b // 4, (b // 2) % 2, b % 2]).astype(jnp.int32)
    length = lax.dynamic_slice_in_dim(src_len, x, 1)

    pairs, other = split_pairs(hidden_in)
    got = swap(other)
    memory_pairs, memory_other = split_pairs(memory)
    memory_got = swap(memory_other)
    cot_pairs, cot_other = split_pairs(out_grad)
    tokens, query_self, key_self, value_self = project(
        place, pairs, got, w_self_qkv, biases, ((0, 0.125), (None, 1.0), (1, 1.0))
    )
    query_self, cot_other = tie(query_self, cot_other)
    cot_got = swap(cot_other)
    out_self, lp_self = attn_fwd(length, query_self, key_self, value_self, True)
    unit_one, scale_one, low_one, query_cross = after_self(
        out_self, tokens, w_self_out, w_cross_q, biases, norm_gain, norm_shift
    )
    sources, key_cross, value_cross = project(
        place, memory_pairs, memory_got, w_cross_kv, biases, ((None, 1.0), (4, 1.0))
    )
    out_cross, lp_cross = attn_fwd(length, query_cross, key_cross, value_cross, False)
    cotangent = whole_sequence(cot_pairs, cot_got)
    layer, grad_two, grad_mixed, sums_ffn, bias_sums, one = ffn(
        out_cross, unit_one, cotangent, w_cross_out, w_ffn_in, w_ffn_out, biases, ffn_bias[None], norm_gain, norm_shift, nb
    )
    span = layer.shape[0] // 2

    ff = w_ffn_in.shape[1]
    layer_other = lax.dynamic_slice_in_dim(layer, (1 - x) * span, span, 0)
    one, layer_other, grad_mixed = tie(one, layer_other, grad_mixed)
    one = lax.psum_scatter(one.reshape(-1, one.shape[-1]), ("seq", "z", "y", "core"), scatter_dimension=0, tiled=True)
    layer_got = swap(layer_other)
    back = partial(attn_bwd, length, query_cross, key_cross, value_cross, out_cross)
    cross_a, sums_ca = back(grad_mixed, lp_cross, False, 0, 1, 3)

    cross_a, grad_mixed, layer_got = tie(cross_a, grad_mixed, layer_got)
    cross_b, sums_cb = back(grad_mixed, lp_cross, False, 3, 1, 3)

    grad_one, grad_mixed, sums_one, other, memory_mine, *three = middle(
        place, grad_two, unit_one, scale_one, cross_a, cross_b, out_self, low_one, sources,
        w_cross_q, w_self_out, w_cross_kv, norm_gain, nb,
    )

    three, other, grad_mixed = tie(three, other, grad_mixed)
    three = core_stage(three, nb)
    cut = span * 5 // 8
    memory_back = swap(other[:cut])
    memory_rest = other[cut:]
    back = partial(attn_bwd, length, query_self, key_self, value_self, out_self)
    self_a, sums_sa, *four = back(
        grad_mixed, lp_self, True, 0, 3, 2, tokens, place, nb, "early", (sums_one, sums_ca, sums_cb, sums_ffn, bias_sums)
    )

    four, three, grad_mixed, memory_back = tie(four, three, grad_mixed, memory_back)
    four = core_stage(four, nb)
    three_out = halves_first(three)
    three_out, grad_mixed = tie(three_out, grad_mixed)
    three = three, halves_move(three_out, nb, False)
    self_b, sums_sb, *five = back(grad_mixed, lp_self, True, 1, 3, 2, tokens, place, nb)

    five, four, three, grad_mixed = tie(five, four, three, grad_mixed)
    five = core_stage(five, nb)
    four_out, four = y_prepare(four)
    three_keep, three_out = halves_second(three)
    four_out, three_out, grad_mixed, memory_rest = tie(four_out, three_out, grad_mixed, memory_rest)
    four = four + (y_move(four_out, nb),)
    memory_rest = swap(memory_rest)
    three = three_keep, halves_move(three_out, nb, True)
    self_c, sums_sc, *six = back(grad_mixed, lp_self, True, 2, 3, 2, tokens, place, nb, "late", (sums_sa, sums_sb))

    self_c, six, five, four, three, memory_rest = tie(self_c, six, five, four, three, memory_rest)
    six = core_stage(six, nb)
    five_out, five = y_prepare(five)
    four_keep, four_out = x_prepare(four)
    three_keep, three_out = halves_third(three)
    five_out, four_out, three_out, self_c = tie(five_out, four_out, three_out, self_c)
    five = five + (y_move(five_out, nb),)
    four = four_keep, x_move(four_out, nb)
    three = three_keep, z_move(three_out, nb, 0)
    spots = [tuple(tuple((m * width + (i + s) * 128, 128) for s in (0, 3)) for m in range(3)) for i in range(3)]
    other = grad_rows(place, [self_a, self_b, self_c], spots, w_self_qkv, grad_one, False)

    other, six, three, four, grad_one = tie(other, six, three, four, grad_one)
    six_out, six = y_prepare(six)
    four_keep, four_out = z_prepare(four)
    three_keep, three_out = z_prepare(three)
    six_out, other, four_out, three_out, grad_one = tie(six_out, other, four_out, three_out, grad_one)
    six = six + (y_move(six_out, nb),)
    four = four_keep, z_move(four_out, nb, 0)
    three = three_keep, z_move(three_out, nb, 1)
    in_back = swap(other)
    mine = grad_rows(place, [self_a, self_b, self_c], spots, w_self_qkv, grad_one, True)

    mine, four, layer_got, one = tie(mine, four, layer_got, one)
    four_keep, four_out = z_prepare(four)
    four = four_keep, z_move(four_out, nb, 1)
    layer_out = join_pairs(lax.dynamic_slice_in_dim(layer, x * span, span, 0), layer_got)
    layer_out, mine, six, five, three, memory_back = tie(layer_out, mine, six, five, three, memory_back)
    both = jnp.concatenate([after_y(six), after_y(five)], axis=2)
    both, memory_back = tie(both, memory_back)
    moved = [send(both[:, d], nb, (d, 0, 0, 0)) for d in range(1, nb // 4)]
    grad_memory = join_pairs(memory_mine, jnp.concatenate([memory_back, memory_rest]))
    grad_memory, moved, one, four = tie(grad_memory, moved, one, four)
    both = both[:, 0].astype(f32)
    for value in moved:
        both = both + value.astype(f32)
    last = both[1].astype(bf16)
    last, one, in_back = tie(last, one, in_back)
    last = x_move(last, nb)
    grad_in = join_pairs(mine, in_back)
    one = one.astype(f32)
    pieces = ff // width
    grad_ffn_out = jnp.concatenate([one[:, c * half : (c + 1) * half] for c in range(pieces)], axis=0)
    grad_ffn_in = one[:, pieces * half :]
    group = [last_part(three, c * half, e * half) for c, e in ((0, 1), (1, 2), (2, 4))]
    four = last_stage(four)
    last, grad_in, grad_ffn_in, grad_ffn_out, group, four = tie(last, grad_in, grad_ffn_in, grad_ffn_out, group, four)
    both = both[0] + last.astype(f32)
    unit = width // nb
    ends = unit, both.shape[0] - unit
    thirds = [s.reshape(unit, 3, 128) for s in (four[:unit], both[ends[1] :], both[: ends[0]])]
    grad_self_qkv = jnp.stack(thirds, axis=2).reshape(unit, 9 * 128)
    late = both[ends[0] : ends[0] + 6, :256].reshape(3, 2, 2, 128)
    late = at(late, x, 2).swapaxes(0, 1).reshape(2, half)
    early = lax.dynamic_slice_in_dim(four[unit:], x * 16, 16, 0)
    vectors = jnp.concatenate([late, early[:11]])
    bias_total = early[11 : 11 + bias_sums.shape[1] // width].reshape(-1)
    return (
        layer_out,
        grad_in,
        grad_memory,
        grad_self_qkv,
        group[0],
        group[1],
        group[2],
        grad_ffn_in[:, -half:],
        grad_ffn_in[:, :-half],
        grad_ffn_out,
        vectors[0:7],
        bias_total,
        vectors[7:10],
        vectors[10:13],
    )


def solution(mesh):
    devices = dict(mesh.shape)

    in_specs = (
        P("seq", "batch", None),
        P("seq", "batch", None),
        P("batch"),
        P("seq", "batch", None),
        P(),
        P(),
        P(),
        P(),
        P(),
        P(),
        P(),
        P(),
        P(),
        P(),
        P(),
    )
    out_specs = (
        P("seq", "batch", None),
        P("seq", "batch", None),
        P("seq", "batch", None),
        P("batch", "seq"),
        P("batch", "seq"),
        P("batch", "seq"),
        P("batch", "seq"),
        P("batch", "seq"),
        P("batch", "seq"),
        P("batch", "seq"),
        P(None, "seq"),
        P("seq"),
        P(None, "seq"),
        P(None, "seq"),
    )
    nb, ns = devices["batch"], devices["seq"]

    def program(hidden_in, *rest):
        whole = ns == 2 and hidden_in.shape[1] == 2 * nb and nb % 8 == 0 and nb & (nb - 1) == 0
        if not whole:
            general = jax.shard_map(
                per_device_general, mesh=mesh, in_specs=in_specs, out_specs=out_specs, check_vma=False
            )
            return general(hidden_in, *rest)
        parts = jax.sharding.Mesh(mesh.devices.reshape(nb // 4, 2, 2, ns), ("z", "y", "core", "seq"))
        split = lambda spec: P(*(("z", "y", "core") if axis == "batch" else axis for axis in spec))
        fast = jax.shard_map(
            per_device_fast,
            mesh=parts,
            in_specs=tuple(split(spec) for spec in in_specs),
            out_specs=tuple(split(spec) for spec in out_specs),
            check_vma=False,
        )
        return fast(hidden_in, *rest)

    return program
```

```python
import functools
from functools import partial

import jax
import jax.numpy as jnp
from jax import lax
from jax.experimental import pallas as pl
from jax.experimental.pallas import tpu as pltpu
from jax.sharding import PartitionSpec as P

H = 12


NEGATIVE = -1e30


def from_behind(value, axis, steps):
    count = lax.axis_size(axis)
    pairs = [(source, (source + steps) % count) for source in range(count)]
    return lax.ppermute(value, axis, pairs)


def shifted(block, axis, distance):
    devices = range(lax.axis_size(axis))
    route = [(i - distance, i) for i in devices if i - distance in devices]
    return lax.ppermute(block, axis, route)


def contract_rows(left, right):
    return lax.dot_general(
        left, right, (((0,), (0,)), ((), ())), preferred_element_type=jnp.float32
    )


def times_transposed(grad, weight):
    return lax.dot_general(
        grad, weight, (((1,), (1,)), ((), ())), preferred_element_type=jnp.float32
    )


def norm_forward(value, gain, shift):
    mean = jnp.mean(value, axis=-1, keepdims=True)
    centred = value - mean
    scale = lax.rsqrt(jnp.mean(centred * centred, axis=-1, keepdims=True) + 1e-05)
    unit = centred * scale
    return (unit * gain + shift, unit, scale)


def norm_backward(grad, unit, scale, gain):
    weighted = grad * gain
    inner = (
        weighted
        - jnp.mean(weighted, axis=-1, keepdims=True)
        - unit * jnp.mean(weighted * unit, axis=-1, keepdims=True)
    )
    return (scale * inner, jnp.sum(grad * unit, axis=0), jnp.sum(grad, axis=0))


def allowed_keys(query_pos, key_pos, lengths, causal):
    if causal:
        return (query_pos[:, None] >= key_pos[None, :])[None, None]
    return (key_pos[None, :] < lengths[:, None])[:, None, None, :]


def attend_forward(query, keys, values, lengths, causal, heads):
    span, batch, width = query.shape
    size = width // heads
    query_heads = query.reshape(span, batch, heads, size)
    query_pos = lax.axis_index("seq") * span + lax.iota(jnp.int32, span)

    def block(carry, key_block, value_block, first):
        previous, total, summed = carry
        rows = key_block.shape[0]
        key_pos = first + lax.iota(jnp.int32, rows)
        scores = jnp.einsum(
            "qshd,kshd->shqk",
            query_heads,
            key_block.reshape(rows, batch, heads, size),
            preferred_element_type=jnp.float32,
        )
        allowed = allowed_keys(query_pos, key_pos, lengths, causal)
        top = jnp.maximum(previous, jnp.max(jnp.where(allowed, scores, NEGATIVE), axis=-1))
        weights = jnp.where(allowed, jnp.exp(scores - top[..., None]), 0.0)
        rescale = jnp.exp(previous - top)
        total = total * rescale + jnp.sum(weights, axis=-1)
        summed = summed * rescale[..., None] + jnp.einsum(
            "shqk,kshd->shqd",
            weights.astype(jnp.bfloat16),
            value_block.reshape(rows, batch, heads, size),
            preferred_element_type=jnp.float32,
        )
        return (top, total, summed)

    def fold(carry, piece):
        key_piece, value_piece = piece
        rows = key_piece.shape[0]
        count = rows // span
        firsts = span * lax.iota(jnp.int32, count)

        def inner(state, parts):
            return (block(state, parts[0], parts[1], parts[2]), None)

        carry, unused = lax.scan(
            inner,
            carry,
            (
                key_piece.reshape(count, span, batch, width),
                value_piece.reshape(count, span, batch, width),
                firsts,
            ),
        )
        return carry

    empty = (
        jnp.full((batch, heads, span), NEGATIVE, jnp.float32),
        jnp.zeros((batch, heads, span), jnp.float32),
        jnp.zeros((batch, heads, span, size), jnp.float32),
    )
    if causal:
        top, total, summed = fold(
            empty,
            (
                lax.all_gather(keys, "seq", axis=0, tiled=True),
                lax.all_gather(values, "seq", axis=0, tiled=True),
            ),
        )
    else:
        top, total, summed = fold(
            empty,
            (
                lax.all_gather(keys, "seq", axis=0, tiled=True),
                lax.all_gather(values, "seq", axis=0, tiled=True),
            ),
        )
    mixed = summed / total[..., None]
    mixed = jnp.transpose(mixed, (2, 0, 1, 3)).reshape(span, batch, width)
    return (mixed, top + jnp.log(total))


def block_backward(
    query_heads, grad_heads, delta, logsum, key_block, value_block, allowed, batch, heads, size
):
    span = key_block.shape[0]
    width = heads * size
    key_heads = key_block.reshape(span, batch, heads, size)
    value_heads = value_block.reshape(span, batch, heads, size)
    scores = jnp.einsum(
        "qshd,kshd->shqk", query_heads, key_heads, preferred_element_type=jnp.float32
    )
    weights = jnp.where(allowed, jnp.exp(scores - logsum[..., None]), 0.0)
    grad_weights = jnp.einsum(
        "qshd,kshd->shqk", grad_heads, value_heads, preferred_element_type=jnp.float32
    )
    grad_scores = (weights * (grad_weights - delta[..., None])).astype(jnp.bfloat16)
    grad_query = jnp.einsum(
        "shqk,kshd->qshd", grad_scores, key_heads, preferred_element_type=jnp.float32
    )
    grad_keys = jnp.einsum(
        "shqk,qshd->kshd", grad_scores, query_heads, preferred_element_type=jnp.float32
    ).reshape(span, batch, width)
    grad_values = jnp.einsum(
        "shqk,qshd->kshd",
        weights.astype(jnp.bfloat16),
        grad_heads,
        preferred_element_type=jnp.float32,
    ).reshape(span, batch, width)
    return (grad_query, grad_keys, grad_values)


def attend_backward(query, keys, values, mixed, grad_mixed, logsum, lengths, causal, heads):
    span, batch, width = query.shape
    size = width // heads
    query_heads = query.reshape(span, batch, heads, size)
    grad_heads = grad_mixed.reshape(span, batch, heads, size)
    delta = jnp.sum(
        grad_heads.astype(jnp.float32) * mixed.reshape(span, batch, heads, size), axis=-1
    )
    delta = jnp.transpose(delta, (1, 2, 0))
    devices = lax.axis_size("seq")
    place = lax.axis_index("seq")
    query_pos = place * span + lax.iota(jnp.int32, span)
    grad_query = jnp.zeros((span, batch, heads, size), jnp.float32)
    grad_keys = jnp.zeros((span, batch, width), jnp.float32)
    grad_values = jnp.zeros((span, batch, width), jnp.float32)
    key_block, value_block = (keys, values)
    for step in range(devices):
        owner = (place - step + devices) % devices
        key_pos = owner * span + lax.iota(jnp.int32, span)
        allowed = allowed_keys(query_pos, key_pos, lengths, causal)
        part_query, part_keys, part_values = block_backward(
            query_heads,
            grad_heads,
            delta,
            logsum,
            key_block,
            value_block,
            allowed,
            batch,
            heads,
            size,
        )
        grad_query = grad_query + part_query
        grad_keys = grad_keys + part_keys
        grad_values = grad_values + part_values
        if causal:
            grad_keys, grad_values = (
                from_behind(grad_keys.astype(jnp.bfloat16), "seq", 1).astype(grad_keys.dtype),
                from_behind(grad_values.astype(jnp.bfloat16), "seq", 1).astype(grad_values.dtype),
            )
        else:
            grad_keys, grad_values = (
                from_behind(grad_keys.astype(jnp.bfloat16), "seq", 1).astype(grad_keys.dtype),
                from_behind(grad_values.astype(jnp.bfloat16), "seq", 1).astype(grad_values.dtype),
            )
        if step + 1 < devices:
            if causal:
                key_block, value_block = shifted((key_block, value_block), "seq", 1)
            else:
                key_block, value_block = from_behind((key_block, value_block), "seq", 1)
    return (grad_query.reshape(span, batch, width), grad_keys, grad_values)


def per_device_general(
    hidden_in,
    memory,
    src_len,
    out_grad,
    w_self_qkv,
    w_self_out,
    w_cross_q,
    w_cross_kv,
    w_cross_out,
    w_ffn_in,
    w_ffn_out,
    biases,
    ffn_bias,
    norm_gain,
    norm_shift,
):
    span, batch, width = hidden_in.shape
    heads = H
    rows = span * batch
    layout = (span, batch, width)
    tokens = hidden_in.reshape(rows, width)
    sources = memory.reshape(rows, width)
    joined = jnp.dot(tokens, w_self_qkv, preferred_element_type=jnp.float32)
    query_self = ((joined[:, :width] + biases[0]) * 0.125).astype(jnp.bfloat16)
    key_self = joined[:, width : 2 * width].astype(jnp.bfloat16)
    value_self = (joined[:, 2 * width :] + biases[1]).astype(jnp.bfloat16)
    mixed_self, logsum_self = attend_forward(
        query_self.reshape(layout),
        key_self.reshape(layout),
        value_self.reshape(layout),
        src_len,
        True,
        heads,
    )
    out_self = mixed_self.reshape(rows, width).astype(jnp.bfloat16)
    resid_one = (
        tokens.astype(jnp.float32)
        + jnp.dot(out_self, w_self_out, preferred_element_type=jnp.float32)
        + biases[2]
    )
    normed_one, unit_one, scale_one = norm_forward(resid_one, norm_gain[0], norm_shift[0])
    normed_one_low = normed_one.astype(jnp.bfloat16)
    query_cross = (
        (jnp.dot(normed_one_low, w_cross_q, preferred_element_type=jnp.float32) + biases[3]) * 0.125
    ).astype(jnp.bfloat16)
    pair = jnp.dot(sources, w_cross_kv, preferred_element_type=jnp.float32)
    key_cross = pair[:, :width].astype(jnp.bfloat16)
    value_cross = (pair[:, width:] + biases[4]).astype(jnp.bfloat16)
    mixed_cross, logsum_cross = attend_forward(
        query_cross.reshape(layout),
        key_cross.reshape(layout),
        value_cross.reshape(layout),
        src_len,
        False,
        heads,
    )
    out_cross = mixed_cross.reshape(rows, width).astype(jnp.bfloat16)
    resid_two = (
        normed_one + jnp.dot(out_cross, w_cross_out, preferred_element_type=jnp.float32) + biases[5]
    )
    normed_two, unit_two, scale_two = norm_forward(resid_two, norm_gain[1], norm_shift[1])
    normed_two_low = normed_two.astype(jnp.bfloat16)
    inner = jnp.dot(normed_two_low, w_ffn_in, preferred_element_type=jnp.float32) + ffn_bias
    active = jax.nn.gelu(inner, approximate=False).astype(jnp.bfloat16)
    resid_three = (
        normed_two + jnp.dot(active, w_ffn_out, preferred_element_type=jnp.float32) + biases[6]
    )
    result, unit_three, scale_three = norm_forward(resid_three, norm_gain[2], norm_shift[2])
    layer_out = result.astype(jnp.bfloat16).reshape(layout)
    grad_three, gain_three, shift_three = norm_backward(
        out_grad.reshape(rows, width).astype(jnp.float32), unit_three, scale_three, norm_gain[2]
    )
    branch_three = grad_three.astype(jnp.bfloat16)
    hidden_pre, hidden_act = (inner, active)
    grad_ffn_out = contract_rows(hidden_act, branch_three)
    grad_act = times_transposed(branch_three, w_ffn_out)
    unused, pull = jax.vjp(partial(jax.nn.gelu, approximate=False), hidden_pre)
    grad_pre = pull(grad_act)[0].astype(jnp.bfloat16)
    grad_ffn_in = contract_rows(normed_two_low, grad_pre)
    grad_normed_two = grad_three + times_transposed(grad_pre, w_ffn_in)
    grad_two, gain_two, shift_two = norm_backward(
        grad_normed_two, unit_two, scale_two, norm_gain[1]
    )
    branch_two = grad_two.astype(jnp.bfloat16)
    grad_cross_out = contract_rows(out_cross, branch_two)
    grad_mixed_cross = times_transposed(branch_two, w_cross_out).astype(jnp.bfloat16)
    raw_query, grad_keys, grad_values = attend_backward(
        query_cross.reshape(layout),
        key_cross.reshape(layout),
        value_cross.reshape(layout),
        mixed_cross,
        grad_mixed_cross.reshape(layout),
        logsum_cross,
        src_len,
        False,
        heads,
    )
    grad_query_cross = (raw_query.reshape(rows, width) * 0.125).astype(jnp.bfloat16)
    grad_pair = jnp.concatenate(
        [
            grad_keys.reshape(rows, width).astype(jnp.bfloat16),
            grad_values.reshape(rows, width).astype(jnp.bfloat16),
        ],
        axis=1,
    )
    grad_cross_q = contract_rows(normed_one_low, grad_query_cross)
    grad_cross_kv = contract_rows(sources, grad_pair)
    grad_memory = times_transposed(grad_pair, w_cross_kv).reshape(layout)
    grad_normed_one = grad_two + times_transposed(grad_query_cross, w_cross_q)
    grad_one, gain_one, shift_one = norm_backward(
        grad_normed_one, unit_one, scale_one, norm_gain[0]
    )
    branch_one = grad_one.astype(jnp.bfloat16)
    grad_self_out = contract_rows(out_self, branch_one)
    grad_mixed_self = times_transposed(branch_one, w_self_out).astype(jnp.bfloat16)
    raw_query, grad_keys, grad_values = attend_backward(
        query_self.reshape(layout),
        key_self.reshape(layout),
        value_self.reshape(layout),
        mixed_self,
        grad_mixed_self.reshape(layout),
        logsum_self,
        src_len,
        True,
        heads,
    )
    grad_joined = jnp.concatenate(
        [
            (raw_query.reshape(rows, width) * 0.125).astype(jnp.bfloat16),
            grad_keys.reshape(rows, width).astype(jnp.bfloat16),
            grad_values.reshape(rows, width).astype(jnp.bfloat16),
        ],
        axis=1,
    )
    grad_self_qkv = contract_rows(tokens, grad_joined)
    grad_in = (grad_one + times_transposed(grad_joined, w_self_qkv)).reshape(layout)
    vector_terms = jnp.stack(
        [
            jnp.sum(grad_joined[:, :width].astype(jnp.float32), axis=0),
            jnp.sum(grad_joined[:, 2 * width :].astype(jnp.float32), axis=0),
            jnp.sum(grad_one, axis=0),
            jnp.sum(grad_query_cross.astype(jnp.float32), axis=0),
            jnp.sum(grad_pair[:, width:].astype(jnp.float32), axis=0),
            jnp.sum(grad_two, axis=0),
            jnp.sum(grad_three, axis=0),
            gain_one,
            gain_two,
            gain_three,
            shift_one,
            shift_two,
            shift_three,
        ]
    )
    bias_terms = jnp.sum(grad_pre.astype(jnp.float32), axis=0)[None]
    (
        grad_self_qkv,
        grad_self_out,
        grad_cross_q,
        grad_cross_kv,
        grad_cross_out,
        grad_ffn_in,
        grad_ffn_out,
        vector_terms,
        bias_terms,
    ) = (
        lax.psum_scatter(
            grad_self_qkv.astype(jnp.bfloat16), "seq", scatter_dimension=1, tiled=True
        ).astype(jnp.float32),
        lax.psum_scatter(
            grad_self_out.astype(jnp.bfloat16), "seq", scatter_dimension=1, tiled=True
        ).astype(jnp.float32),
        lax.psum_scatter(
            grad_cross_q.astype(jnp.bfloat16), "seq", scatter_dimension=1, tiled=True
        ).astype(jnp.float32),
        lax.psum_scatter(
            grad_cross_kv.astype(jnp.bfloat16), "seq", scatter_dimension=1, tiled=True
        ).astype(jnp.float32),
        lax.psum_scatter(
            grad_cross_out.astype(jnp.bfloat16), "seq", scatter_dimension=1, tiled=True
        ).astype(jnp.float32),
        lax.psum_scatter(
            grad_ffn_in.astype(jnp.bfloat16), "seq", scatter_dimension=1, tiled=True
        ).astype(jnp.float32),
        lax.psum_scatter(
            grad_ffn_out.astype(jnp.bfloat16), "seq", scatter_dimension=1, tiled=True
        ).astype(jnp.float32),
        lax.psum_scatter(
            vector_terms.astype(jnp.bfloat16), "seq", scatter_dimension=1, tiled=True
        ).astype(jnp.float32),
        lax.psum_scatter(
            bias_terms.astype(jnp.bfloat16), "seq", scatter_dimension=1, tiled=True
        ).astype(jnp.float32),
    )
    (
        grad_self_qkv,
        grad_self_out,
        grad_cross_q,
        grad_cross_kv,
        grad_cross_out,
        grad_ffn_in,
        grad_ffn_out,
    ) = (
        lax.psum_scatter(
            grad_self_qkv.astype(jnp.bfloat16), "batch", scatter_dimension=0, tiled=True
        ).astype(jnp.float32),
        lax.psum_scatter(
            grad_self_out.astype(jnp.bfloat16), "batch", scatter_dimension=0, tiled=True
        ).astype(jnp.float32),
        lax.psum_scatter(
            grad_cross_q.astype(jnp.bfloat16), "batch", scatter_dimension=0, tiled=True
        ).astype(jnp.float32),
        lax.psum_scatter(
            grad_cross_kv.astype(jnp.bfloat16), "batch", scatter_dimension=0, tiled=True
        ).astype(jnp.float32),
        lax.psum_scatter(
            grad_cross_out.astype(jnp.bfloat16), "batch", scatter_dimension=0, tiled=True
        ).astype(jnp.float32),
        lax.psum_scatter(
            grad_ffn_in.astype(jnp.bfloat16), "batch", scatter_dimension=0, tiled=True
        ).astype(jnp.float32),
        lax.psum_scatter(
            grad_ffn_out.astype(jnp.bfloat16), "batch", scatter_dimension=0, tiled=True
        ).astype(jnp.float32),
    )
    vector_terms, bias_terms = lax.psum((vector_terms, bias_terms), "batch")
    return (
        layer_out,
        grad_in,
        grad_memory,
        grad_self_qkv,
        grad_self_out,
        grad_cross_q,
        grad_cross_kv,
        grad_cross_out,
        grad_ffn_in,
        grad_ffn_out,
        vector_terms[0:7],
        bias_terms[0],
        vector_terms[7:10],
        vector_terms[10:13],
    )


LOG2E = 1.4426950408889634
NN = (((1,), (0,)), ((), ()))
NT = (((1,), (1,)), ((), ()))
HD = 64
BIG = -1e30
f32, bf16 = jnp.float32, jnp.bfloat16

def dot(a, b, dims=NN):
    return lax.dot_general(a, b, dims, preferred_element_type=f32)

def lanes(shape):
    return lax.broadcasted_iota(jnp.int32, shape, len(shape) - 1)

def swap_halves(x):
    return jnp.concatenate([x[:, HD:], x[:, :HD]], axis=1)

def fwd_kernel(len_ref, q_ref, k_ref, v_ref, o_ref, lp_ref, acc_ref, *, causal, heads, qb, ahead):
    p = pl.program_id(0)
    n = q_ref.shape[0]
    nk = k_ref.shape[0]
    scaled = q_ref[...].astype(f32) * LOG2E
    hi = scaled.astype(bf16)
    lo = (scaled - hi.astype(f32)).astype(bf16)
    first = lanes((n, 128)) < HD
    hi_s, lo_s = swap_halves(hi), swap_halves(lo)
    q_aug = (jnp.where(first, hi, lo_s), jnp.where(first, hi_s, lo))
    kk = k_ref[...]
    k_s = swap_halves(kk)
    k_aug = [jnp.where(first, kk, k_s), jnp.where(first, k_s, kk)]
    if not causal:
        length = len_ref[0]
        row = lax.broadcasted_iota(jnp.int32, (nk, 128), 0)
        extra = jnp.where((row >= length) & (lanes((nk, 128)) == 0), BIG, 0.0).astype(bf16)
        k_aug = [jnp.concatenate([x, extra], axis=1) for x in k_aug]
        one = (lanes((n, 128)) == 0).astype(bf16)
        q_aug = [jnp.concatenate([x, one], axis=1) for x in q_aug]
    vt = jnp.transpose(v_ref[...])
    ones = jnp.ones((16, nk), bf16)
    va = [jnp.concatenate([vt[h * HD:(h + 1) * HD], ones], axis=0) for h in range(2)]

    def scores(c, h):
        top_k = (c + 1) * qb if causal else nk
        s = dot(k_aug[h][:top_k], q_aug[h][c * qb:(c + 1) * qb], NT)
        if causal:
            r = lax.broadcasted_iota(jnp.int32, (qb, qb), 0)
            d = jnp.where(r <= lanes((qb, qb)), s[c * qb:], BIG)
            s = jnp.concatenate([s[:c * qb], d], axis=0) if c else d
        return s

    steps = [(c, h) for c in range(n // qb) for h in range(2)]
    queue = [scores(*x) for x in steps[:ahead]]
    parts = []
    for i, (c, h) in enumerate(steps):
        if i + ahead < len(steps):
            queue.append(scores(*steps[i + ahead]))
        s = queue.pop(0)
        m = jnp.max(s, axis=0, keepdims=True)
        pt = jnp.exp2(s - m).astype(bf16)
        ot = dot(va[h][:, :s.shape[0]], pt)
        l = ot[HD:HD + 1]
        parts.append(ot[:HD] * (1.0 / l))
        acc_ref[pl.ds(2 * p + h, 1), c * qb:(c + 1) * qb] = m + jnp.log2(l)
        if h == 1:
            o_ref[c * qb:(c + 1) * qb, :] = jnp.transpose(jnp.concatenate(parts, axis=0)).astype(bf16)
            parts = []

    @pl.when(p == pl.num_programs(0) - 1)
    def _():
        rows = acc_ref[...]
        wide = jnp.concatenate([rows, jnp.zeros((128 - rows.shape[0], n), f32)], axis=0)
        cols = jnp.transpose(wide)
        a = cols.astype(bf16)
        cols = cols - a.astype(f32)
        b = cols.astype(bf16)
        c = (cols - b.astype(f32)).astype(bf16)
        lane = lanes((n, 128))
        sh = lambda x, k: jnp.concatenate([jnp.zeros((n, k), bf16), x[:, :128 - k]], axis=1)
        out = jnp.where(lane < 16, a, jnp.where(lane < 32, sh(b, 16), jnp.where(lane < 48, sh(c, 32), jnp.where(lane == 127, 1.0, 0.0).astype(bf16))))
        lp_ref[...] = out

def attn_fwd(length, q, k, v, causal, qb=256, ahead=4):
    n, d = q.shape
    blk = lambda r: pl.BlockSpec((r, 128), lambda p, l: (0, p))
    return pl.pallas_call(
        functools.partial(fwd_kernel, causal=causal, heads=d // HD, qb=qb, ahead=ahead),
        grid_spec=pltpu.PrefetchScalarGridSpec(
            num_scalar_prefetch=1, grid=(d // 128,),
            in_specs=[blk(n), blk(k.shape[0]), blk(k.shape[0])],
            out_specs=[blk(n), pl.BlockSpec((n, 128), lambda p, l: (0, 0))],
            scratch_shapes=[pltpu.VMEM((16, n), f32)]),
        out_shape=[pltpu.HBM((n, d), bf16), pltpu.HBM((n, 128), bf16)],
        compiler_params=params(40),
        cost_estimate=cost((n + 256) * n * 1024 // (2 if causal else 1) * (d // HD), 8 * n * d, n * n * d // HD),
        name="attn_fwd",
    )(length, *hbm(q, k, v))

def side_rows(kind, refs, own):
    if kind == "early":
        one, cross_a, cross_b, ffn, bias = refs
        both = lambda r: jnp.concatenate([cross_a[r : r + 1, :], cross_b[r : r + 1, :]], axis=1)
        rows = [one[2:3, :], both(0), both(1), ffn[5:6, :], ffn[2:3, :], one[0:1, :], ffn[3:4, :], ffn[0:1, :], one[1:2, :], ffn[4:5, :], ffn[1:2, :]]
        half = rows[0].shape[1] // 2
        wide = bias.shape[1] // 2
        sides = []
        for x in range(2):
            sides += [r[:, x * half : (x + 1) * half] for r in rows]
            sides += [bias[0:1, x * wide + c * half : x * wide + (c + 1) * half] for c in range(wide // half)]
            sides += [jnp.zeros((1, half), f32)] * (16 - len(rows) - wide // half)
        return jnp.concatenate(sides, axis=0).astype(bf16)
    rows = [refs[0][0:2, :], refs[1][0:2, :], own[0:2, :], jnp.zeros((10, own.shape[1]), f32)]
    rows = jnp.concatenate(rows, axis=0)
    return jnp.concatenate([rows, jnp.zeros((16, 128), f32)], axis=1).astype(bf16)


def bwd_kernel(len_ref, q_ref, k_ref, v_ref, o_ref, g_ref, lp_ref, *rest, causal, qb, first_pair, stride, unit, kind):
    if unit:
        place, tok_ref, *side, out_ref, sums_ref, send_ref, own_ref = rest
    else:
        out_ref, sums_ref = rest
    p = pl.program_id(0) * stride + first_pair
    n, nk = q_ref.shape[0], k_ref.shape[0]
    first = lanes((n, 128)) < HD
    q = q_ref[...]
    scaled = q.astype(f32) * LOG2E
    hi = scaled.astype(bf16)
    lo = (scaled - hi.astype(f32)).astype(bf16)
    hi_s, lo_s = swap_halves(hi), swap_halves(lo)
    lp = lp_ref[...]
    q_aug = [jnp.concatenate([x, lp], axis=1) for x in (jnp.where(first, hi, lo_s), jnp.where(first, hi_s, lo))]
    kk = k_ref[...]
    k_s = swap_halves(kk)
    v = v_ref[...]
    lane = lanes((nk, 128))
    g = g_ref[...]
    zero = jnp.zeros((), bf16)
    go = g.astype(f32) * o_ref[...].astype(f32)
    go_hi = go.astype(bf16)
    go_lo = (go - go_hi.astype(f32)).astype(bf16)
    br = lax.broadcasted_iota(jnp.int32, (128, 128), 0)
    bl = lanes((128, 128))
    pick = jnp.where(((bl < 3) & (br < HD)) | ((bl >= 3) & (bl < 6) & (br >= HD)), 1.0, 0.0).astype(bf16)
    dl = dot(go_hi, pick) + dot(go_lo, pick)
    da = dl.astype(bf16)
    rest = dl - da.astype(f32)
    db = rest.astype(bf16)
    dc = (rest - db.astype(f32)).astype(bf16)
    part = lanes((n, 128))
    part = jnp.where(part >= 3, part - 3, part)
    dpack = jnp.where(part == 0, da, jnp.where(part == 1, db, dc))
    g_aug = jnp.concatenate([g, dpack], axis=1)
    qt = jnp.transpose(q)
    gt = jnp.transpose(g)
    minus = jnp.full((), -1.0, bf16)
    row = lax.broadcasted_iota(jnp.int32, (nk, 128), 0)
    k_augs, v_augs = [], []
    for h in range(2):
        head = 2 * p + h
        sel = jnp.where((lane < 48) & ((lane & 15) == head), -1.0, 0.0)
        if not causal:
            sel = jnp.where((lane == 127) & (row >= len_ref[0]), BIG, sel)
        k_augs.append(jnp.concatenate([jnp.where(first, kk, k_s) if h == 0 else jnp.where(first, k_s, kk), sel.astype(bf16)], axis=1))
        dsel = jnp.where((lane >= 3 * h) & (lane < 3 * h + 3), -1.0, 0.0).astype(bf16)
        v_m = jnp.where(first, v, zero) if h == 0 else jnp.where(first, zero, v)
        v_augs.append(jnp.concatenate([v_m, dsel], axis=1))

    def products(c, h):
        rows = slice(c * qb, (c + 1) * qb)
        top_k = (c + 1) * qb if causal else nk
        return dot(q_aug[h][rows], k_augs[h][:top_k], NT), dot(g_aug[rows], v_augs[h][:top_k], NT)

    def weigh(c, s, dp):
        w = jnp.exp2(s)
        if causal:
            r = lax.broadcasted_iota(jnp.int32, (qb, qb), 0)
            dg = jnp.where(r >= lanes((qb, qb)), w[:, c * qb:], 0.0)
            w = jnp.concatenate([w[:, :c * qb], dg], axis=1) if c else dg
        return w.astype(bf16), (w * dp).astype(bf16)

    def collect(c, h, wb, ds):
        rows = slice(c * qb, (c + 1) * qb)
        top_k = ds.shape[1]
        grow = lambda total, part: part + total if top_k == nk else jnp.concatenate([total[:, :top_k] + part, total[:, top_k:]], axis=1)
        dvts[h] = grow(dvts[h], dot(gt[h * HD:(h + 1) * HD, rows], wb))
        dkts[h] = grow(dkts[h], dot(qt[h * HD:(h + 1) * HD, rows], ds))
        dq_parts[h][c] = dot(ds, kk[:top_k])

    dkts = [jnp.zeros((HD, nk), f32)] * 2
    dvts = [jnp.zeros((HD, nk), f32)] * 2
    dq_parts = [{}, {}]
    steps = [(c, h) for h in range(2) for c in range(n // qb)]
    ahead = products(*steps[0])
    for i, (c, h) in enumerate(steps):
        s, dp = ahead
        if i + 1 < len(steps):
            ahead = products(*steps[i + 1])
        collect(c, h, *weigh(c, s, dp))
    sums = jnp.zeros((1, 128), f32)
    dqs = []
    for c in range(n // qb):
        rows = slice(c * qb, (c + 1) * qb)
        fl = lanes((qb, 128)) < HD
        dq = (jnp.where(fl, dq_parts[0][c], dq_parts[1][c]) * 0.125).astype(bf16)
        dqs.append(dq)
        sums = sums + jnp.sum(dq.astype(f32), axis=0, keepdims=True)
    dk = jnp.transpose(jnp.concatenate(dkts, axis=0)).astype(bf16)
    dv = jnp.transpose(jnp.concatenate(dvts, axis=0)).astype(bf16)
    v_sums = jnp.sum(dv.astype(f32), axis=0, keepdims=True)
    grads = (jnp.concatenate(dqs, axis=0), dk, dv)
    if not unit:
        sums_ref[...] = jnp.concatenate([sums, v_sums, jnp.zeros((6, 128), f32)], axis=0)
        for m, part in enumerate(grads):
            out_ref[m] = part
        return
    for at in range(2):
        @pl.when(pl.program_id(0) == at)
        def _(at=at):
            cols = slice(at * 128, (at + 1) * 128)
            sums_ref[:, cols] = jnp.concatenate([sums, v_sums, jnp.zeros((6, 128), f32)], axis=0)
            for m, part in enumerate(grads):
                out_ref[m, :, cols] = part

    @pl.when(pl.program_id(0) == 1)
    def _():
        joined = jnp.concatenate([out_ref[0], out_ref[1], out_ref[2]], axis=1)
        store_units(place, dot(tok_ref[...], joined, TN).astype(bf16), unit, send_ref, own_ref)
        if kind:
            rows = side_rows(kind, side, sums_ref[...])
            for ref in (send_ref, own_ref):
                for y in range(2):
                    for x in range(2):
                        for z in range(ref.shape[2]):
                            ref[y, x, z, unit:] = rows


def attn_bwd(length, q, k, v, o, g, lp, causal, first, stride, count, tokens=None, place=None, nb=0, kind="", side=(), qb=256):
    n, d = q.shape
    blk = pl.BlockSpec((n, 128), lambda p, l: (0, first + stride * p))
    ins = [blk] * 5 + [pl.BlockSpec((n, 128), lambda p, l: (0, 0))]
    outs = [pl.BlockSpec((3, n, 128), lambda p, l: (0, 0, p)), pl.BlockSpec((8, 128), lambda p, l: (0, p))]
    shapes = [pltpu.HBM((3, n, count * 128), bf16), pltpu.HBM((8, count * 128), f32)]
    args = hbm(q, k, v, o, g, lp)
    unit = 0
    if tokens is not None:
        unit = d // nb
        rows = unit + {"early": 32, "late": 16, "": 0}[kind]
        ins += [pl.BlockSpec(memory_space=pltpu.SMEM), pl.BlockSpec((n, d), lambda p, l: (0, 0))]
        ins += [pl.BlockSpec(s.shape, lambda p, l: (0, 0)) for s in side]
        args += [place] + hbm(tokens, *side)
        outs = [pl.BlockSpec((3, n, 256), lambda p, l: (0, 0, 0)), pl.BlockSpec((8, 256), lambda p, l: (0, 0))]
        outs += [pl.BlockSpec((2, 2, nb // 4, rows, 384), lambda p, l: (0, 0, 0, 0, 0))] * 2
        shapes += [pltpu.HBM((2, 2, nb // 4, rows, 384), bf16)] * 2
    return pl.pallas_call(
        functools.partial(bwd_kernel, causal=causal, qb=qb, first_pair=first, stride=stride, unit=unit, kind=kind),
        grid_spec=pltpu.PrefetchScalarGridSpec(
            num_scalar_prefetch=1, grid=(count,), in_specs=ins, out_specs=outs),
        out_shape=shapes,
        compiler_params=params(40),
        cost_estimate=cost((n + 256) * n * 2560 // (2 if causal else 1) * count * 2, 16 * n * count * 128, 2 * n * n * count),
        name="attn_bwd",
    )(length, *args)


TN = (((0,), (0,)), ((), ()))


def cost(flops, moved, exps=0):
    return pl.CostEstimate(flops=int(flops), bytes_accessed=int(moved), transcendentals=int(exps))


def params(mib):
    return pltpu.CompilerParams(vmem_limit_bytes=mib * 2**20)


def hbm(*values):
    return [pltpu.with_memory_space_constraint(v, pltpu.HBM) for v in values]


def whole():
    return pl.BlockSpec(memory_space=pltpu.VMEM)


def fixed(shape):
    return pl.BlockSpec(shape, lambda *_: (0,) * len(shape), pipeline_mode=pl.Buffered(1))


def spread_rows(block):
    return lambda i, *_: (i, 0)


def project_kernel(place, mine, got, weight, biases, *outs, step, plan):
    i = pl.program_id(0)
    x = jnp.where(i // step == place[0], mine[...], got[...])
    outs[0][...] = x
    joined = dot(x, weight[...])
    width = x.shape[1]
    for n, (bias, scale) in enumerate(plan):
        part = joined[:, n * width : (n + 1) * width]
        if bias is not None:
            part = part + biases[bias : bias + 1, :]
        if scale != 1.0:
            part = part * scale
        outs[n + 1][...] = part.astype(bf16)


def project(place, pairs, got, weight, biases, plan, rows=256):
    half, width = got.shape
    step = half // rows
    cols = weight.shape[1]
    block = pl.BlockSpec((rows, width), lambda i, p: (i, 0))
    return pl.pallas_call(
        functools.partial(project_kernel, step=step, plan=plan),
        grid_spec=pltpu.PrefetchScalarGridSpec(
            num_scalar_prefetch=1,
            grid=(2 * step,),
            in_specs=[
                pl.BlockSpec((rows, width), lambda i, p: (i % step, p[0])),
                pl.BlockSpec((rows, width), lambda i, p: (i % step, 0)),
                whole(),
                whole(),
            ],
            out_specs=[block] * (1 + len(plan)),
        ),
        out_shape=[pltpu.HBM((2 * half, width), bf16)] * (1 + len(plan)),
        compiler_params=params(32),
        cost_estimate=cost(4 * half * width * cols, 2 * width * cols + 12 * half * width),
        name="project",
    )(place, *hbm(pairs, got), weight, biases)


def norm_unit(value):
    mean = jnp.mean(value, axis=-1, keepdims=True)
    centred = value - mean
    scale = lax.rsqrt(jnp.mean(centred * centred, axis=-1, keepdims=True) + 1e-05)
    return centred * scale, scale


def norm_back(grad, unit, scale, gain):
    weighted = grad * gain
    return scale * (
        weighted
        - jnp.mean(weighted, axis=-1, keepdims=True)
        - unit * jnp.mean(weighted * unit, axis=-1, keepdims=True)
    )


def row_sum(value):
    return jnp.sum(value, axis=0, keepdims=True)


def after_self_kernel(o, tok, w_out, w_q, biases, gain, shift, unit_ref, scale_ref, low_ref, q_ref):
    resid = tok[...].astype(f32) + dot(o[...], w_out[...]) + biases[2:3, :]
    unit, scale = norm_unit(resid)
    unit_ref[...] = unit
    scale_ref[...] = jnp.broadcast_to(scale, scale_ref.shape)
    low_ = (unit * gain[0:1, :] + shift[0:1, :]).astype(bf16)
    low_ref[...] = low_
    q_ref[...] = ((dot(low_, w_q[...]) + biases[3:4, :]) * 0.125).astype(bf16)


def after_self(o, tok, w_out, w_q, biases, gain, shift, rows=256):
    n, d = o.shape
    block = pl.BlockSpec((rows, d), lambda i: (i, 0))
    return pl.pallas_call(
        after_self_kernel,
        grid=(n // rows,),
        in_specs=[block, block, whole(), whole()] + [whole()] * 3,
        out_specs=[block, pl.BlockSpec((rows, 128), lambda i: (i, 0)), block, block],
        out_shape=[
            pltpu.HBM((n, d), f32),
            pltpu.HBM((n, 128), f32),
            pltpu.HBM((n, d), bf16),
            pltpu.HBM((n, d), bf16),
        ],
        compiler_params=params(32),
        cost_estimate=cost(4 * n * d * d, 4 * d * d + 12 * n * d),
        name="after_self",
    )(*hbm(o, tok), w_out, w_q, biases, gain, shift)


RATE = 0.3275911 * 0.7071067811865476
TAIL = tuple(0.5 * c for c in (0.254829592, -0.284496736, 1.421413741, -1.453152027, 1.061405429))
DENSITY = 0.3989422804014327


def gelu_pair(v):
    size = jnp.abs(v)
    base = 1.0 + RATE * size
    t = pl.reciprocal(base, approx=True)
    t = t * (2.0 - base * t)
    poly = TAIL[4]
    for c in TAIL[3::-1]:
        poly = c + t * poly
    bell = jnp.exp2((v * v) * (-0.5 * LOG2E))
    tail = t * poly * bell
    below = jnp.where(v >= 0.0, 1.0 - tail, tail)
    return v * below, below + v * (DENSITY * bell)


def ffn_kernel(
    place, o, unit_one, cot_mine, cot_got, w_co, w_in, w_out, biases, ffn_bias, gain, shift,
    layer_ref, g2_ref, gm_ref, sums_ref, fsum_ref, grads_ref,
    slope, act_all, pre_all, b3_all, b2_all, low_turned, o_turned, *, blocks, nz,
):
    i = pl.program_id(0)
    rows, d = o.shape
    n_chunks, _, chunk = act_all.shape

    @pl.when(i == 0)
    def _():
        sums_ref[...] = jnp.zeros_like(sums_ref)
        fsum_ref[...] = jnp.zeros_like(fsum_ref)

    @pl.when(i < blocks)
    def _():
        here = pl.ds(pl.multiple_of(i * rows, rows), rows)
        o_turned[:, here] = jnp.transpose(o[...])
        normed_one = unit_one[...] * gain[0:1, :] + shift[0:1, :]
        resid = normed_one + dot(o[...], w_co[...]) + biases[5:6, :]
        unit_two, scale_two = norm_unit(resid)
        normed_two = unit_two * gain[1:2, :] + shift[1:2, :]
        low_two = normed_two.astype(bf16)
        low_turned[:, here] = jnp.transpose(low_two)

        def inner(j):
            at = slice(j * chunk, (j + 1) * chunk)
            return dot(low_two, w_in[:, at]) + ffn_bias[0:1, at]

        total = normed_two + biases[6:7, :]
        ahead = inner(0)
        for j in range(n_chunks):
            v = ahead
            if j + 1 < n_chunks:
                ahead = inner(j + 1)
            act, grad = gelu_pair(v)
            act = act.astype(bf16)
            act_all[j, here, :] = act
            slope[:, j * chunk : (j + 1) * chunk] = grad
            total = total + dot(act, w_out[j * chunk : (j + 1) * chunk, :])
        unit, scale = norm_unit(total)
        layer_ref[...] = (unit * gain[2:3, :] + shift[2:3, :]).astype(bf16)
        g = jnp.where(i // (blocks // 2) == place[0], cot_mine[...], cot_got[...]).astype(f32)
        grad_three = norm_back(g, unit, scale, gain[2:3, :])
        branch = grad_three.astype(bf16)
        b3_all[here, :] = branch
        sums_ref[0:1, :] += row_sum(g * unit)
        sums_ref[1:2, :] += row_sum(g)
        sums_ref[2:3, :] += row_sum(grad_three)

        def back(j):
            return dot(branch, w_out[j * chunk : (j + 1) * chunk, :], NT)

        total = grad_three
        ahead = back(0)
        for j in range(n_chunks):
            v = ahead
            if j + 1 < n_chunks:
                ahead = back(j + 1)
            at = slice(j * chunk, (j + 1) * chunk)
            pre = (v * slope[:, at]).astype(bf16)
            pre_all[j, here, :] = pre
            fsum_ref[0:1, at] += row_sum(pre.astype(f32))
            total = total + dot(pre, w_in[:, at], NT)
        grad_two = norm_back(total, unit_two, scale_two, gain[1:2, :])
        g2_ref[...] = grad_two
        branch = grad_two.astype(bf16)
        b2_all[here, :] = branch
        sums_ref[3:4, :] += row_sum(total * unit_two)
        sums_ref[4:5, :] += row_sum(total)
        sums_ref[5:6, :] += row_sum(grad_two)
        gm_ref[...] = dot(branch, w_co[...], NT).astype(bf16)

    @pl.when(i >= blocks)
    def _():
        z = i - blocks
        half = d // 2
        count = grads_ref.shape[1]
        unit = grads_ref.shape[2]
        value = dot(act_all[z], b3_all[...], TN).astype(bf16)
        pieces = value.shape[0] // (count * unit)
        for u in range(count):
            for c in range(pieces):
                top = (u * pieces + c) * unit
                for x in range(2):
                    grads_ref[x, u, :, c * half : (c + 1) * half] = value[top : top + unit, x * half : (x + 1) * half]
        start = pieces * half
        own = pl.ds(pl.multiple_of(z * count * unit, count * unit), count * unit)
        a = low_turned[own, :]
        for j in range(n_chunks):
            value = dot(a, pre_all[j]).astype(bf16)
            x, left = divmod(j, n_chunks // 2)
            for u in range(count):
                grads_ref[x, u, :, start + left * chunk : start + (left + 1) * chunk] = value[u * unit : (u + 1) * unit]
        start += n_chunks // 2 * chunk
        value = dot(o_turned[own, :], b2_all[...]).astype(bf16)
        for u in range(count):
            for x in range(2):
                grads_ref[x, u, :, start : start + half] = value[u * unit : (u + 1) * unit, x * half : (x + 1) * half]


def ffn(place, o, unit_one, cot_pairs, cot_got, w_co, w_in, w_out, biases, ffn_bias, gain, shift, nb, rows=256):
    n, d = o.shape
    ff = w_in.shape[1]
    blocks = n // rows
    nz = ff // d
    unit = d // nb
    at = lambda i: jnp.minimum(i, blocks - 1)
    block = pl.BlockSpec((rows, d), lambda i, p: (at(i), 0))
    width = ff + d // 2
    scratch = [
        pltpu.VMEM((rows, ff), f32),
        pltpu.VMEM((nz, n, d), bf16),
        pltpu.VMEM((nz, n, d), bf16),
        pltpu.VMEM((n, d), bf16),
        pltpu.VMEM((n, d), bf16),
        pltpu.VMEM((d, n), bf16),
        pltpu.VMEM((d, n), bf16),
    ]
    return pl.pallas_call(
        functools.partial(ffn_kernel, blocks=blocks, nz=nz),
        grid_spec=pltpu.PrefetchScalarGridSpec(
            num_scalar_prefetch=1,
            grid=(blocks + nz,),
            in_specs=[
                block,
                block,
                pl.BlockSpec((rows, d), lambda i, p: (at(i) % (blocks // 2), p[0])),
                pl.BlockSpec((rows, d), lambda i, p: (at(i) % (blocks // 2), 0)),
            ] + [whole()] * 7,
            out_specs=[
                block,
                block,
                block,
                pl.BlockSpec((8, d), lambda i, p: (0, 0)),
                pl.BlockSpec((8, ff), lambda i, p: (0, 0)),
                pl.BlockSpec((2, nb // nz, unit, width), lambda i, p: (0, jnp.maximum(i - blocks, 0), 0, 0)),
            ],
            scratch_shapes=scratch,
        ),
        out_shape=[
            pltpu.HBM((n, d), bf16),
            pltpu.HBM((n, d), f32),
            pltpu.HBM((n, d), bf16),
            pltpu.HBM((8, d), f32),
            pltpu.HBM((8, ff), f32),
            pltpu.HBM((2, nb, unit, width), bf16),
        ],
        compiler_params=params(60),
        cost_estimate=cost(12 * n * d * ff + 6 * n * d * d, 8 * d * ff + 20 * n * d, 2 * n * ff),
        name="ffn",
    )(place, *hbm(o, unit_one, cot_pairs, cot_got), w_co, w_in, w_out, biases, ffn_bias, gain, shift)


def store_units(place, value, unit, send_ref, own_ref, first=0, z_local=False):
    mx, mz, my, core = place[0], place[1], place[2], place[3]
    half = value.shape[1] // 2
    for mine in range(2):
        @pl.when(core == mine)
        def _():
            for u in range(value.shape[0] // unit):
                ref = own_ref if u % 2 == mine else send_ref
                z = 0 if z_local else jnp.bitwise_xor(u // 4, mz)
                y = jnp.bitwise_xor((u // 2) % 2, my)
                for x in range(2):
                    ref[y, jnp.bitwise_xor(x, mx), z, :unit] = value[u * unit : (u + 1) * unit, x * half : (x + 1) * half]


def middle_kernel(
    place, g2, unit_ref, scale_ref, grad_a, grad_b, out_self, low_one, sources, w_q, w_out, w_kv, gain,
    g1_ref, gm_ref, sums_ref, other_ref, mine_ref, send_ref, own_ref, gq_all, b1_all, *, blocks, unit,
):
    i = pl.program_id(0)
    rows, d = g2.shape

    @pl.when(i == 0)
    def _():
        sums_ref[...] = jnp.zeros_like(sums_ref)

    @pl.when(i < blocks)
    def _():
        half = blocks // 2
        mine = i >= half
        at = jnp.where(mine, place[0] * half + i - half, (1 - place[0]) * half + i)
        here = pl.ds(pl.multiple_of(at * rows, rows), rows)
        gq = jnp.concatenate([grad_a[0, here, :], grad_b[0, here, :]], axis=1)
        gq_all[here, :] = gq
        g = g2[...] + dot(gq, w_q[...], NT)
        unit_one = unit_ref[...]
        grad = norm_back(g, unit_one, scale_ref[:, 0:1], gain[0:1, :])
        g1_ref[...] = grad
        branch = grad.astype(bf16)
        b1_all[here, :] = branch
        sums_ref[0:1, :] += row_sum(g * unit_one)
        sums_ref[1:2, :] += row_sum(g)
        sums_ref[2:3, :] += row_sum(grad)
        gm_ref[...] = dot(branch, w_out[...], NT).astype(bf16)
        pair = jnp.concatenate([r[m, here, :] for m in (1, 2) for r in (grad_a, grad_b)], axis=1)
        value = dot(pair, w_kv[...], NT)

        @pl.when(mine)
        def _():
            mine_ref[...] = value

        @pl.when(jnp.logical_not(mine))
        def _():
            other_ref[...] = value.astype(bf16)

    def store(value):
        store_units(place, value.astype(bf16), unit, send_ref, own_ref)

    @pl.when(i == blocks)
    def _():
        store(dot(out_self[...], b1_all[...], TN))

    @pl.when(i == blocks + 1)
    def _():
        store(dot(low_one[...], gq_all[...], TN))

    for step, grads in ((2, grad_a), (3, grad_b)):
        @pl.when(i == blocks + step)
        def _(grads=grads):
            store(dot(sources[...], jnp.concatenate([grads[1], grads[2]], axis=1), TN))


def middle(place, g2, unit_one, scale, grad_a, grad_b, out_self, low_one, sources, w_q, w_out, w_kv, gain, nb, rows=256):
    n, d = g2.shape
    blocks = n // rows
    unit = d // nb
    half = blocks // 2

    def block_at(i, p):
        i = jnp.minimum(i, blocks - 1)
        return (jnp.where(i < half, (1 - p[0]) * half + i, p[0] * half + i - half), 0)

    block = pl.BlockSpec((rows, d), block_at)
    fixed_block = lambda shape: pl.BlockSpec(shape, lambda i, p: (0,) * len(shape), pipeline_mode=pl.Buffered(1))
    piece = pl.BlockSpec((2, 2, nb // 4, unit, d // 2), lambda i, p: (0, 0, 0, 0, jnp.maximum(i - blocks, 0)))
    big = pltpu.HBM((2, 2, nb // 4, unit, 2 * d), bf16)
    return pl.pallas_call(
        functools.partial(middle_kernel, blocks=blocks, unit=unit),
        grid_spec=pltpu.PrefetchScalarGridSpec(
            num_scalar_prefetch=1,
            grid=(blocks + 4,),
            in_specs=[block, block, pl.BlockSpec((rows, 128), block_at), fixed_block(grad_a.shape), fixed_block(grad_b.shape)]
            + [fixed_block((n, d))] * 3 + [whole()] * 4,
            out_specs=[
                block,
                block,
                pl.BlockSpec((8, d), lambda i, p: (0, 0)),
                pl.BlockSpec((rows, d), lambda i, p: (jnp.minimum(i, half - 1), 0)),
                pl.BlockSpec((rows, d), lambda i, p: (jnp.clip(i - half, 0, half - 1), 0)),
                piece,
                piece,
            ],
            scratch_shapes=[pltpu.VMEM((n, d), bf16), pltpu.VMEM((n, d), bf16)],
        ),
        out_shape=[
            pltpu.HBM((n, d), f32),
            pltpu.HBM((n, d), bf16),
            pltpu.HBM((8, d), f32),
            pltpu.HBM((n // 2, d), bf16),
            pltpu.HBM((n // 2, d), f32),
            big,
            big,
        ],
        compiler_params=params(48),
        cost_estimate=cost(16 * n * d * d, 40 * n * d),
        name="middle",
    )(place, *hbm(g2, unit_one, scale, grad_a, grad_b, out_self, low_one, sources), w_q, w_out, w_kv, gain)


def grad_rows_kernel(place, *refs, columns, based):
    gs, weight = refs[: len(columns)], refs[len(columns)]
    out_ref = refs[-1]
    value = None
    for g, chunks in zip(gs, columns):
        for m, starts in enumerate(chunks):
            if not starts:
                continue
            w = [weight[:, s : s + size] for s, size in starts]
            w = w[0] if len(w) == 1 else jnp.concatenate(w, axis=1)
            term = dot(g[m], w, NT)
            value = term if value is None else value + term
    if based:
        value = value + refs[len(columns) + 1][...]

    out_ref[...] = value.astype(out_ref.dtype)


def grad_rows(place, terms, columns, weight, base, mine, rows=256):
    n = terms[0].shape[1]
    d, k = weight.shape
    steps = n // 2 // rows
    half = lambda i, p: (p[0] if mine else 1 - p[0]) * steps + i
    ins = [pl.BlockSpec((t.shape[0], rows, t.shape[2]), lambda i, p: (0, half(i, p), 0)) for t in terms] + [whole()]
    args = hbm(*terms) + [weight]
    if base is not None:
        ins.append(pl.BlockSpec((rows, d), lambda i, p: (half(i, p), 0)))
        args += hbm(base)
    return pl.pallas_call(
        functools.partial(grad_rows_kernel, columns=columns, based=base is not None),
        grid_spec=pltpu.PrefetchScalarGridSpec(
            num_scalar_prefetch=1,
            grid=(steps,),
            in_specs=ins,
            out_specs=pl.BlockSpec((rows, d), lambda i, p: (i, 0)),
        ),
        out_shape=pltpu.HBM((n // 2, d), f32 if mine else bf16),
        compiler_params=params(40),
        cost_estimate=cost(n * k * d, n * k + 2 * k * d + 4 * n * d),
        name="grad_rows",
    )(place, *args)


def route(nb, move):
    dz, dy, dc, dx = move
    pairs = []
    for b in range(nb):
        z, y, core = b // 4, (b // 2) % 2, b % 2
        for x in range(2):
            target = (z ^ dz) * 4 + (y ^ dy) * 2 + (core ^ dc)
            pairs.append((b * 2 + x, target * 2 + (x ^ dx)))
    return pairs


def send(value, nb, move):
    return lax.ppermute(value, ("z", "y", "core", "seq"), route(nb, move))


def core_stage(buffers, nb):
    to_send, own = buffers
    return own, send(to_send, nb, (0, 0, 1, 0))


def y_prepare(state):
    own, got = state
    return (own[1].astype(f32) + got[1].astype(f32)).astype(bf16), (own, got)


def y_move(value, nb):
    return send(value, nb, (0, 1, 0, 0))


def x_prepare(state):
    own, got, more = state
    total = own[0].astype(f32) + got[0].astype(f32) + more.astype(f32)
    return total[0].astype(bf16), total[1].astype(bf16)


def x_move(value, nb):
    return send(value, nb, (0, 0, 0, 1))


def z_prepare(state):
    kept, got = state
    total = kept.astype(f32) + got.astype(f32)
    return total[0::2].astype(bf16), total[1::2].astype(bf16)


def z_move(value, nb, bit):
    return send(value, nb, (1 << bit, 0, 0, 0))


def halves_first(state):
    own, got = state
    h = own.shape[2] // 2
    over_y = own[1, :, :h].astype(f32) + got[1, :, :h].astype(f32)
    over_x = own[:, 1, h:].astype(f32) + got[:, 1, h:].astype(f32)
    return over_y.astype(bf16), over_x.astype(bf16)


def halves_move(values, nb, turn):
    a, b = ((0, 0, 0, 1), (0, 1, 0, 0)) if turn else ((0, 1, 0, 0), (0, 0, 0, 1))
    return send(values[0], nb, a), send(values[1], nb, b)


def halves_second(state):
    (own, got), (from_y, from_x) = state
    h = own.shape[2] // 2
    a = own[0, :, :h].astype(f32) + got[0, :, :h].astype(f32) + from_y.astype(f32)
    b = own[:, 0, h:].astype(f32) + got[:, 0, h:].astype(f32) + from_x.astype(f32)
    return (a[0].astype(bf16), b[0].astype(bf16)), (a[1].astype(bf16), b[1].astype(bf16))


def halves_third(state):
    kept, got = state
    total = jnp.concatenate([k.astype(f32) + g.astype(f32) for k, g in zip(kept, got)], axis=0)
    return total[0::2].astype(bf16), total[1::2].astype(bf16)


def after_y(state):
    own, got, more = state
    return (own[0].astype(f32) + got[0].astype(f32) + more.astype(f32)).astype(bf16)


def direct_z(total, nb):
    result = total[:, 0].astype(f32)
    for d in range(1, nb // 4):
        result = result + send(total[:, d], nb, (d, 0, 0, 0)).astype(f32)
    return result


def at(value, index, axis):
    return lax.dynamic_index_in_dim(value, index, axis, keepdims=False)


def last_stage(state):
    kept, got = state
    return (kept.astype(f32) + got.astype(f32))[0]


def last_part(state, start, end):
    kept, got = state
    return (kept[:, :, start:end].astype(f32) + got[:, :, start:end].astype(f32))[0]


def tie(*values):
    return lax.optimization_barrier(values)


def swap(value):
    return lax.ppermute(value, "seq", [(0, 1), (1, 0)])


def split_pairs(local):
    positions, _, width = local.shape
    pairs = local.reshape(positions, 2 * width)
    x = lax.axis_index("seq")
    return pairs, lax.dynamic_slice(pairs, (0, (1 - x) * width), (positions, width))


def join_pairs(mine, got):
    x = lax.axis_index("seq")
    got = got.astype(mine.dtype)
    both = jnp.concatenate([jnp.where(x == 0, mine, got), jnp.where(x == 0, got, mine)], axis=1)
    return both.reshape(mine.shape[0], 2, mine.shape[1])


def per_device_fast(
    hidden_in,
    memory,
    src_len,
    out_grad,
    w_self_qkv,
    w_self_out,
    w_cross_q,
    w_cross_kv,
    w_cross_out,
    w_ffn_in,
    w_ffn_out,
    biases,
    ffn_bias,
    norm_gain,
    norm_shift,
):
    nb = lax.axis_size(("z", "y", "core"))
    width = hidden_in.shape[2]
    half = width // 2
    x, b = lax.axis_index("seq"), lax.axis_index(("z", "y", "core"))
    place = jnp.stack([x, b // 4, (b // 2) % 2, b % 2]).astype(jnp.int32)
    length = lax.dynamic_slice_in_dim(src_len, x, 1)

    pairs, other = split_pairs(hidden_in)
    got = swap(other)
    memory_pairs, memory_other = split_pairs(memory)
    memory_got = swap(memory_other)
    cot_pairs, cot_other = split_pairs(out_grad)
    tokens, query_self, key_self, value_self = project(
        place, pairs, got, w_self_qkv, biases, ((0, 0.125), (None, 1.0), (1, 1.0))
    )
    query_self, cot_other = tie(query_self, cot_other)
    cot_got = swap(cot_other)
    out_self, lp_self = attn_fwd(length, query_self, key_self, value_self, True)
    unit_one, scale_one, low_one, query_cross = after_self(
        out_self, tokens, w_self_out, w_cross_q, biases, norm_gain, norm_shift
    )
    sources, key_cross, value_cross = project(
        place, memory_pairs, memory_got, w_cross_kv, biases, ((None, 1.0), (4, 1.0))
    )
    out_cross, lp_cross = attn_fwd(length, query_cross, key_cross, value_cross, False)
    layer, grad_two, grad_mixed, sums_ffn, bias_sums, one = ffn(
        place, out_cross, unit_one, cot_pairs, cot_got, w_cross_out, w_ffn_in, w_ffn_out, biases, ffn_bias[None], norm_gain, norm_shift, nb
    )
    span = layer.shape[0] // 2

    ff = w_ffn_in.shape[1]
    layer_other = lax.dynamic_slice_in_dim(layer, (1 - x) * span, span, 0)
    one, layer_other, grad_mixed = tie(one, layer_other, grad_mixed)
    one = lax.psum_scatter(one.reshape(-1, one.shape[-1]), ("seq", "z", "y", "core"), scatter_dimension=0, tiled=True)
    layer_got = swap(layer_other)
    back = partial(attn_bwd, length, query_cross, key_cross, value_cross, out_cross)
    cross_a, sums_ca = back(grad_mixed, lp_cross, False, 0, 1, 3)

    cross_a, grad_mixed, layer_got = tie(cross_a, grad_mixed, layer_got)
    cross_b, sums_cb = back(grad_mixed, lp_cross, False, 3, 1, 3)

    grad_one, grad_mixed, sums_one, other, memory_mine, *three = middle(
        place, grad_two, unit_one, scale_one, cross_a, cross_b, out_self, low_one, sources,
        w_cross_q, w_self_out, w_cross_kv, norm_gain, nb,
    )

    three, other, grad_mixed = tie(three, other, grad_mixed)
    three = core_stage(three, nb)
    cut = span * 5 // 8
    memory_back = swap(other[:cut])
    memory_rest = other[cut:]
    back = partial(attn_bwd, length, query_self, key_self, value_self, out_self)
    self_a, sums_sa, *four = back(
        grad_mixed, lp_self, True, 0, 3, 2, tokens, place, nb, "early", (sums_one, sums_ca, sums_cb, sums_ffn, bias_sums)
    )

    four, three, grad_mixed, memory_back = tie(four, three, grad_mixed, memory_back)
    four = core_stage(four, nb)
    three_out = halves_first(three)
    three_out, grad_mixed = tie(three_out, grad_mixed)
    three = three, halves_move(three_out, nb, False)
    self_b, sums_sb, *five = back(grad_mixed, lp_self, True, 1, 3, 2, tokens, place, nb)

    five, four, three, grad_mixed = tie(five, four, three, grad_mixed)
    five = core_stage(five, nb)
    four_out, four = y_prepare(four)
    three_keep, three_out = halves_second(three)
    four_out, three_out, grad_mixed, memory_rest = tie(four_out, three_out, grad_mixed, memory_rest)
    memory_rest = swap(memory_rest)
    three = three_keep, halves_move(three_out, nb, True)
    self_c, sums_sc, *six = back(grad_mixed, lp_self, True, 2, 3, 2, tokens, place, nb, "late", (sums_sa, sums_sb))

    self_c, six, five, three, memory_rest = tie(self_c, six, five, three, memory_rest)
    six = core_stage(six, nb)
    five_out, five = y_prepare(five)
    three_keep, three_out = halves_third(three)
    five_out, three_out, self_c = tie(five_out, three_out, self_c)
    four = four + (y_move(four_out, nb),)
    five = five + (y_move(five_out, nb),)
    three = three_keep, z_move(three_out, nb, 0)
    spots = [tuple(tuple((m * width + (i + s) * 128, 128) for s in (0, 3)) for m in range(3)) for i in range(3)]
    other = grad_rows(place, [self_a, self_b, self_c], spots, w_self_qkv, grad_one, False)

    other, six, three, grad_one = tie(other, six, three, grad_one)
    six_out, six = y_prepare(six)
    three_keep, three_out = z_prepare(three)
    six_out, other, three_out, grad_one = tie(six_out, other, three_out, grad_one)
    six = six + (y_move(six_out, nb),)
    three = three_keep, z_move(three_out, nb, 1)
    in_back = swap(other)
    mine = grad_rows(place, [self_a, self_b, self_c], spots, w_self_qkv, grad_one, True)

    mine, five, four, layer_got, one = tie(mine, five, four, layer_got, one)
    layer_out = join_pairs(lax.dynamic_slice_in_dim(layer, x * span, span, 0), layer_got)
    layer_out, mine, six, five, three, memory_back = tie(layer_out, mine, six, five, three, memory_back)
    both = jnp.concatenate([after_y(six), after_y(five), after_y(four)], axis=2)
    both, memory_back = tie(both, memory_back)
    moved = [send(both[:, d], nb, (d, 0, 0, 0)) for d in range(1, nb // 4)]
    grad_memory = join_pairs(memory_mine, jnp.concatenate([memory_back, memory_rest]))
    grad_memory, moved, one = tie(grad_memory, moved, one)
    both = both[:, 0].astype(f32)
    for value in moved:
        both = both + value.astype(f32)
    last = both[1].astype(bf16)
    last, one, in_back = tie(last, one, in_back)
    last = x_move(last, nb)
    grad_in = join_pairs(mine, in_back)
    one = one.astype(f32)
    pieces = ff // width
    grad_ffn_out = jnp.concatenate([one[:, c * half : (c + 1) * half] for c in range(pieces)], axis=0)
    grad_ffn_in = one[:, pieces * half :]
    group = [last_part(three, c * half, e * half) for c, e in ((0, 1), (1, 2), (2, 4))]
    last, grad_in, grad_ffn_in, grad_ffn_out, group = tie(last, grad_in, grad_ffn_in, grad_ffn_out, group)
    both = both[0] + last.astype(f32)
    unit = width // nb
    tops = 0, unit + 16, 2 * unit + 16
    thirds = [both[top : top + unit].reshape(unit, 3, 128) for top in tops[::-1]]
    grad_self_qkv = jnp.stack(thirds, axis=2).reshape(unit, 9 * 128)
    late = both[unit : unit + 6, :256].reshape(3, 2, 2, 128)
    late = at(late, x, 2).swapaxes(0, 1).reshape(2, half)
    early = lax.dynamic_slice_in_dim(both[3 * unit + 16 :], x * 16, 16, 0)
    vectors = jnp.concatenate([late, early[:11]])
    bias_total = early[11 : 11 + bias_sums.shape[1] // width].reshape(-1)
    return (
        layer_out,
        grad_in,
        grad_memory,
        grad_self_qkv,
        group[0],
        group[1],
        group[2],
        grad_ffn_in[:, -half:],
        grad_ffn_in[:, :-half],
        grad_ffn_out,
        vectors[0:7],
        bias_total,
        vectors[7:10],
        vectors[10:13],
    )


def solution(mesh):
    devices = dict(mesh.shape)

    in_specs = (
        P("seq", "batch", None),
        P("seq", "batch", None),
        P("batch"),
        P("seq", "batch", None),
        P(),
        P(),
        P(),
        P(),
        P(),
        P(),
        P(),
        P(),
        P(),
        P(),
        P(),
    )
    out_specs = (
        P("seq", "batch", None),
        P("seq", "batch", None),
        P("seq", "batch", None),
        P("batch", "seq"),
        P("batch", "seq"),
        P("batch", "seq"),
        P("batch", "seq"),
        P("batch", "seq"),
        P("batch", "seq"),
        P("batch", "seq"),
        P(None, "seq"),
        P("seq"),
        P(None, "seq"),
        P(None, "seq"),
    )
    nb, ns = devices["batch"], devices["seq"]

    def program(hidden_in, *rest):
        whole = ns == 2 and hidden_in.shape[1] == 2 * nb and nb % 8 == 0 and nb & (nb - 1) == 0
        if not whole:
            general = jax.shard_map(
                per_device_general, mesh=mesh, in_specs=in_specs, out_specs=out_specs, check_vma=False
            )
            return general(hidden_in, *rest)
        parts = jax.sharding.Mesh(mesh.devices.reshape(nb // 4, 2, 2, ns), ("z", "y", "core", "seq"))
        split = lambda spec: P(*(("z", "y", "core") if axis == "batch" else axis for axis in spec))
        fast = jax.shard_map(
            per_device_fast,
            mesh=parts,
            in_specs=tuple(split(spec) for spec in in_specs),
            out_specs=tuple(split(spec) for spec in out_specs),
            check_vma=False,
        )
        return fast(hidden_in, *rest)

    return program
```

```python
import functools
from functools import partial

import jax
import jax.numpy as jnp
from jax import lax
from jax.experimental import pallas as pl
from jax.experimental.pallas import tpu as pltpu
from jax.sharding import PartitionSpec as P

H = 12


NEGATIVE = -1e30


def from_behind(value, axis, steps):
    count = lax.axis_size(axis)
    pairs = [(source, (source + steps) % count) for source in range(count)]
    return lax.ppermute(value, axis, pairs)


def shifted(block, axis, distance):
    devices = range(lax.axis_size(axis))
    route = [(i - distance, i) for i in devices if i - distance in devices]
    return lax.ppermute(block, axis, route)


def contract_rows(left, right):
    return lax.dot_general(
        left, right, (((0,), (0,)), ((), ())), preferred_element_type=jnp.float32
    )


def times_transposed(grad, weight):
    return lax.dot_general(
        grad, weight, (((1,), (1,)), ((), ())), preferred_element_type=jnp.float32
    )


def norm_forward(value, gain, shift):
    mean = jnp.mean(value, axis=-1, keepdims=True)
    centred = value - mean
    scale = lax.rsqrt(jnp.mean(centred * centred, axis=-1, keepdims=True) + 1e-05)
    unit = centred * scale
    return (unit * gain + shift, unit, scale)


def norm_backward(grad, unit, scale, gain):
    weighted = grad * gain
    inner = (
        weighted
        - jnp.mean(weighted, axis=-1, keepdims=True)
        - unit * jnp.mean(weighted * unit, axis=-1, keepdims=True)
    )
    return (scale * inner, jnp.sum(grad * unit, axis=0), jnp.sum(grad, axis=0))


def allowed_keys(query_pos, key_pos, lengths, causal):
    if causal:
        return (query_pos[:, None] >= key_pos[None, :])[None, None]
    return (key_pos[None, :] < lengths[:, None])[:, None, None, :]


def attend_forward(query, keys, values, lengths, causal, heads):
    span, batch, width = query.shape
    size = width // heads
    query_heads = query.reshape(span, batch, heads, size)
    query_pos = lax.axis_index("seq") * span + lax.iota(jnp.int32, span)

    def block(carry, key_block, value_block, first):
        previous, total, summed = carry
        rows = key_block.shape[0]
        key_pos = first + lax.iota(jnp.int32, rows)
        scores = jnp.einsum(
            "qshd,kshd->shqk",
            query_heads,
            key_block.reshape(rows, batch, heads, size),
            preferred_element_type=jnp.float32,
        )
        allowed = allowed_keys(query_pos, key_pos, lengths, causal)
        top = jnp.maximum(previous, jnp.max(jnp.where(allowed, scores, NEGATIVE), axis=-1))
        weights = jnp.where(allowed, jnp.exp(scores - top[..., None]), 0.0)
        rescale = jnp.exp(previous - top)
        total = total * rescale + jnp.sum(weights, axis=-1)
        summed = summed * rescale[..., None] + jnp.einsum(
            "shqk,kshd->shqd",
            weights.astype(jnp.bfloat16),
            value_block.reshape(rows, batch, heads, size),
            preferred_element_type=jnp.float32,
        )
        return (top, total, summed)

    def fold(carry, piece):
        key_piece, value_piece = piece
        rows = key_piece.shape[0]
        count = rows // span
        firsts = span * lax.iota(jnp.int32, count)

        def inner(state, parts):
            return (block(state, parts[0], parts[1], parts[2]), None)

        carry, unused = lax.scan(
            inner,
            carry,
            (
                key_piece.reshape(count, span, batch, width),
                value_piece.reshape(count, span, batch, width),
                firsts,
            ),
        )
        return carry

    empty = (
        jnp.full((batch, heads, span), NEGATIVE, jnp.float32),
        jnp.zeros((batch, heads, span), jnp.float32),
        jnp.zeros((batch, heads, span, size), jnp.float32),
    )
    if causal:
        top, total, summed = fold(
            empty,
            (
                lax.all_gather(keys, "seq", axis=0, tiled=True),
                lax.all_gather(values, "seq", axis=0, tiled=True),
            ),
        )
    else:
        top, total, summed = fold(
            empty,
            (
                lax.all_gather(keys, "seq", axis=0, tiled=True),
                lax.all_gather(values, "seq", axis=0, tiled=True),
            ),
        )
    mixed = summed / total[..., None]
    mixed = jnp.transpose(mixed, (2, 0, 1, 3)).reshape(span, batch, width)
    return (mixed, top + jnp.log(total))


def block_backward(
    query_heads, grad_heads, delta, logsum, key_block, value_block, allowed, batch, heads, size
):
    span = key_block.shape[0]
    width = heads * size
    key_heads = key_block.reshape(span, batch, heads, size)
    value_heads = value_block.reshape(span, batch, heads, size)
    scores = jnp.einsum(
        "qshd,kshd->shqk", query_heads, key_heads, preferred_element_type=jnp.float32
    )
    weights = jnp.where(allowed, jnp.exp(scores - logsum[..., None]), 0.0)
    grad_weights = jnp.einsum(
        "qshd,kshd->shqk", grad_heads, value_heads, preferred_element_type=jnp.float32
    )
    grad_scores = (weights * (grad_weights - delta[..., None])).astype(jnp.bfloat16)
    grad_query = jnp.einsum(
        "shqk,kshd->qshd", grad_scores, key_heads, preferred_element_type=jnp.float32
    )
    grad_keys = jnp.einsum(
        "shqk,qshd->kshd", grad_scores, query_heads, preferred_element_type=jnp.float32
    ).reshape(span, batch, width)
    grad_values = jnp.einsum(
        "shqk,qshd->kshd",
        weights.astype(jnp.bfloat16),
        grad_heads,
        preferred_element_type=jnp.float32,
    ).reshape(span, batch, width)
    return (grad_query, grad_keys, grad_values)


def attend_backward(query, keys, values, mixed, grad_mixed, logsum, lengths, causal, heads):
    span, batch, width = query.shape
    size = width // heads
    query_heads = query.reshape(span, batch, heads, size)
    grad_heads = grad_mixed.reshape(span, batch, heads, size)
    delta = jnp.sum(
        grad_heads.astype(jnp.float32) * mixed.reshape(span, batch, heads, size), axis=-1
    )
    delta = jnp.transpose(delta, (1, 2, 0))
    devices = lax.axis_size("seq")
    place = lax.axis_index("seq")
    query_pos = place * span + lax.iota(jnp.int32, span)
    grad_query = jnp.zeros((span, batch, heads, size), jnp.float32)
    grad_keys = jnp.zeros((span, batch, width), jnp.float32)
    grad_values = jnp.zeros((span, batch, width), jnp.float32)
    key_block, value_block = (keys, values)
    for step in range(devices):
        owner = (place - step + devices) % devices
        key_pos = owner * span + lax.iota(jnp.int32, span)
        allowed = allowed_keys(query_pos, key_pos, lengths, causal)
        part_query, part_keys, part_values = block_backward(
            query_heads,
            grad_heads,
            delta,
            logsum,
            key_block,
            value_block,
            allowed,
            batch,
            heads,
            size,
        )
        grad_query = grad_query + part_query
        grad_keys = grad_keys + part_keys
        grad_values = grad_values + part_values
        if causal:
            grad_keys, grad_values = (
                from_behind(grad_keys.astype(jnp.bfloat16), "seq", 1).astype(grad_keys.dtype),
                from_behind(grad_values.astype(jnp.bfloat16), "seq", 1).astype(grad_values.dtype),
            )
        else:
            grad_keys, grad_values = (
                from_behind(grad_keys.astype(jnp.bfloat16), "seq", 1).astype(grad_keys.dtype),
                from_behind(grad_values.astype(jnp.bfloat16), "seq", 1).astype(grad_values.dtype),
            )
        if step + 1 < devices:
            if causal:
                key_block, value_block = shifted((key_block, value_block), "seq", 1)
            else:
                key_block, value_block = from_behind((key_block, value_block), "seq", 1)
    return (grad_query.reshape(span, batch, width), grad_keys, grad_values)


def per_device_general(
    hidden_in,
    memory,
    src_len,
    out_grad,
    w_self_qkv,
    w_self_out,
    w_cross_q,
    w_cross_kv,
    w_cross_out,
    w_ffn_in,
    w_ffn_out,
    biases,
    ffn_bias,
    norm_gain,
    norm_shift,
):
    span, batch, width = hidden_in.shape
    heads = H
    rows = span * batch
    layout = (span, batch, width)
    tokens = hidden_in.reshape(rows, width)
    sources = memory.reshape(rows, width)
    joined = jnp.dot(tokens, w_self_qkv, preferred_element_type=jnp.float32)
    query_self = ((joined[:, :width] + biases[0]) * 0.125).astype(jnp.bfloat16)
    key_self = joined[:, width : 2 * width].astype(jnp.bfloat16)
    value_self = (joined[:, 2 * width :] + biases[1]).astype(jnp.bfloat16)
    mixed_self, logsum_self = attend_forward(
        query_self.reshape(layout),
        key_self.reshape(layout),
        value_self.reshape(layout),
        src_len,
        True,
        heads,
    )
    out_self = mixed_self.reshape(rows, width).astype(jnp.bfloat16)
    resid_one = (
        tokens.astype(jnp.float32)
        + jnp.dot(out_self, w_self_out, preferred_element_type=jnp.float32)
        + biases[2]
    )
    normed_one, unit_one, scale_one = norm_forward(resid_one, norm_gain[0], norm_shift[0])
    normed_one_low = normed_one.astype(jnp.bfloat16)
    query_cross = (
        (jnp.dot(normed_one_low, w_cross_q, preferred_element_type=jnp.float32) + biases[3]) * 0.125
    ).astype(jnp.bfloat16)
    pair = jnp.dot(sources, w_cross_kv, preferred_element_type=jnp.float32)
    key_cross = pair[:, :width].astype(jnp.bfloat16)
    value_cross = (pair[:, width:] + biases[4]).astype(jnp.bfloat16)
    mixed_cross, logsum_cross = attend_forward(
        query_cross.reshape(layout),
        key_cross.reshape(layout),
        value_cross.reshape(layout),
        src_len,
        False,
        heads,
    )
    out_cross = mixed_cross.reshape(rows, width).astype(jnp.bfloat16)
    resid_two = (
        normed_one + jnp.dot(out_cross, w_cross_out, preferred_element_type=jnp.float32) + biases[5]
    )
    normed_two, unit_two, scale_two = norm_forward(resid_two, norm_gain[1], norm_shift[1])
    normed_two_low = normed_two.astype(jnp.bfloat16)
    inner = jnp.dot(normed_two_low, w_ffn_in, preferred_element_type=jnp.float32) + ffn_bias
    active = jax.nn.gelu(inner, approximate=False).astype(jnp.bfloat16)
    resid_three = (
        normed_two + jnp.dot(active, w_ffn_out, preferred_element_type=jnp.float32) + biases[6]
    )
    result, unit_three, scale_three = norm_forward(resid_three, norm_gain[2], norm_shift[2])
    layer_out = result.astype(jnp.bfloat16).reshape(layout)
    grad_three, gain_three, shift_three = norm_backward(
        out_grad.reshape(rows, width).astype(jnp.float32), unit_three, scale_three, norm_gain[2]
    )
    branch_three = grad_three.astype(jnp.bfloat16)
    hidden_pre, hidden_act = (inner, active)
    grad_ffn_out = contract_rows(hidden_act, branch_three)
    grad_act = times_transposed(branch_three, w_ffn_out)
    unused, pull = jax.vjp(partial(jax.nn.gelu, approximate=False), hidden_pre)
    grad_pre = pull(grad_act)[0].astype(jnp.bfloat16)
    grad_ffn_in = contract_rows(normed_two_low, grad_pre)
    grad_normed_two = grad_three + times_transposed(grad_pre, w_ffn_in)
    grad_two, gain_two, shift_two = norm_backward(
        grad_normed_two, unit_two, scale_two, norm_gain[1]
    )
    branch_two = grad_two.astype(jnp.bfloat16)
    grad_cross_out = contract_rows(out_cross, branch_two)
    grad_mixed_cross = times_transposed(branch_two, w_cross_out).astype(jnp.bfloat16)
    raw_query, grad_keys, grad_values = attend_backward(
        query_cross.reshape(layout),
        key_cross.reshape(layout),
        value_cross.reshape(layout),
        mixed_cross,
        grad_mixed_cross.reshape(layout),
        logsum_cross,
        src_len,
        False,
        heads,
    )
    grad_query_cross = (raw_query.reshape(rows, width) * 0.125).astype(jnp.bfloat16)
    grad_pair = jnp.concatenate(
        [
            grad_keys.reshape(rows, width).astype(jnp.bfloat16),
            grad_values.reshape(rows, width).astype(jnp.bfloat16),
        ],
        axis=1,
    )
    grad_cross_q = contract_rows(normed_one_low, grad_query_cross)
    grad_cross_kv = contract_rows(sources, grad_pair)
    grad_memory = times_transposed(grad_pair, w_cross_kv).reshape(layout)
    grad_normed_one = grad_two + times_transposed(grad_query_cross, w_cross_q)
    grad_one, gain_one, shift_one = norm_backward(
        grad_normed_one, unit_one, scale_one, norm_gain[0]
    )
    branch_one = grad_one.astype(jnp.bfloat16)
    grad_self_out = contract_rows(out_self, branch_one)
    grad_mixed_self = times_transposed(branch_one, w_self_out).astype(jnp.bfloat16)
    raw_query, grad_keys, grad_values = attend_backward(
        query_self.reshape(layout),
        key_self.reshape(layout),
        value_self.reshape(layout),
        mixed_self,
        grad_mixed_self.reshape(layout),
        logsum_self,
        src_len,
        True,
        heads,
    )
    grad_joined = jnp.concatenate(
        [
            (raw_query.reshape(rows, width) * 0.125).astype(jnp.bfloat16),
            grad_keys.reshape(rows, width).astype(jnp.bfloat16),
            grad_values.reshape(rows, width).astype(jnp.bfloat16),
        ],
        axis=1,
    )
    grad_self_qkv = contract_rows(tokens, grad_joined)
    grad_in = (grad_one + times_transposed(grad_joined, w_self_qkv)).reshape(layout)
    vector_terms = jnp.stack(
        [
            jnp.sum(grad_joined[:, :width].astype(jnp.float32), axis=0),
            jnp.sum(grad_joined[:, 2 * width :].astype(jnp.float32), axis=0),
            jnp.sum(grad_one, axis=0),
            jnp.sum(grad_query_cross.astype(jnp.float32), axis=0),
            jnp.sum(grad_pair[:, width:].astype(jnp.float32), axis=0),
            jnp.sum(grad_two, axis=0),
            jnp.sum(grad_three, axis=0),
            gain_one,
            gain_two,
            gain_three,
            shift_one,
            shift_two,
            shift_three,
        ]
    )
    bias_terms = jnp.sum(grad_pre.astype(jnp.float32), axis=0)[None]
    (
        grad_self_qkv,
        grad_self_out,
        grad_cross_q,
        grad_cross_kv,
        grad_cross_out,
        grad_ffn_in,
        grad_ffn_out,
        vector_terms,
        bias_terms,
    ) = (
        lax.psum_scatter(
            grad_self_qkv.astype(jnp.bfloat16), "seq", scatter_dimension=1, tiled=True
        ).astype(jnp.float32),
        lax.psum_scatter(
            grad_self_out.astype(jnp.bfloat16), "seq", scatter_dimension=1, tiled=True
        ).astype(jnp.float32),
        lax.psum_scatter(
            grad_cross_q.astype(jnp.bfloat16), "seq", scatter_dimension=1, tiled=True
        ).astype(jnp.float32),
        lax.psum_scatter(
            grad_cross_kv.astype(jnp.bfloat16), "seq", scatter_dimension=1, tiled=True
        ).astype(jnp.float32),
        lax.psum_scatter(
            grad_cross_out.astype(jnp.bfloat16), "seq", scatter_dimension=1, tiled=True
        ).astype(jnp.float32),
        lax.psum_scatter(
            grad_ffn_in.astype(jnp.bfloat16), "seq", scatter_dimension=1, tiled=True
        ).astype(jnp.float32),
        lax.psum_scatter(
            grad_ffn_out.astype(jnp.bfloat16), "seq", scatter_dimension=1, tiled=True
        ).astype(jnp.float32),
        lax.psum_scatter(
            vector_terms.astype(jnp.bfloat16), "seq", scatter_dimension=1, tiled=True
        ).astype(jnp.float32),
        lax.psum_scatter(
            bias_terms.astype(jnp.bfloat16), "seq", scatter_dimension=1, tiled=True
        ).astype(jnp.float32),
    )
    (
        grad_self_qkv,
        grad_self_out,
        grad_cross_q,
        grad_cross_kv,
        grad_cross_out,
        grad_ffn_in,
        grad_ffn_out,
    ) = (
        lax.psum_scatter(
            grad_self_qkv.astype(jnp.bfloat16), "batch", scatter_dimension=0, tiled=True
        ).astype(jnp.float32),
        lax.psum_scatter(
            grad_self_out.astype(jnp.bfloat16), "batch", scatter_dimension=0, tiled=True
        ).astype(jnp.float32),
        lax.psum_scatter(
            grad_cross_q.astype(jnp.bfloat16), "batch", scatter_dimension=0, tiled=True
        ).astype(jnp.float32),
        lax.psum_scatter(
            grad_cross_kv.astype(jnp.bfloat16), "batch", scatter_dimension=0, tiled=True
        ).astype(jnp.float32),
        lax.psum_scatter(
            grad_cross_out.astype(jnp.bfloat16), "batch", scatter_dimension=0, tiled=True
        ).astype(jnp.float32),
        lax.psum_scatter(
            grad_ffn_in.astype(jnp.bfloat16), "batch", scatter_dimension=0, tiled=True
        ).astype(jnp.float32),
        lax.psum_scatter(
            grad_ffn_out.astype(jnp.bfloat16), "batch", scatter_dimension=0, tiled=True
        ).astype(jnp.float32),
    )
    vector_terms, bias_terms = lax.psum((vector_terms, bias_terms), "batch")
    return (
        layer_out,
        grad_in,
        grad_memory,
        grad_self_qkv,
        grad_self_out,
        grad_cross_q,
        grad_cross_kv,
        grad_cross_out,
        grad_ffn_in,
        grad_ffn_out,
        vector_terms[0:7],
        bias_terms[0],
        vector_terms[7:10],
        vector_terms[10:13],
    )


LOG2E = 1.4426950408889634
NN = (((1,), (0,)), ((), ()))
NT = (((1,), (1,)), ((), ()))
HD = 64
BIG = -1e30
f32, bf16 = jnp.float32, jnp.bfloat16

def dot(a, b, dims=NN):
    return lax.dot_general(a, b, dims, preferred_element_type=f32)

def lanes(shape):
    return lax.broadcasted_iota(jnp.int32, shape, len(shape) - 1)

def swap_halves(x):
    return jnp.concatenate([x[:, HD:], x[:, :HD]], axis=1)

def fwd_kernel(len_ref, q_ref, k_ref, v_ref, o_ref, lp_ref, acc_ref, *, causal, heads, qb, ahead):
    p = pl.program_id(0)
    n = q_ref.shape[0]
    nk = k_ref.shape[0]
    scaled = q_ref[...].astype(f32) * LOG2E
    hi = scaled.astype(bf16)
    lo = (scaled - hi.astype(f32)).astype(bf16)
    first = lanes((n, 128)) < HD
    hi_s, lo_s = swap_halves(hi), swap_halves(lo)
    q_aug = (jnp.where(first, hi, lo_s), jnp.where(first, hi_s, lo))
    kk = k_ref[...]
    k_s = swap_halves(kk)
    k_aug = [jnp.where(first, kk, k_s), jnp.where(first, k_s, kk)]
    if not causal:
        length = len_ref[0]
        row = lax.broadcasted_iota(jnp.int32, (nk, 128), 0)
        extra = jnp.where((row >= length) & (lanes((nk, 128)) == 0), BIG, 0.0).astype(bf16)
        k_aug = [jnp.concatenate([x, extra], axis=1) for x in k_aug]
        one = (lanes((n, 128)) == 0).astype(bf16)
        q_aug = [jnp.concatenate([x, one], axis=1) for x in q_aug]
    vt = jnp.transpose(v_ref[...])
    ones = jnp.ones((16, nk), bf16)
    va = [jnp.concatenate([vt[h * HD:(h + 1) * HD], ones], axis=0) for h in range(2)]

    def scores(c, h):
        top_k = (c + 1) * qb if causal else nk
        s = dot(k_aug[h][:top_k], q_aug[h][c * qb:(c + 1) * qb], NT)
        if causal:
            r = lax.broadcasted_iota(jnp.int32, (qb, qb), 0)
            d = jnp.where(r <= lanes((qb, qb)), s[c * qb:], BIG)
            s = jnp.concatenate([s[:c * qb], d], axis=0) if c else d
        return s

    steps = [(c, h) for c in range(n // qb) for h in range(2)]
    queue = [scores(*x) for x in steps[:ahead]]
    parts = []
    for i, (c, h) in enumerate(steps):
        if i + ahead < len(steps):
            queue.append(scores(*steps[i + ahead]))
        s = queue.pop(0)
        m = jnp.max(s, axis=0, keepdims=True)
        pt = jnp.exp2(s - m).astype(bf16)
        ot = dot(va[h][:, :s.shape[0]], pt)
        l = ot[HD:HD + 1]
        parts.append(ot[:HD] * (1.0 / l))
        acc_ref[pl.ds(2 * p + h, 1), c * qb:(c + 1) * qb] = m + jnp.log2(l)
        if h == 1:
            o_ref[c * qb:(c + 1) * qb, :] = jnp.transpose(jnp.concatenate(parts, axis=0)).astype(bf16)
            parts = []

    @pl.when(p == pl.num_programs(0) - 1)
    def _():
        rows = acc_ref[...]
        wide = jnp.concatenate([rows, jnp.zeros((128 - rows.shape[0], n), f32)], axis=0)
        cols = jnp.transpose(wide)
        a = cols.astype(bf16)
        cols = cols - a.astype(f32)
        b = cols.astype(bf16)
        c = (cols - b.astype(f32)).astype(bf16)
        lane = lanes((n, 128))
        sh = lambda x, k: jnp.concatenate([jnp.zeros((n, k), bf16), x[:, :128 - k]], axis=1)
        out = jnp.where(lane < 16, a, jnp.where(lane < 32, sh(b, 16), jnp.where(lane < 48, sh(c, 32), jnp.where(lane == 127, 1.0, 0.0).astype(bf16))))
        lp_ref[...] = out

def attn_fwd(length, q, k, v, causal, qb=256, ahead=4):
    n, d = q.shape
    blk = lambda r: pl.BlockSpec((r, 128), lambda p, l: (0, p))
    return pl.pallas_call(
        functools.partial(fwd_kernel, causal=causal, heads=d // HD, qb=qb, ahead=ahead),
        grid_spec=pltpu.PrefetchScalarGridSpec(
            num_scalar_prefetch=1, grid=(d // 128,),
            in_specs=[blk(n), blk(k.shape[0]), blk(k.shape[0])],
            out_specs=[blk(n), pl.BlockSpec((n, 128), lambda p, l: (0, 0))],
            scratch_shapes=[pltpu.VMEM((16, n), f32)]),
        out_shape=[pltpu.HBM((n, d), bf16), pltpu.HBM((n, 128), bf16)],
        compiler_params=params(40),
        cost_estimate=cost((n + 256) * n * 1024 // (2 if causal else 1) * (d // HD), 8 * n * d, n * n * d // HD),
        name="attn_fwd",
    )(length, *hbm(q, k, v))

def side_rows(kind, refs, own):
    if kind == "early":
        one, cross_a, cross_b, ffn, bias = refs
        both = lambda r: jnp.concatenate([cross_a[r : r + 1, :], cross_b[r : r + 1, :]], axis=1)
        rows = [one[2:3, :], both(0), both(1), ffn[5:6, :], ffn[2:3, :], one[0:1, :], ffn[3:4, :], ffn[0:1, :], one[1:2, :], ffn[4:5, :], ffn[1:2, :]]
        half = rows[0].shape[1] // 2
        wide = bias.shape[1] // 2
        sides = []
        for x in range(2):
            sides += [r[:, x * half : (x + 1) * half] for r in rows]
            sides += [bias[0:1, x * wide + c * half : x * wide + (c + 1) * half] for c in range(wide // half)]
            sides += [jnp.zeros((1, half), f32)] * (16 - len(rows) - wide // half)
        return jnp.concatenate(sides, axis=0).astype(bf16)
    rows = [refs[0][0:2, :], refs[1][0:2, :], own[0:2, :], jnp.zeros((10, own.shape[1]), f32)]
    rows = jnp.concatenate(rows, axis=0)
    return jnp.concatenate([rows, jnp.zeros((16, 128), f32)], axis=1).astype(bf16)


def bwd_kernel(len_ref, q_ref, k_ref, v_ref, o_ref, g_ref, lp_ref, *rest, causal, qb, first_pair, stride, unit, kind):
    if unit:
        place, tok_ref, *side, out_ref, sums_ref, send_ref, own_ref = rest
    else:
        out_ref, sums_ref = rest
    p = pl.program_id(0) * stride + first_pair
    n, nk = q_ref.shape[0], k_ref.shape[0]
    first = lanes((n, 128)) < HD
    q = q_ref[...]
    scaled = q.astype(f32) * LOG2E
    hi = scaled.astype(bf16)
    lo = (scaled - hi.astype(f32)).astype(bf16)
    hi_s, lo_s = swap_halves(hi), swap_halves(lo)
    lp = lp_ref[...]
    q_aug = [jnp.concatenate([x, lp], axis=1) for x in (jnp.where(first, hi, lo_s), jnp.where(first, hi_s, lo))]
    kk = k_ref[...]
    k_s = swap_halves(kk)
    v = v_ref[...]
    lane = lanes((nk, 128))
    g = g_ref[...]
    zero = jnp.zeros((), bf16)
    go = g.astype(f32) * o_ref[...].astype(f32)
    go_hi = go.astype(bf16)
    go_lo = (go - go_hi.astype(f32)).astype(bf16)
    br = lax.broadcasted_iota(jnp.int32, (128, 128), 0)
    bl = lanes((128, 128))
    pick = jnp.where(((bl < 3) & (br < HD)) | ((bl >= 3) & (bl < 6) & (br >= HD)), 1.0, 0.0).astype(bf16)
    dl = dot(go_hi, pick) + dot(go_lo, pick)
    da = dl.astype(bf16)
    rest = dl - da.astype(f32)
    db = rest.astype(bf16)
    dc = (rest - db.astype(f32)).astype(bf16)
    part = lanes((n, 128))
    part = jnp.where(part >= 3, part - 3, part)
    dpack = jnp.where(part == 0, da, jnp.where(part == 1, db, dc))
    g_aug = jnp.concatenate([g, dpack], axis=1)
    qt = jnp.transpose(q)
    gt = jnp.transpose(g)
    minus = jnp.full((), -1.0, bf16)
    row = lax.broadcasted_iota(jnp.int32, (nk, 128), 0)
    k_augs, v_augs = [], []
    for h in range(2):
        head = 2 * p + h
        sel = jnp.where((lane < 48) & ((lane & 15) == head), -1.0, 0.0)
        if not causal:
            sel = jnp.where((lane == 127) & (row >= len_ref[0]), BIG, sel)
        k_augs.append(jnp.concatenate([jnp.where(first, kk, k_s) if h == 0 else jnp.where(first, k_s, kk), sel.astype(bf16)], axis=1))
        dsel = jnp.where((lane >= 3 * h) & (lane < 3 * h + 3), -1.0, 0.0).astype(bf16)
        v_m = jnp.where(first, v, zero) if h == 0 else jnp.where(first, zero, v)
        v_augs.append(jnp.concatenate([v_m, dsel], axis=1))

    def products(c, h):
        rows = slice(c * qb, (c + 1) * qb)
        top_k = (c + 1) * qb if causal else nk
        return dot(q_aug[h][rows], k_augs[h][:top_k], NT), dot(g_aug[rows], v_augs[h][:top_k], NT)

    def weigh(c, s, dp):
        w = jnp.exp2(s)
        if causal:
            r = lax.broadcasted_iota(jnp.int32, (qb, qb), 0)
            dg = jnp.where(r >= lanes((qb, qb)), w[:, c * qb:], 0.0)
            w = jnp.concatenate([w[:, :c * qb], dg], axis=1) if c else dg
        return w.astype(bf16), (w * dp).astype(bf16)

    def collect(c, h, wb, ds):
        rows = slice(c * qb, (c + 1) * qb)
        top_k = ds.shape[1]
        grow = lambda total, part: part + total if top_k == nk else jnp.concatenate([total[:, :top_k] + part, total[:, top_k:]], axis=1)
        dvts[h] = grow(dvts[h], dot(gt[h * HD:(h + 1) * HD, rows], wb))
        dkts[h] = grow(dkts[h], dot(qt[h * HD:(h + 1) * HD, rows], ds))
        dq_parts[h][c] = dot(ds, kk[:top_k])

    dkts = [jnp.zeros((HD, nk), f32)] * 2
    dvts = [jnp.zeros((HD, nk), f32)] * 2
    dq_parts = [{}, {}]
    steps = [(c, h) for h in range(2) for c in range(n // qb)]
    ahead = products(*steps[0])
    for i, (c, h) in enumerate(steps):
        s, dp = ahead
        if i + 1 < len(steps):
            ahead = products(*steps[i + 1])
        collect(c, h, *weigh(c, s, dp))
    sums = jnp.zeros((1, 128), f32)
    dqs = []
    for c in range(n // qb):
        rows = slice(c * qb, (c + 1) * qb)
        fl = lanes((qb, 128)) < HD
        dq = (jnp.where(fl, dq_parts[0][c], dq_parts[1][c]) * 0.125).astype(bf16)
        dqs.append(dq)
        sums = sums + jnp.sum(dq.astype(f32), axis=0, keepdims=True)
    dk = jnp.transpose(jnp.concatenate(dkts, axis=0)).astype(bf16)
    dv = jnp.transpose(jnp.concatenate(dvts, axis=0)).astype(bf16)
    v_sums = jnp.sum(dv.astype(f32), axis=0, keepdims=True)
    grads = (jnp.concatenate(dqs, axis=0), dk, dv)
    if not unit:
        sums_ref[...] = jnp.concatenate([sums, v_sums, jnp.zeros((6, 128), f32)], axis=0)
        for m, part in enumerate(grads):
            out_ref[m] = part
        return
    for at in range(2):
        @pl.when(pl.program_id(0) == at)
        def _(at=at):
            cols = slice(at * 128, (at + 1) * 128)
            sums_ref[:, cols] = jnp.concatenate([sums, v_sums, jnp.zeros((6, 128), f32)], axis=0)
            for m, part in enumerate(grads):
                out_ref[m, :, cols] = part

    @pl.when(pl.program_id(0) == 1)
    def _():
        joined = jnp.concatenate([out_ref[0], out_ref[1], out_ref[2]], axis=1)
        store_units(place, dot(tok_ref[...], joined, TN).astype(bf16), unit, send_ref, own_ref)
        if kind:
            rows = side_rows(kind, side, sums_ref[...])
            for ref in (send_ref, own_ref):
                for y in range(2):
                    for x in range(2):
                        for z in range(ref.shape[2]):
                            ref[y, x, z, unit:] = rows


def attn_bwd(length, q, k, v, o, g, lp, causal, first, stride, count, tokens=None, place=None, nb=0, kind="", side=(), qb=256):
    n, d = q.shape
    blk = pl.BlockSpec((n, 128), lambda p, l: (0, first + stride * p))
    ins = [blk] * 5 + [pl.BlockSpec((n, 128), lambda p, l: (0, 0))]
    outs = [pl.BlockSpec((3, n, 128), lambda p, l: (0, 0, p)), pl.BlockSpec((8, 128), lambda p, l: (0, p))]
    shapes = [pltpu.HBM((3, n, count * 128), bf16), pltpu.HBM((8, count * 128), f32)]
    args = hbm(q, k, v, o, g, lp)
    unit = 0
    if tokens is not None:
        unit = d // nb
        rows = unit + {"early": 32, "late": 16, "": 0}[kind]
        ins += [pl.BlockSpec(memory_space=pltpu.SMEM), pl.BlockSpec((n, d), lambda p, l: (0, 0))]
        ins += [pl.BlockSpec(s.shape, lambda p, l: (0, 0)) for s in side]
        args += [place] + hbm(tokens, *side)
        outs = [pl.BlockSpec((3, n, 256), lambda p, l: (0, 0, 0)), pl.BlockSpec((8, 256), lambda p, l: (0, 0))]
        outs += [pl.BlockSpec((2, 2, nb // 4, rows, 384), lambda p, l: (0, 0, 0, 0, 0))] * 2
        shapes += [pltpu.HBM((2, 2, nb // 4, rows, 384), bf16)] * 2
    return pl.pallas_call(
        functools.partial(bwd_kernel, causal=causal, qb=qb, first_pair=first, stride=stride, unit=unit, kind=kind),
        grid_spec=pltpu.PrefetchScalarGridSpec(
            num_scalar_prefetch=1, grid=(count,), in_specs=ins, out_specs=outs),
        out_shape=shapes,
        compiler_params=params(40),
        cost_estimate=cost((n + 256) * n * 2560 // (2 if causal else 1) * count * 2, 16 * n * count * 128, 2 * n * n * count),
        name="attn_bwd",
    )(length, *args)


TN = (((0,), (0,)), ((), ()))


def cost(flops, moved, exps=0):
    return pl.CostEstimate(flops=int(flops), bytes_accessed=int(moved), transcendentals=int(exps))


def params(mib):
    return pltpu.CompilerParams(vmem_limit_bytes=mib * 2**20)


def hbm(*values):
    return [pltpu.with_memory_space_constraint(v, pltpu.HBM) for v in values]


def whole():
    return pl.BlockSpec(memory_space=pltpu.VMEM)


def fixed(shape):
    return pl.BlockSpec(shape, lambda *_: (0,) * len(shape), pipeline_mode=pl.Buffered(1))


def spread_rows(block):
    return lambda i, *_: (i, 0)


def project_kernel(place, mine, got, weight, biases, *outs, step, plan):
    i = pl.program_id(0)
    x = jnp.where(i // step == place[0], mine[...], got[...])
    outs[0][...] = x
    joined = dot(x, weight[...])
    width = x.shape[1]
    for n, (bias, scale) in enumerate(plan):
        part = joined[:, n * width : (n + 1) * width]
        if bias is not None:
            part = part + biases[bias : bias + 1, :]
        if scale != 1.0:
            part = part * scale
        outs[n + 1][...] = part.astype(bf16)


def project(place, pairs, got, weight, biases, plan, rows=256):
    half, width = got.shape
    step = half // rows
    cols = weight.shape[1]
    block = pl.BlockSpec((rows, width), lambda i, p: (i, 0))
    return pl.pallas_call(
        functools.partial(project_kernel, step=step, plan=plan),
        grid_spec=pltpu.PrefetchScalarGridSpec(
            num_scalar_prefetch=1,
            grid=(2 * step,),
            in_specs=[
                pl.BlockSpec((rows, width), lambda i, p: (i % step, p[0])),
                pl.BlockSpec((rows, width), lambda i, p: (i % step, 0)),
                whole(),
                whole(),
            ],
            out_specs=[block] * (1 + len(plan)),
        ),
        out_shape=[pltpu.HBM((2 * half, width), bf16)] * (1 + len(plan)),
        compiler_params=params(32),
        cost_estimate=cost(4 * half * width * cols, 2 * width * cols + 12 * half * width),
        name="project",
    )(place, *hbm(pairs, got), weight, biases)


def norm_unit(value):
    mean = jnp.mean(value, axis=-1, keepdims=True)
    centred = value - mean
    scale = lax.rsqrt(jnp.mean(centred * centred, axis=-1, keepdims=True) + 1e-05)
    return centred * scale, scale


def norm_back(grad, unit, scale, gain):
    weighted = grad * gain
    return scale * (
        weighted
        - jnp.mean(weighted, axis=-1, keepdims=True)
        - unit * jnp.mean(weighted * unit, axis=-1, keepdims=True)
    )


def row_sum(value):
    return jnp.sum(value, axis=0, keepdims=True)


def after_self_kernel(o, tok, w_out, w_q, biases, gain, shift, unit_ref, scale_ref, low_ref, q_ref):
    resid = tok[...].astype(f32) + dot(o[...], w_out[...]) + biases[2:3, :]
    unit, scale = norm_unit(resid)
    unit_ref[...] = unit
    scale_ref[...] = jnp.broadcast_to(scale, scale_ref.shape)
    low_ = (unit * gain[0:1, :] + shift[0:1, :]).astype(bf16)
    low_ref[...] = low_
    q_ref[...] = ((dot(low_, w_q[...]) + biases[3:4, :]) * 0.125).astype(bf16)


def after_self(o, tok, w_out, w_q, biases, gain, shift, rows=256):
    n, d = o.shape
    block = pl.BlockSpec((rows, d), lambda i: (i, 0))
    return pl.pallas_call(
        after_self_kernel,
        grid=(n // rows,),
        in_specs=[block, block, whole(), whole()] + [whole()] * 3,
        out_specs=[block, pl.BlockSpec((rows, 128), lambda i: (i, 0)), block, block],
        out_shape=[
            pltpu.HBM((n, d), f32),
            pltpu.HBM((n, 128), f32),
            pltpu.HBM((n, d), bf16),
            pltpu.HBM((n, d), bf16),
        ],
        compiler_params=params(32),
        cost_estimate=cost(4 * n * d * d, 4 * d * d + 12 * n * d),
        name="after_self",
    )(*hbm(o, tok), w_out, w_q, biases, gain, shift)


RATE = 0.3275911 * 0.7071067811865476
TAIL = tuple(0.5 * c for c in (0.254829592, -0.284496736, 1.421413741, -1.453152027, 1.061405429))
DENSITY = 0.3989422804014327


def gelu_pair(v):
    size = jnp.abs(v)
    base = 1.0 + RATE * size
    t = pl.reciprocal(base, approx=True)
    t = t * (2.0 - base * t)
    poly = TAIL[4]
    for c in TAIL[3::-1]:
        poly = c + t * poly
    bell = jnp.exp2((v * v) * (-0.5 * LOG2E))
    tail = t * poly * bell
    below = jnp.where(v >= 0.0, 1.0 - tail, tail)
    return v * below, below + v * (DENSITY * bell)


def ffn_kernel(
    place, o, unit_one, cot_mine, cot_got, w_co, w_in, w_out, biases, ffn_bias, gain, shift,
    layer_ref, g2_ref, gm_ref, sums_ref, fsum_ref, grads_ref,
    slope, act_all, pre_all, b3_all, b2_all, low_turned, o_turned, *, blocks, nz,
):
    i = pl.program_id(0)
    rows, d = o.shape
    n_chunks, _, chunk = act_all.shape

    @pl.when(i == 0)
    def _():
        sums_ref[...] = jnp.zeros_like(sums_ref)
        fsum_ref[...] = jnp.zeros_like(fsum_ref)

    @pl.when(i < blocks)
    def _():
        here = pl.ds(pl.multiple_of(i * rows, rows), rows)
        o_turned[:, here] = jnp.transpose(o[...])
        normed_one = unit_one[...] * gain[0:1, :] + shift[0:1, :]
        resid = normed_one + dot(o[...], w_co[...]) + biases[5:6, :]
        unit_two, scale_two = norm_unit(resid)
        normed_two = unit_two * gain[1:2, :] + shift[1:2, :]
        low_two = normed_two.astype(bf16)
        low_turned[:, here] = jnp.transpose(low_two)

        def inner(j):
            at = slice(j * chunk, (j + 1) * chunk)
            return dot(low_two, w_in[:, at]) + ffn_bias[0:1, at]

        total = normed_two + biases[6:7, :]
        ahead = inner(0)
        for j in range(n_chunks):
            v = ahead
            if j + 1 < n_chunks:
                ahead = inner(j + 1)
            act, grad = gelu_pair(v)
            act = act.astype(bf16)
            act_all[j, here, :] = act
            slope[:, j * chunk : (j + 1) * chunk] = grad
            total = total + dot(act, w_out[j * chunk : (j + 1) * chunk, :])
        unit, scale = norm_unit(total)
        layer_ref[...] = (unit * gain[2:3, :] + shift[2:3, :]).astype(bf16)
        g = jnp.where(i // (blocks // 2) == place[0], cot_mine[...], cot_got[...]).astype(f32)
        grad_three = norm_back(g, unit, scale, gain[2:3, :])
        branch = grad_three.astype(bf16)
        b3_all[here, :] = branch
        sums_ref[0:1, :] += row_sum(g * unit)
        sums_ref[1:2, :] += row_sum(g)
        sums_ref[2:3, :] += row_sum(grad_three)

        def back(j):
            return dot(branch, w_out[j * chunk : (j + 1) * chunk, :], NT)

        total = grad_three
        ahead = back(0)
        for j in range(n_chunks):
            v = ahead
            if j + 1 < n_chunks:
                ahead = back(j + 1)
            at = slice(j * chunk, (j + 1) * chunk)
            pre = (v * slope[:, at]).astype(bf16)
            pre_all[j, here, :] = pre
            fsum_ref[0:1, at] += row_sum(pre.astype(f32))
            total = total + dot(pre, w_in[:, at], NT)
        grad_two = norm_back(total, unit_two, scale_two, gain[1:2, :])
        g2_ref[...] = grad_two
        branch = grad_two.astype(bf16)
        b2_all[here, :] = branch
        sums_ref[3:4, :] += row_sum(total * unit_two)
        sums_ref[4:5, :] += row_sum(total)
        sums_ref[5:6, :] += row_sum(grad_two)
        gm_ref[...] = dot(branch, w_co[...], NT).astype(bf16)

    @pl.when(i >= blocks)
    def _():
        z = i - blocks
        half = d // 2
        count = grads_ref.shape[1]
        unit = grads_ref.shape[2]
        value = dot(act_all[z], b3_all[...], TN).astype(bf16)
        pieces = value.shape[0] // (count * unit)
        for u in range(count):
            for c in range(pieces):
                top = (u * pieces + c) * unit
                for x in range(2):
                    grads_ref[x, u, :, c * half : (c + 1) * half] = value[top : top + unit, x * half : (x + 1) * half]
        start = pieces * half
        own = pl.ds(pl.multiple_of(z * count * unit, count * unit), count * unit)
        a = low_turned[own, :]
        for j in range(n_chunks):
            value = dot(a, pre_all[j]).astype(bf16)
            x, left = divmod(j, n_chunks // 2)
            for u in range(count):
                grads_ref[x, u, :, start + left * chunk : start + (left + 1) * chunk] = value[u * unit : (u + 1) * unit]
        start += n_chunks // 2 * chunk
        value = dot(o_turned[own, :], b2_all[...]).astype(bf16)
        for u in range(count):
            for x in range(2):
                grads_ref[x, u, :, start : start + half] = value[u * unit : (u + 1) * unit, x * half : (x + 1) * half]


def ffn(place, o, unit_one, cot_pairs, cot_got, w_co, w_in, w_out, biases, ffn_bias, gain, shift, nb, rows=256):
    n, d = o.shape
    ff = w_in.shape[1]
    blocks = n // rows
    nz = ff // d
    unit = d // nb
    at = lambda i: jnp.minimum(i, blocks - 1)
    block = pl.BlockSpec((rows, d), lambda i, p: (at(i), 0))
    width = ff + d // 2
    scratch = [
        pltpu.VMEM((rows, ff), f32),
        pltpu.VMEM((nz, n, d), bf16),
        pltpu.VMEM((nz, n, d), bf16),
        pltpu.VMEM((n, d), bf16),
        pltpu.VMEM((n, d), bf16),
        pltpu.VMEM((d, n), bf16),
        pltpu.VMEM((d, n), bf16),
    ]
    return pl.pallas_call(
        functools.partial(ffn_kernel, blocks=blocks, nz=nz),
        grid_spec=pltpu.PrefetchScalarGridSpec(
            num_scalar_prefetch=1,
            grid=(blocks + nz,),
            in_specs=[
                block,
                block,
                pl.BlockSpec((rows, d), lambda i, p: (at(i) % (blocks // 2), p[0])),
                pl.BlockSpec((rows, d), lambda i, p: (at(i) % (blocks // 2), 0)),
            ] + [whole()] * 7,
            out_specs=[
                block,
                block,
                block,
                pl.BlockSpec((8, d), lambda i, p: (0, 0)),
                pl.BlockSpec((8, ff), lambda i, p: (0, 0)),
                pl.BlockSpec((2, nb // nz, unit, width), lambda i, p: (0, jnp.maximum(i - blocks, 0), 0, 0)),
            ],
            scratch_shapes=scratch,
        ),
        out_shape=[
            pltpu.HBM((n, d), bf16),
            pltpu.HBM((n, d), f32),
            pltpu.HBM((n, d), bf16),
            pltpu.HBM((8, d), f32),
            pltpu.HBM((8, ff), f32),
            pltpu.HBM((2, nb, unit, width), bf16),
        ],
        compiler_params=params(60),
        cost_estimate=cost(12 * n * d * ff + 6 * n * d * d, 8 * d * ff + 20 * n * d, 2 * n * ff),
        name="ffn",
    )(place, *hbm(o, unit_one, cot_pairs, cot_got), w_co, w_in, w_out, biases, ffn_bias, gain, shift)


def store_units(place, value, unit, send_ref, own_ref, first=0, z_local=False):
    mx, mz, my, core = place[0], place[1], place[2], place[3]
    half = value.shape[1] // 2
    for mine in range(2):
        @pl.when(core == mine)
        def _():
            for u in range(value.shape[0] // unit):
                ref = own_ref if u % 2 == mine else send_ref
                z = 0 if z_local else jnp.bitwise_xor(u // 4, mz)
                y = jnp.bitwise_xor((u // 2) % 2, my)
                for x in range(2):
                    ref[y, jnp.bitwise_xor(x, mx), z, :unit] = value[u * unit : (u + 1) * unit, x * half : (x + 1) * half]


def middle_kernel(
    place, g2, unit_ref, scale_ref, grad_a, grad_b, out_self, low_one, sources, w_q, w_out, w_kv, gain,
    g1_ref, gm_ref, sums_ref, other_ref, mine_ref, send_ref, own_ref, gq_all, b1_all, *, blocks, unit,
):
    i = pl.program_id(0)
    rows, d = g2.shape

    @pl.when(i == 0)
    def _():
        sums_ref[...] = jnp.zeros_like(sums_ref)

    @pl.when(i < blocks)
    def _():
        half = blocks // 2
        mine = i >= half
        at = jnp.where(mine, place[0] * half + i - half, (1 - place[0]) * half + i)
        here = pl.ds(pl.multiple_of(at * rows, rows), rows)
        gq = jnp.concatenate([grad_a[0, here, :], grad_b[0, here, :]], axis=1)
        gq_all[here, :] = gq
        g = g2[...] + dot(gq, w_q[...], NT)
        unit_one = unit_ref[...]
        grad = norm_back(g, unit_one, scale_ref[:, 0:1], gain[0:1, :])
        g1_ref[...] = grad
        branch = grad.astype(bf16)
        b1_all[here, :] = branch
        sums_ref[0:1, :] += row_sum(g * unit_one)
        sums_ref[1:2, :] += row_sum(g)
        sums_ref[2:3, :] += row_sum(grad)
        gm_ref[...] = dot(branch, w_out[...], NT).astype(bf16)
        pair = jnp.concatenate([r[m, here, :] for m in (1, 2) for r in (grad_a, grad_b)], axis=1)
        value = dot(pair, w_kv[...], NT)

        @pl.when(mine)
        def _():
            mine_ref[...] = value

        @pl.when(jnp.logical_not(mine))
        def _():
            other_ref[...] = value.astype(bf16)

    def store(value):
        store_units(place, value.astype(bf16), unit, send_ref, own_ref)

    @pl.when(i == blocks)
    def _():
        store(dot(out_self[...], b1_all[...], TN))

    @pl.when(i == blocks + 1)
    def _():
        store(dot(low_one[...], gq_all[...], TN))

    for step, grads in ((2, grad_a), (3, grad_b)):
        @pl.when(i == blocks + step)
        def _(grads=grads):
            store(dot(sources[...], jnp.concatenate([grads[1], grads[2]], axis=1), TN))


def middle(place, g2, unit_one, scale, grad_a, grad_b, out_self, low_one, sources, w_q, w_out, w_kv, gain, nb, rows=256):
    n, d = g2.shape
    blocks = n // rows
    unit = d // nb
    half = blocks // 2

    def block_at(i, p):
        i = jnp.minimum(i, blocks - 1)
        return (jnp.where(i < half, (1 - p[0]) * half + i, p[0] * half + i - half), 0)

    block = pl.BlockSpec((rows, d), block_at)
    fixed_block = lambda shape: pl.BlockSpec(shape, lambda i, p: (0,) * len(shape), pipeline_mode=pl.Buffered(1))
    piece = pl.BlockSpec((2, 2, nb // 4, unit, d // 2), lambda i, p: (0, 0, 0, 0, jnp.maximum(i - blocks, 0)))
    big = pltpu.HBM((2, 2, nb // 4, unit, 2 * d), bf16)
    return pl.pallas_call(
        functools.partial(middle_kernel, blocks=blocks, unit=unit),
        grid_spec=pltpu.PrefetchScalarGridSpec(
            num_scalar_prefetch=1,
            grid=(blocks + 4,),
            in_specs=[block, block, pl.BlockSpec((rows, 128), block_at), fixed_block(grad_a.shape), fixed_block(grad_b.shape)]
            + [fixed_block((n, d))] * 3 + [whole()] * 4,
            out_specs=[
                block,
                block,
                pl.BlockSpec((8, d), lambda i, p: (0, 0)),
                pl.BlockSpec((rows, d), lambda i, p: (jnp.minimum(i, half - 1), 0)),
                pl.BlockSpec((rows, d), lambda i, p: (jnp.clip(i - half, 0, half - 1), 0)),
                piece,
                piece,
            ],
            scratch_shapes=[pltpu.VMEM((n, d), bf16), pltpu.VMEM((n, d), bf16)],
        ),
        out_shape=[
            pltpu.HBM((n, d), f32),
            pltpu.HBM((n, d), bf16),
            pltpu.HBM((8, d), f32),
            pltpu.HBM((n // 2, d), bf16),
            pltpu.HBM((n // 2, d), f32),
            big,
            big,
        ],
        compiler_params=params(48),
        cost_estimate=cost(16 * n * d * d, 40 * n * d),
        name="middle",
    )(place, *hbm(g2, unit_one, scale, grad_a, grad_b, out_self, low_one, sources), w_q, w_out, w_kv, gain)


def grad_rows_kernel(place, *refs, columns, based):
    gs, weight = refs[: len(columns)], refs[len(columns)]
    out_ref = refs[-1]
    value = None
    for g, chunks in zip(gs, columns):
        for m, starts in enumerate(chunks):
            if not starts:
                continue
            w = [weight[:, s : s + size] for s, size in starts]
            w = w[0] if len(w) == 1 else jnp.concatenate(w, axis=1)
            term = dot(g[m], w, NT)
            value = term if value is None else value + term
    if based:
        value = value + refs[len(columns) + 1][...]

    out_ref[...] = value.astype(out_ref.dtype)


def grad_rows(place, terms, columns, weight, base, mine, rows=256):
    n = terms[0].shape[1]
    d, k = weight.shape
    steps = n // 2 // rows
    half = lambda i, p: (p[0] if mine else 1 - p[0]) * steps + i
    ins = [pl.BlockSpec((t.shape[0], rows, t.shape[2]), lambda i, p: (0, half(i, p), 0)) for t in terms] + [whole()]
    args = hbm(*terms) + [weight]
    if base is not None:
        ins.append(pl.BlockSpec((rows, d), lambda i, p: (half(i, p), 0)))
        args += hbm(base)
    return pl.pallas_call(
        functools.partial(grad_rows_kernel, columns=columns, based=base is not None),
        grid_spec=pltpu.PrefetchScalarGridSpec(
            num_scalar_prefetch=1,
            grid=(steps,),
            in_specs=ins,
            out_specs=pl.BlockSpec((rows, d), lambda i, p: (i, 0)),
        ),
        out_shape=pltpu.HBM((n // 2, d), f32 if mine else bf16),
        compiler_params=params(40),
        cost_estimate=cost(n * k * d, n * k + 2 * k * d + 4 * n * d),
        name="grad_rows",
    )(place, *args)


def route(nb, move):
    dz, dy, dc, dx = move
    pairs = []
    for b in range(nb):
        z, y, core = b // 4, (b // 2) % 2, b % 2
        for x in range(2):
            target = (z ^ dz) * 4 + (y ^ dy) * 2 + (core ^ dc)
            pairs.append((b * 2 + x, target * 2 + (x ^ dx)))
    return pairs


def send(value, nb, move):
    return lax.ppermute(value, ("z", "y", "core", "seq"), route(nb, move))


def core_stage(buffers, nb):
    to_send, own = buffers
    return own, send(to_send, nb, (0, 0, 1, 0))


def y_prepare(state):
    own, got = state
    return (own[1].astype(f32) + got[1].astype(f32)).astype(bf16), (own, got)


def y_move(value, nb):
    return send(value, nb, (0, 1, 0, 0))


def x_prepare(state):
    own, got, more = state
    total = own[0].astype(f32) + got[0].astype(f32) + more.astype(f32)
    return total[0].astype(bf16), total[1].astype(bf16)


def x_move(value, nb):
    return send(value, nb, (0, 0, 0, 1))


def z_prepare(state):
    kept, got = state
    total = kept.astype(f32) + got.astype(f32)
    return total[0::2].astype(bf16), total[1::2].astype(bf16)


def z_move(value, nb, bit):
    return send(value, nb, (1 << bit, 0, 0, 0))


def halves_first(state):
    own, got = state
    h = own.shape[2] // 2
    over_y = own[1, :, :h].astype(f32) + got[1, :, :h].astype(f32)
    over_x = own[:, 1, h:].astype(f32) + got[:, 1, h:].astype(f32)
    return over_y.astype(bf16), over_x.astype(bf16)


def halves_move(values, nb, turn):
    a, b = ((0, 0, 0, 1), (0, 1, 0, 0)) if turn else ((0, 1, 0, 0), (0, 0, 0, 1))
    return send(values[0], nb, a), send(values[1], nb, b)


def halves_second(state):
    (own, got), (from_y, from_x) = state
    h = own.shape[2] // 2
    a = own[0, :, :h].astype(f32) + got[0, :, :h].astype(f32) + from_y.astype(f32)
    b = own[:, 0, h:].astype(f32) + got[:, 0, h:].astype(f32) + from_x.astype(f32)
    return (a[0].astype(bf16), b[0].astype(bf16)), (a[1].astype(bf16), b[1].astype(bf16))


def halves_third(state):
    kept, got = state
    total = jnp.concatenate([k.astype(f32) + g.astype(f32) for k, g in zip(kept, got)], axis=0)
    return total[0::2].astype(bf16), total[1::2].astype(bf16)


def after_y(state):
    own, got, more = state
    return (own[0].astype(f32) + got[0].astype(f32) + more.astype(f32)).astype(bf16)


def direct_z(total, nb):
    result = total[:, 0].astype(f32)
    for d in range(1, nb // 4):
        result = result + send(total[:, d], nb, (d, 0, 0, 0)).astype(f32)
    return result


def at(value, index, axis):
    return lax.dynamic_index_in_dim(value, index, axis, keepdims=False)


def last_stage(state):
    kept, got = state
    return (kept.astype(f32) + got.astype(f32))[0]


def last_part(state, start, end):
    kept, got = state
    return (kept[:, :, start:end].astype(f32) + got[:, :, start:end].astype(f32))[0]


def tie(*values):
    return lax.optimization_barrier(values)


def swap(value):
    return lax.ppermute(value, "seq", [(0, 1), (1, 0)])


def split_pairs(local):
    positions, _, width = local.shape
    pairs = local.reshape(positions, 2 * width)
    x = lax.axis_index("seq")
    return pairs, lax.dynamic_slice(pairs, (0, (1 - x) * width), (positions, width))


def join_pairs(mine, got):
    x = lax.axis_index("seq")
    got = got.astype(mine.dtype)
    both = jnp.concatenate([jnp.where(x == 0, mine, got), jnp.where(x == 0, got, mine)], axis=1)
    return both.reshape(mine.shape[0], 2, mine.shape[1])


def per_device_fast(
    hidden_in,
    memory,
    src_len,
    out_grad,
    w_self_qkv,
    w_self_out,
    w_cross_q,
    w_cross_kv,
    w_cross_out,
    w_ffn_in,
    w_ffn_out,
    biases,
    ffn_bias,
    norm_gain,
    norm_shift,
):
    nb = lax.axis_size(("z", "y", "core"))
    width = hidden_in.shape[2]
    half = width // 2
    x, b = lax.axis_index("seq"), lax.axis_index(("z", "y", "core"))
    place = jnp.stack([x, b // 4, (b // 2) % 2, b % 2]).astype(jnp.int32)
    length = lax.dynamic_slice_in_dim(src_len, x, 1)

    pairs, other = split_pairs(hidden_in)
    got = swap(other)
    memory_pairs, memory_other = split_pairs(memory)
    memory_got = swap(memory_other)
    cot_pairs, cot_other = split_pairs(out_grad)
    tokens, query_self, key_self, value_self = project(
        place, pairs, got, w_self_qkv, biases, ((0, 0.125), (None, 1.0), (1, 1.0))
    )
    query_self, cot_other = tie(query_self, cot_other)
    cot_got = swap(cot_other)
    out_self, lp_self = attn_fwd(length, query_self, key_self, value_self, True)
    unit_one, scale_one, low_one, query_cross = after_self(
        out_self, tokens, w_self_out, w_cross_q, biases, norm_gain, norm_shift
    )
    sources, key_cross, value_cross = project(
        place, memory_pairs, memory_got, w_cross_kv, biases, ((None, 1.0), (4, 1.0))
    )
    out_cross, lp_cross = attn_fwd(length, query_cross, key_cross, value_cross, False)
    layer, grad_two, grad_mixed, sums_ffn, bias_sums, one = ffn(
        place, out_cross, unit_one, cot_pairs, cot_got, w_cross_out, w_ffn_in, w_ffn_out, biases, ffn_bias[None], norm_gain, norm_shift, nb
    )
    span = layer.shape[0] // 2

    ff = w_ffn_in.shape[1]
    layer_other = lax.dynamic_slice_in_dim(layer, (1 - x) * span, span, 0)
    one, layer_other, grad_mixed = tie(one, layer_other, grad_mixed)
    one = lax.psum_scatter(one.reshape(-1, one.shape[-1]), ("seq", "z", "y", "core"), scatter_dimension=0, tiled=True)
    layer_got = swap(layer_other)
    back = partial(attn_bwd, length, query_cross, key_cross, value_cross, out_cross)
    cross_a, sums_ca = back(grad_mixed, lp_cross, False, 0, 1, 3)

    cross_a, grad_mixed, layer_got = tie(cross_a, grad_mixed, layer_got)
    cross_b, sums_cb = back(grad_mixed, lp_cross, False, 3, 1, 3)

    grad_one, grad_mixed, sums_one, other, memory_mine, *three = middle(
        place, grad_two, unit_one, scale_one, cross_a, cross_b, out_self, low_one, sources,
        w_cross_q, w_self_out, w_cross_kv, norm_gain, nb,
    )

    three, other, grad_mixed = tie(three, other, grad_mixed)
    three = core_stage(three, nb)
    cut = span * 5 // 8
    memory_back = swap(other[:cut])
    memory_rest = other[cut:]
    back = partial(attn_bwd, length, query_self, key_self, value_self, out_self)
    self_a, sums_sa, *four = back(
        grad_mixed, lp_self, True, 0, 3, 2, tokens, place, nb, "early", (sums_one, sums_ca, sums_cb, sums_ffn, bias_sums)
    )

    four, three, grad_mixed, memory_back = tie(four, three, grad_mixed, memory_back)
    four = core_stage(four, nb)
    three_out = halves_first(three)
    three_out, grad_mixed = tie(three_out, grad_mixed)
    three = three, halves_move(three_out, nb, False)
    self_b, sums_sb, *five = back(grad_mixed, lp_self, True, 1, 3, 2, tokens, place, nb)

    five, four, three, grad_mixed = tie(five, four, three, grad_mixed)
    five = core_stage(five, nb)
    four_out, four = y_prepare(four)
    three_keep, three_out = halves_second(three)
    four_out, three_out, grad_mixed, memory_rest = tie(four_out, three_out, grad_mixed, memory_rest)
    four = four + (y_move(four_out, nb),)
    memory_rest = swap(memory_rest)
    three = three_keep, halves_move(three_out, nb, True)
    self_c, sums_sc, *six = back(grad_mixed, lp_self, True, 2, 3, 2, tokens, place, nb, "late", (sums_sa, sums_sb))

    self_c, six, five, four, three, memory_rest = tie(self_c, six, five, four, three, memory_rest)
    six = core_stage(six, nb)
    five_out, five = y_prepare(five)
    four_keep, four_out = x_prepare(four)
    three_keep, three_out = halves_third(three)
    five_out, four_out, three_out, self_c = tie(five_out, four_out, three_out, self_c)
    five = five + (y_move(five_out, nb),)
    four = four_keep, x_move(four_out, nb)
    three = three_keep, z_move(three_out, nb, 0)
    spots = [tuple(tuple((m * width + (i + s) * 128, 128) for s in (0, 3)) for m in range(3)) for i in range(3)]
    other = grad_rows(place, [self_a, self_b, self_c], spots, w_self_qkv, grad_one, False)

    other, six, three, four, grad_one = tie(other, six, three, four, grad_one)
    six_out, six = y_prepare(six)
    four_keep, four_out = z_prepare(four)
    three_keep, three_out = z_prepare(three)
    six_out, other, four_out, three_out, grad_one = tie(six_out, other, four_out, three_out, grad_one)
    six = six + (y_move(six_out, nb),)
    four = four_keep, z_move(four_out, nb, 0)
    three = three_keep, z_move(three_out, nb, 1)
    in_back = swap(other)
    mine = grad_rows(place, [self_a, self_b, self_c], spots, w_self_qkv, grad_one, True)

    mine, four, layer_got, one = tie(mine, four, layer_got, one)
    four_keep, four_out = z_prepare(four)
    four = four_keep, z_move(four_out, nb, 1)
    layer_out = join_pairs(lax.dynamic_slice_in_dim(layer, x * span, span, 0), layer_got)
    layer_out, mine, six, five, three, memory_back = tie(layer_out, mine, six, five, three, memory_back)
    both = jnp.concatenate([after_y(six), after_y(five)], axis=2)
    both, memory_back = tie(both, memory_back)
    moved = [send(both[:, d], nb, (d, 0, 0, 0)) for d in range(1, nb // 4)]
    grad_memory = join_pairs(memory_mine, jnp.concatenate([memory_back, memory_rest]))
    grad_memory, moved, one, four = tie(grad_memory, moved, one, four)
    both = both[:, 0].astype(f32)
    for value in moved:
        both = both + value.astype(f32)
    last = both[1].astype(bf16)
    last, one, in_back = tie(last, one, in_back)
    last = x_move(last, nb)
    grad_in = join_pairs(mine, in_back)
    one = one.astype(f32)
    pieces = ff // width
    grad_ffn_out = jnp.concatenate([one[:, c * half : (c + 1) * half] for c in range(pieces)], axis=0)
    grad_ffn_in = one[:, pieces * half :]
    group = [last_part(three, c * half, e * half) for c, e in ((0, 1), (1, 2), (2, 4))]
    four = last_stage(four)
    last, grad_in, grad_ffn_in, grad_ffn_out, group, four = tie(last, grad_in, grad_ffn_in, grad_ffn_out, group, four)
    both = both[0] + last.astype(f32)
    unit = width // nb
    ends = unit, both.shape[0] - unit
    thirds = [s.reshape(unit, 3, 128) for s in (four[:unit], both[ends[1] :], both[: ends[0]])]
    grad_self_qkv = jnp.stack(thirds, axis=2).reshape(unit, 9 * 128)
    late = both[ends[0] : ends[0] + 6, :256].reshape(3, 2, 2, 128)
    late = at(late, x, 2).swapaxes(0, 1).reshape(2, half)
    early = lax.dynamic_slice_in_dim(four[unit:], x * 16, 16, 0)
    vectors = jnp.concatenate([late, early[:11]])
    bias_total = early[11 : 11 + bias_sums.shape[1] // width].reshape(-1)
    return (
        layer_out,
        grad_in,
        grad_memory,
        grad_self_qkv,
        group[0],
        group[1],
        group[2],
        grad_ffn_in[:, -half:],
        grad_ffn_in[:, :-half],
        grad_ffn_out,
        vectors[0:7],
        bias_total,
        vectors[7:10],
        vectors[10:13],
    )


def solution(mesh):
    devices = dict(mesh.shape)

    in_specs = (
        P("seq", "batch", None),
        P("seq", "batch", None),
        P("batch"),
        P("seq", "batch", None),
        P(),
        P(),
        P(),
        P(),
        P(),
        P(),
        P(),
        P(),
        P(),
        P(),
        P(),
    )
    out_specs = (
        P("seq", "batch", None),
        P("seq", "batch", None),
        P("seq", "batch", None),
        P("batch", "seq"),
        P("batch", "seq"),
        P("batch", "seq"),
        P("batch", "seq"),
        P("batch", "seq"),
        P("batch", "seq"),
        P("batch", "seq"),
        P(None, "seq"),
        P("seq"),
        P(None, "seq"),
        P(None, "seq"),
    )
    nb, ns = devices["batch"], devices["seq"]

    def program(hidden_in, *rest):
        whole = ns == 2 and hidden_in.shape[1] == 2 * nb and nb % 8 == 0 and nb & (nb - 1) == 0
        if not whole:
            general = jax.shard_map(
                per_device_general, mesh=mesh, in_specs=in_specs, out_specs=out_specs, check_vma=False
            )
            return general(hidden_in, *rest)
        parts = jax.sharding.Mesh(mesh.devices.reshape(nb // 4, 2, 2, ns), ("z", "y", "core", "seq"))
        split = lambda spec: P(*(("z", "y", "core") if axis == "batch" else axis for axis in spec))
        fast = jax.shard_map(
            per_device_fast,
            mesh=parts,
            in_specs=tuple(split(spec) for spec in in_specs),
            out_specs=tuple(split(spec) for spec in out_specs),
            check_vma=False,
        )
        return fast(hidden_in, *rest)

    return program
```
